128 devices in a mesh: rep: 32 (over x_lo, z, y), shard: 4 (over x_hi, core).
Axes of the slice: x: 4 (x_hi: 2, x_lo: 2; x = x_hi * 2 + x_lo), y: 4, z: 4, core: 2. Of those that a mesh axis runs over, the one named last changes fastest.
Arguments:
- prompt_x: bfloat16 [16384, 1024], P(('rep', 'shard')), may hold values from -6 to 6
- cont_x: bfloat16 [128, 128, 1024], P(('rep', 'shard')), may hold values from -6 to 6
- prompt_cot: bfloat16 [16384, 1024], P(('rep', 'shard')), may hold values from -6 to 6
- cont_cot: bfloat16 [128, 128, 1024], P(('rep', 'shard')), may hold values from -6 to 6
- prompt_routes: int32 [16384, 8], P(('rep', 'shard')), may hold values from 0 to 8, all different within a row
- cont_routes: int32 [128, 128, 8], P(('rep', 'shard')), may hold values from 0 to 8, all different within a row
- attn_gain: float32 [1024], P('shard'), may hold values from 0.5 to 1.5
- w_query: float32 [1024, 1024], P('shard'), may hold values from -0.1875 to 0.1875
- w_key: float32 [1024, 512], P('shard'), may hold values from -0.1875 to 0.1875
- w_value: float32 [1024, 512], P('shard'), may hold values from -0.1875 to 0.1875
- query_gain: float32 [1024], P('shard'), may hold values from 0.25 to 1.75
- key_gain: float32 [512], P('shard'), may hold values from 0.25 to 1.75
- w_out: float32 [1024, 1024], P(None, 'shard'), may hold values from -6 to 6
- ffn_gain: float32 [1024], P('shard'), may hold values from 0.5 to 1.5
- w_router: float32 [1024, 9], P('shard'), may hold values from -0.09375 to 0.09375
- w_gate: float32 [9, 1024, 512], P(None, 'shard'), may hold values from -0.1875 to 0.1875
- w_up: float32 [9, 1024, 512], P(None, 'shard'), may hold values from -0.1875 to 0.1875
- w_down: float32 [9, 512, 1024], P(None, None, 'shard'), may hold values from -6 to 6
Outputs:
- prompt_out: bfloat16 [16384, 1024], P(('rep', 'shard'))
- cont_out: bfloat16 [128, 128, 1024], P(('rep', 'shard'))
- prompt_x_grad: bfloat16 [16384, 1024], P(('rep', 'shard'))
- cont_x_grad: bfloat16 [128, 128, 1024], P(('rep', 'shard'))
- attn_gain_grad: float32 [1024], P('shard')
- w_query_grad: float32 [1024, 1024], P('shard')
- w_key_grad: float32 [1024, 512], P('shard')
- w_value_grad: float32 [1024, 512], P('shard')
- query_gain_grad: float32 [1024], P('shard')
- key_gain_grad: float32 [512], P('shard')
- w_out_grad: float32 [1024, 1024], P(None, 'shard')
- ffn_gain_grad: float32 [1024], P('shard')
- w_router_grad: float32 [1024, 9], P('shard')
- w_gate_grad: float32 [9, 1024, 512], P(None, 'shard')
- w_up_grad: float32 [9, 1024, 512], P(None, 'shard')
- w_down_grad: float32 [9, 512, 1024], P(None, None, 'shard')
The draws below stay inside these ranges and needn't reach their ends.
Inputs may be any that keep to these rules, and one draw needn't show every extreme that they name: `prompt_routes`: each token names 8 different experts. `cont_routes`: each token names 8 different experts.
All inputs are finite; a program needn't handle non-finite values.
Results may differ from the reference program's by a relative error of at most 0.03.
The reference program's roundings to bfloat16 on the way count: a program that leaves them out, or rounds other values in their place, can miss the bound.
Values may be sent and summed in bfloat16 or wider, within the bound.
No kernel may reach another device: no remote copies, remote signals or barrier semaphores. Data moves between devices by JAX's collectives and lax.ppermute only.
A program may use at most 192 MiB of HBM per device.

```python
import jax
import jax.numpy as jnp
from jax import lax

D = 1024
HEADS = 16
KVHEADS = 8
HDIM = 64
FF = 512
EXPERTS = 9
TOPK = 8
PROMPT = 512
CLEN = 128
CONT_DEV = 1
GROUP_CONTS = 4
N_REP = 32
N_SHARD = 4


def block_levels(own_key, shape, pieces, low, high):
    def one(dim, blocks):
        heights = jax.random.uniform(jax.random.fold_in(jax.random.fold_in(own_key, 6), dim), (blocks,), jnp.float32, low / len(pieces), high / len(pieces))
        return jnp.repeat(jnp.exp(heights), shape[dim] // blocks).reshape((-1,) + (1,) * (len(shape) - dim - 1))

    loudness = one(*pieces[0])
    for cut in pieces[1:]:
        loudness = loudness * one(*cut)
    return loudness


def distinct(own_key, rows, amount, top, lift):
    sequence = jax.random.permutation(jax.random.fold_in(own_key, 1), amount)
    favour = sequence
    for power in range(3):
        favour = favour * favour // amount
    favour = favour * lift // amount
    lots = jax.random.randint(jax.random.fold_in(own_key, 2), (rows, amount), 0, 4096) + favour
    sure = jax.random.permutation(jax.random.fold_in(own_key, 3), rows)[jnp.arange(amount) % rows]
    lots = jnp.where(jnp.arange(rows)[:, None] == sure[None, :], 1 << 14, lots)
    merit = lots * amount + jnp.arange(amount)
    return lax.top_k(merit.astype(jnp.int32), top)[1].astype(jnp.int32)


def scatter_about(key, extent, deviation, most, shards=(), kind=jnp.bfloat16):
    values = deviation * jax.random.normal(key, extent, jnp.float32)
    if shards:
        values = values * block_levels(key, extent, shards, -0.22, 0.18)
    return jnp.clip(values, -most, most).astype(kind)


def setup_inputs(seed: int = 0) -> dict:
    arg_keys = jax.random.split(jax.random.key(seed), 19)
    return {
        "prompt_x": scatter_about(arg_keys[0], (N_REP * PROMPT, D), 1.0, 6.0, ((0, 128),)),
        "cont_x": scatter_about(arg_keys[1], (N_REP * GROUP_CONTS, CLEN, D), 1.0, 6.0, ((0, 128),)),
        "prompt_cot": scatter_about(arg_keys[2], (N_REP * PROMPT, D), 1.0, 6.0, ((0, 128),)),
        "cont_cot": scatter_about(arg_keys[3], (N_REP * GROUP_CONTS, CLEN, D), 1.0, 6.0, ((0, 128),)),
        "prompt_routes": distinct(arg_keys[4], (N_REP * PROMPT), EXPERTS, TOPK, 0),
        "cont_routes": distinct(arg_keys[5], (N_REP * GROUP_CONTS) * CLEN, EXPERTS, TOPK, 0).reshape((N_REP * GROUP_CONTS, CLEN, TOPK)),
        "attn_gain": jnp.clip(1.0 + 0.1 * jax.random.normal(arg_keys[6], (D,), jnp.float32), 0.5, 1.5),
        "w_query": scatter_about(arg_keys[7], (D, HEADS * HDIM), D ** -0.5, 0.1875, ((0, 4),), jnp.float32),
        "w_key": scatter_about(arg_keys[8], (D, KVHEADS * HDIM), D ** -0.5, 0.1875, ((0, 4),), jnp.float32),
        "w_value": scatter_about(arg_keys[9], (D, KVHEADS * HDIM), D ** -0.5, 0.1875, ((0, 4),), jnp.float32),
        "query_gain": jnp.clip(1.0 + 0.15 * jax.random.normal(arg_keys[10], (HEADS * HDIM,), jnp.float32), 0.25, 1.75),
        "key_gain": jnp.clip(1.0 + 0.15 * jax.random.normal(arg_keys[11], (KVHEADS * HDIM,), jnp.float32), 0.25, 1.75),
        "w_out": scatter_about(arg_keys[12], (HEADS * HDIM, D), 1.0, 6.0, ((1, 4),), jnp.float32),
        "ffn_gain": jnp.clip(1.0 + 0.1 * jax.random.normal(arg_keys[13], (D,), jnp.float32), 0.5, 1.5),
        "w_router": scatter_about(arg_keys[14], (D, EXPERTS), (4 * D) ** -0.5, 0.09375, ((0, 4),), jnp.float32),
        "w_gate": scatter_about(arg_keys[15], (EXPERTS, D, FF), D ** -0.5, 0.1875, ((1, 4),), jnp.float32),
        "w_up": scatter_about(arg_keys[16], (EXPERTS, D, FF), D ** -0.5, 0.1875, ((1, 4),), jnp.float32),
        "w_down": scatter_about(arg_keys[17], (EXPERTS, FF, D), 1.0, 6.0, ((2, 4),), jnp.float32),
    }


@jax.custom_vjp
def low(v):
    return lax.optimization_barrier(v.astype(jnp.bfloat16)).astype(jnp.float32)

@jax.custom_vjp
def low_back(v):
    return v

def low_keep(v):
    return (low(v), None)

def low_pass(kept, grad):
    return (grad,)

def back_keep(v):
    return (v, None)

def back_low(kept, grad):
    return (low(grad),)
low.defvjp(low_keep, low_pass)
low_back.defvjp(back_keep, back_low)
EPSILON = 1e-06
SCORE_SCALE = 0.25
RESIDUAL_SCALE = 0.22
ROTARY_BASE = 10000.0
MASKED = -1e+30

def matmul_high(operand, other):
    return jnp.dot(operand, other, precision=lax.Precision.HIGHEST, preferred_element_type=jnp.float32)

def einsum_high(formula, operand, other):
    return jnp.einsum(formula, operand, other, precision=lax.Precision.HIGHEST, preferred_element_type=jnp.float32)

def rms_gain(values, gain_row):
    inverse = lax.rsqrt(lax.optimization_barrier(jnp.mean(values * values, axis=-1, keepdims=True)) + EPSILON)
    return values * inverse * gain_row

def rotary(values, cosine, sine_part):
    half_width = values.shape[-1] // 2
    first_half = values[..., :half_width]
    second_half = values[..., half_width:]
    return jnp.concatenate([first_half * cosine - second_half * sine_part, second_half * cosine + first_half * sine_part], axis=-1)

def angles(position):
    frequency = ROTARY_BASE ** (-jnp.arange(0, HDIM, 2).astype(jnp.float32) / HDIM)
    turned = position.astype(jnp.float32)[:, None] * frequency[None, :]
    return (jnp.cos(turned)[:, None, :], jnp.sin(turned)[:, None, :])

def group_layer(weights, tokens, routes, position, segment):
    attn_gain, w_query, w_key, w_value, query_gain, key_gain, w_out, ffn_gain, w_router, w_gate, w_up, w_down = weights
    row_count = tokens.shape[0]
    group_size = HEADS // KVHEADS
    cosine, sine_part = angles(position)
    normed = low(rms_gain(tokens, attn_gain))
    query_proj = low_back(matmul_high(normed, w_query))
    key_proj = low_back(matmul_high(normed, w_key))
    query_normed = rms_gain(query_proj, query_gain)
    key_normed = rms_gain(key_proj, key_gain)
    query_rows = low(rotary(query_normed.reshape(row_count, HEADS, HDIM), cosine, sine_part))
    key_rows = low(rotary(key_normed.reshape(row_count, KVHEADS, HDIM), cosine, sine_part))
    value_rows = low(low_back(matmul_high(normed, w_value))).reshape(row_count, KVHEADS, HDIM)
    query_split = query_rows.reshape(row_count, KVHEADS, group_size, HDIM)
    scores = low_back(SCORE_SCALE * einsum_high('nkgd,mkd->kgnm', query_split, key_rows))
    allowed = (position[None, :] <= position[:, None]) & ((segment[None, :] == 0) | (segment[None, :] == segment[:, None]))
    scores = jnp.where(allowed[None, None], scores, MASKED)
    probs = low(jax.nn.softmax(scores, axis=-1))
    mixed_heads = low(low_back(einsum_high('kgnm,mkd->nkgd', probs, value_rows))).reshape(row_count, HEADS * HDIM)
    hidden = tokens + RESIDUAL_SCALE * low_back(matmul_high(mixed_heads, w_out))
    normed_two = low(rms_gain(hidden, ffn_gain))
    logits = low_back(matmul_high(normed_two, w_router))
    chosen = (routes[:, :, None] == jnp.arange(EXPERTS, dtype=jnp.int32)[None, None, :]).astype(jnp.float32)
    gate_weights = jax.nn.softmax(lax.optimization_barrier(jnp.sum(chosen * logits[:, None, :], axis=2)), axis=1)
    dense_gates = lax.optimization_barrier(jnp.sum(gate_weights[:, :, None] * chosen, axis=1))
    gate_in = low_back(einsum_high('td,edf->tef', normed_two, w_gate))
    up_in = low_back(einsum_high('td,edf->tef', normed_two, w_up))
    inner_units = low(jax.nn.silu(gate_in) * up_in)
    expert_out = low_back(einsum_high('tef,efd->ted', inner_units, w_down))
    mixture = einsum_high('te,ted->td', dense_gates, expert_out)
    return hidden + RESIDUAL_SCALE * mixture

def reference(prompt_x, cont_x, prompt_cot, cont_cot, prompt_routes, cont_routes, attn_gain, w_query, w_key, w_value, query_gain, key_gain, w_out, ffn_gain, w_router, w_gate, w_up, w_down):
    cont_count = CONT_DEV * N_SHARD
    cont_steps = jnp.arange(CLEN, dtype=jnp.int32)
    position = jnp.concatenate([jnp.arange(PROMPT, dtype=jnp.int32), PROMPT + jnp.tile(cont_steps, cont_count)])
    segment = jnp.concatenate([jnp.zeros((PROMPT,), jnp.int32), 1 + jnp.repeat(jnp.arange(cont_count, dtype=jnp.int32), CLEN)])

    def by_group(prompt_part, cont_part):
        row_width = prompt_part.shape[-1]
        return jnp.concatenate([prompt_part.reshape(N_REP, PROMPT, row_width), cont_part.reshape(N_REP, cont_count * CLEN, row_width)], axis=1)
    routes = by_group(prompt_routes, cont_routes)

    def forward(masters, prompt_in, cont_in):
        weights = tuple((low(master) for master in masters))
        tokens = by_group(prompt_in, cont_in)

        def group_step(inputs):
            return group_layer(weights, inputs[0], inputs[1], position, segment)
        result = lax.map(jax.checkpoint(group_step), (tokens, routes))
        return (result[:, :PROMPT].reshape(prompt_in.shape), result[:, PROMPT:].reshape(cont_in.shape))
    masters = (attn_gain, w_query, w_key, w_value, query_gain, key_gain, w_out, ffn_gain, w_router, w_gate, w_up, w_down)
    outputs, pullback = jax.vjp(forward, masters, prompt_x.astype(jnp.float32), cont_x.astype(jnp.float32))
    weight_grads, prompt_grad, cont_grad = pullback((prompt_cot.astype(jnp.float32), cont_cot.astype(jnp.float32)))
    return (outputs[0].astype(jnp.bfloat16), outputs[1].astype(jnp.bfloat16), prompt_grad.astype(jnp.bfloat16), cont_grad.astype(jnp.bfloat16), weight_grads[0], weight_grads[1], weight_grads[2], weight_grads[3], weight_grads[4], weight_grads[5], weight_grads[6], weight_grads[7], weight_grads[8], weight_grads[9], weight_grads[10], weight_grads[11])
```

```python
import jax
import jax.numpy as jnp
from jax import lax
from jax.experimental import pallas as pl
from jax.experimental.pallas import tpu as pltpu
from jax.sharding import Mesh, PartitionSpec as P

EPSILON = 1e-06
SCORE_SCALE = 0.25
RESIDUAL_SCALE = 0.22
ROTARY_BASE = 10000.0
MASKED = -1e30

D = 1024
HDIM = 64
PAIRS = 4
KVW = 512
QKVW = 2048
ROWS = 256
HALF = 128
QUART = 256
EXPERTS = 9
FSLICE = 128
TILE = 3 * FSLICE
TOKENS = 4 * ROWS
KEYS = 5 * HALF
BOUT = D + 128
ATTW = QKVW + D + 128
PIECES = 16
PROWS = QUART // PIECES

F32 = jnp.float32
BF16 = jnp.bfloat16

AXES = ("xl", "z", "y", "xh", "c")


def nn(left, right):
    return lax.dot_general(left, right, (((1,), (0,)), ((), ())), preferred_element_type=F32)


def nt(left, right):
    return lax.dot_general(left, right, (((1,), (1,)), ((), ())), preferred_element_type=F32)


def tn(left, right):
    return lax.dot_general(left, right, (((0,), (0,)), ((), ())), preferred_element_type=F32)


def spot(index, width):
    return pl.ds(pl.multiple_of(index * width, width), width)


def block(index, width):
    return slice(index * width, (index + 1) * width)


SMEM = pl.BlockSpec(memory_space=pltpu.SMEM)
VMEM = pl.BlockSpec(memory_space=pltpu.VMEM)


COST = pl.CostEstimate(flops=1_000_000, bytes_accessed=1_000_000, transcendentals=0)


def whole_call(kernel, name, out_shape, scratch=(), limit=56):
    def call(*operands):
        return pl.pallas_call(
            kernel,
            name=name,
            out_shape=out_shape,
            in_specs=[SMEM] + [VMEM] * (len(operands) - 1),
            out_specs=jax.tree.map(lambda _: VMEM, out_shape),
            scratch_shapes=list(scratch),
            compiler_params=pltpu.CompilerParams(vmem_limit_bytes=limit * 1024 * 1024),
            cost_estimate=COST,
        )(*operands)

    return call


def shaped(shape, dtype):
    return jax.ShapeDtypeStruct(shape, dtype)


def pack_kernel(s_ref, gate, up, down, *outs):
    for k in range(4):
        spotted = spot(s_ref[0] ^ k, FSLICE)
        outs[k][0, :, 0:FSLICE] = gate[0, :, spotted].astype(BF16)
        outs[k][0, :, FSLICE : 2 * FSLICE] = up[0, :, spotted].astype(BF16)
        outs[k][0, :, 2 * FSLICE :] = down[0, spotted, :].T.astype(BF16)


def pack_experts(place, w_gate, w_up, w_down):
    return pl.pallas_call(
        pack_kernel,
        name="pack_experts",
        grid=(EXPERTS,),
        in_specs=[
            SMEM,
            pl.BlockSpec((1, QUART, 512), lambda e: (e, 0, 0)),
            pl.BlockSpec((1, QUART, 512), lambda e: (e, 0, 0)),
            pl.BlockSpec((1, 512, QUART), lambda e: (e, 0, 0)),
        ],
        out_specs=[pl.BlockSpec((1, QUART, TILE), lambda e: (e, 0, 0))] * 4,
        out_shape=[shaped((EXPERTS, QUART, TILE), BF16)] * 4,
        cost_estimate=COST,
    )(place, w_gate, w_up, w_down)


def swapped(values):
    lane = lax.broadcasted_iota(jnp.int32, values.shape, 1)
    return jnp.where(
        lane % HDIM < HDIM // 2, pltpu.roll(values, 96, axis=1), pltpu.roll(values, 32, axis=1)
    )


def project_kernel(
    s_ref, xp, xc, a0, a1, a2, a3, cos, sin, q_o, k_o, v_o, nq_o, nk_o, inv_o, xr_o, ar_o, gain_o, rt_o, acc
):
    parts = (a0, a1, a2, a3)
    for k in range(4):
        there = s_ref[0] ^ k
        xr_o[0:HALF, block(k, QUART)] = xp[:, spot(there, QUART)]
        xr_o[HALF:ROWS, block(k, QUART)] = xc[:, spot(there, QUART)]
        small = parts[k][QUART : QUART + 16, 0:1024].astype(F32)[0:1]
        gain_o[0:1, block(k, QUART)] = small[:, 0:256]
        gain_o[0:1, slice(D + k * QUART, D + (k + 1) * QUART)] = small[:, 256:512]
        gain_o[0:1, pl.ds(pl.multiple_of(2 * D + there * QUART, 128), QUART)] = small[:, 512:768]
        gain_o[0:1, pl.ds(pl.multiple_of(3 * D + there * HALF, 128), HALF)] = small[:, 768:896]
        rt_o[:, block(k, QUART)] = parts[k][QUART + 16 : QUART + 32, 0:QUART]
    x = xr_o[...].astype(F32)
    inverse = lax.rsqrt(jnp.mean(x * x, axis=1, keepdims=True) + EPSILON)
    ar_o[...] = (x * inverse * gain_o[0:1, 0:D]).astype(BF16)
    for n in range(4):
        total = nn(ar_o[:, block(0, QUART)], parts[0][0:QUART, block(n, 512)])
        for k in range(1, 4):
            total = total + nn(ar_o[:, block(k, QUART)], parts[k][0:QUART, block(n, 512)])
        acc[:, block(n, 512)] = total
    qp = acc[:, 0:D]
    inv_q = lax.rsqrt(jnp.mean(qp * qp, axis=1, keepdims=True) + EPSILON)
    kp = acc[:, D : D + KVW]
    inv_k = lax.rsqrt(jnp.mean(kp * kp, axis=1, keepdims=True) + EPSILON)
    nq_o[...] = qp * inv_q
    nk_o[...] = kp * inv_k
    lane = lax.broadcasted_iota(jnp.int32, (ROWS, 128), 1)
    inv_o[...] = jnp.where(lane == 0, inv_q, jnp.where(lane == 1, inv_k, inverse))
    v_o[...] = acc[:, D + KVW : QKVW].astype(BF16)
    cosine = cos[...]
    sine = sin[...]
    for g in range(8):
        at = block(g, 128)
        u = nq_o[:, at] * gain_o[0:1, 2 * D + g * 128 : 2 * D + (g + 1) * 128]
        q_o[:, at] = (u * cosine + swapped(u) * sine).astype(BF16)
    for g in range(4):
        at = block(g, 128)
        u = nk_o[:, at] * gain_o[0:1, 3 * D + g * 128 : 3 * D + (g + 1) * 128]
        k_o[:, at] = (u * cosine + swapped(u) * sine).astype(BF16)


project = whole_call(
    project_kernel,
    "project",
    [
        shaped((ROWS, D), BF16),
        shaped((ROWS, KVW), BF16),
        shaped((ROWS, KVW), BF16),
        shaped((ROWS, D), F32),
        shaped((ROWS, KVW), F32),
        shaped((ROWS, 128), F32),
        shaped((ROWS, D), BF16),
        shaped((ROWS, D), BF16),
        shaped((8, 3 * D + KVW), F32),
        shaped((16, D), BF16),
    ],
    scratch=[pltpu.VMEM((ROWS, QKVW), F32)],
)


def fill_bias(place, bias):
    row = lax.broadcasted_iota(jnp.int32, (HALF, 512), 0)
    lane = lax.broadcasted_iota(jnp.int32, (HALF, 512), 1)
    causal = jnp.where(row <= lane % HALF, 0.0, MASKED)
    is_prompt = lane % ROWS < HALF
    bias[0:HALF, :] = jnp.where(is_prompt, causal, 0.0)
    for k in range(1, 4):
        level = jnp.where((place ^ k) < place, 0.0, MASKED)
        bias[block(k, HALF), :] = jnp.where(is_prompt, level, 0.0)
    bias[4 * HALF :, :] = jnp.where(is_prompt, MASKED, causal)


def fill_keys(refs, dest):
    for j in range(4):
        dest[block(j, HALF), :] = refs[j][0:HALF, :]
    dest[4 * HALF :, :] = refs[0][HALF:ROWS, :]


def doubled(ref, pair, odd):
    both = ref[:, spot(pair, 128)]
    other = pltpu.roll(both.astype(F32), HDIM, axis=1).astype(BF16)
    lane = lax.broadcasted_iota(jnp.int32, both.shape, 1)
    return jnp.where((lane < HDIM) == (odd == 0), both, other)


def stacked(ref, head, scale):
    rows = ref[:, spot(head, 128)]
    lane = lax.broadcasted_iota(jnp.int32, rows.shape, 1)
    rows = rows * jnp.asarray(scale, rows.dtype)
    none = jnp.zeros_like(rows)
    return jnp.concatenate(
        [jnp.where(lane < HDIM, rows, none), jnp.where(lane < HDIM, none, rows)], axis=0
    )


def attend_kernel(
    s_ref, q, k0, k1, k2, k3, v0, v1, v2, v3, o0, o1, o2, o3, xr, gain, rt, rp, rc,
    mixed_o, lse_o, hid_o, b_o, gates_o, bias, keys, values
):
    fill_bias(s_ref[0], bias)
    fill_keys((k0, k1, k2, k3), keys)
    fill_keys((v0, v1, v2, v3), values)

    def one_pair(pair, carry):
        for odd in range(2):
            head = 2 * pair + odd
            kk = doubled(keys, pair, odd)
            vv = doubled(values, pair, odd)
            scores = nt(kk, stacked(q, head, SCORE_SCALE)) + bias[...]
            highest = jnp.max(scores, axis=0, keepdims=True)
            raised = jnp.exp(scores - highest)
            totals = jnp.sum(raised, axis=0, keepdims=True)
            probs = (raised * (1.0 / totals)).astype(BF16)
            lse_o[pl.ds(head, 1), :] = highest + jnp.log(totals)
            out = tn(vv, probs).T
            lane = lax.broadcasted_iota(jnp.int32, (ROWS, 128), 1)
            mixed_o[:, spot(head, 128)] = jnp.where(
                lane < HDIM, out[0:ROWS], out[ROWS : 2 * ROWS]
            ).astype(BF16)
        return carry

    lax.fori_loop(0, PAIRS, one_pair, 0)
    mixed = mixed_o[...]
    for k, part in enumerate((o0, o1, o2, o3)):
        hid_o[:, block(k, QUART)] = xr[:, block(k, QUART)].astype(F32) + RESIDUAL_SCALE * nn(
            mixed, part[...]
        )
    hidden = hid_o[...]
    inverse = lax.rsqrt(jnp.mean(hidden * hidden, axis=1, keepdims=True) + EPSILON)
    b_o[:, 0:D] = (hidden * inverse * gain[0:1, D : 2 * D]).astype(BF16)
    logits = nt(b_o[:, 0:D], rt[...])
    expert = lax.broadcasted_iota(jnp.int32, (HALF, 16), 1)
    for half, routes in enumerate((rp, rc)):
        chosen = routes[:, 0:1] == expert
        for r in range(1, 8):
            chosen = chosen | (routes[:, r : r + 1] == expert)
        level = jnp.where(chosen, logits[block(half, HALF)], MASKED)
        raised = jnp.exp(level - jnp.max(level, axis=1, keepdims=True))
        gates = raised / jnp.sum(raised, axis=1, keepdims=True)
        gates_o[block(half, HALF), 0:16] = gates
        high = gates.astype(BF16).astype(F32)
        b_o[block(half, HALF), D:BOUT] = jnp.concatenate(
            [high, gates - high, jnp.zeros((HALF, 96), F32)], axis=1
        ).astype(BF16)


attend = whole_call(
    attend_kernel,
    "attend",
    [
        shaped((ROWS, D), BF16),
        shaped((8, 512), F32),
        shaped((ROWS, D), F32),
        shaped((ROWS, BOUT), BF16),
        shaped((ROWS, 128), F32),
    ],
    scratch=[
        pltpu.VMEM((KEYS, 512), F32),
        pltpu.VMEM((KEYS, KVW), BF16),
        pltpu.VMEM((KEYS, KVW), BF16),
    ],
)


def expert_kernel(
    s_ref, b0, b1, b2, b3, g0, g1, g2, g3, w0, w1, w2, w3,
    dudw_o, gz_o, dbk_o, dbs_o, xs, gs, gates, dgs, wgu, ws
):
    e = pl.program_id(0)
    place = s_ref[0]

    @pl.when(e == 0)
    def _():
        for j, (b_ref, g_ref) in enumerate(zip((b0, b1, b2, b3), (g0, g1, g2, g3))):
            rows = block(j, ROWS)
            for k in range(4):
                xs[rows, block(k, QUART)] = b_ref[:, block(k ^ j, QUART)]
                gs[rows, block(k, QUART)] = g_ref[:, spot(place ^ k, QUART)]
            both = b_ref[:, D:BOUT].astype(F32)
            gates[rows, :] = both + pltpu.roll(both, 112, axis=1)
        dgs[...] = jnp.zeros_like(dgs)

    for k, part in enumerate((w0, w1, w2, w3)):
        ws[block(k, QUART), :] = part[0]
    wgu[:, spot(e, 2 * FSLICE)] = ws[:, 0 : 2 * FSLICE]
    both = nn(xs[...], ws[:, 0 : 2 * FSLICE])
    h = RESIDUAL_SCALE * nn(gs[...], ws[:, 2 * FSLICE :])
    u = both[:, 0:FSLICE]
    w = both[:, FSLICE:]
    lane = lax.broadcasted_iota(jnp.int32, (TOKENS, 128), 1)
    gate = jnp.sum(jnp.where(lane == e, gates[...], 0.0), axis=1, keepdims=True)
    sig = jax.nn.sigmoid(u)
    silu = u * sig
    z = (silu * w).astype(BF16).astype(F32)
    gz_o[:, spot(e, FSLICE)] = (gate * z).astype(BF16)
    dgate = jnp.sum(z * h, axis=1, keepdims=True)
    dgs[...] += jnp.where(lane == e, dgate, 0.0)
    dz = gate * h
    du = (dz * w * sig * (1.0 + u * (1.0 - sig))).astype(BF16)
    dw = (dz * silu).astype(BF16)
    dudw_o[:, spot(e, 2 * FSLICE)] = jnp.concatenate([du, dw], axis=1)

    @pl.when(e == EXPERTS - 1)
    def _():
        for j in range(4):
            out = (dbk_o, dbs_o)[j % 2]
            rows = block(j, ROWS)
            total = nt(dudw_o[rows, :], wgu[...]).astype(BF16)
            for k in range(4):
                out[j // 2, :, block(k ^ j, QUART)] = total[:, block(k, QUART)]
            dg = dgs[rows, 0:16]
            high = dg.astype(BF16).astype(F32)
            out[j // 2, :, D:BOUT] = jnp.concatenate(
                [high, dg - high, jnp.zeros((ROWS, 96), F32)], axis=1
            ).astype(BF16)


def fixed(rank):
    return lambda e: (0,) * rank


def experts(place, b_parts, g_parts, w_parts):
    return pl.pallas_call(
        expert_kernel,
        name="experts",
        grid=(EXPERTS,),
        in_specs=[SMEM]
        + [pl.BlockSpec((ROWS, BOUT), fixed(2))] * 4
        + [pl.BlockSpec((ROWS, D), fixed(2))] * 4
        + [pl.BlockSpec((1, QUART, TILE), lambda e: (e, 0, 0))] * 4,
        out_specs=[
            pl.BlockSpec((TOKENS, EXPERTS * 2 * FSLICE), fixed(2)),
            pl.BlockSpec((TOKENS, EXPERTS * FSLICE), fixed(2)),
            pl.BlockSpec((2, ROWS, BOUT), fixed(3)),
            pl.BlockSpec((2, ROWS, BOUT), fixed(3)),
        ],
        out_shape=[
            shaped((TOKENS, EXPERTS * 2 * FSLICE), BF16),
            shaped((TOKENS, EXPERTS * FSLICE), BF16),
            shaped((2, ROWS, BOUT), BF16),
            shaped((2, ROWS, BOUT), BF16),
        ],
        scratch_shapes=[
            pltpu.VMEM((TOKENS, D), BF16),
            pltpu.VMEM((TOKENS, D), BF16),
            pltpu.VMEM((TOKENS, 128), F32),
            pltpu.VMEM((TOKENS, 128), F32),
            pltpu.VMEM((D, EXPERTS * 2 * FSLICE), BF16),
            pltpu.VMEM((D, TILE), BF16),
        ],
        compiler_params=pltpu.CompilerParams(vmem_limit_bytes=56 * 1024 * 1024),
        cost_estimate=COST,
    )(place, *b_parts, *g_parts, *w_parts)


def expert_grad_kernel(
    s_ref, b0, b1, b2, b3, g0, g1, g2, g3, dudw, gz, grad_o, xt, gt
):
    @pl.when(pl.program_id(0) == 0)
    def _():
        for j, (b_ref, g_ref) in enumerate(zip((b0, b1, b2, b3), (g0, g1, g2, g3))):
            for k in range(4):
                xt[block(k, QUART), block(j, ROWS)] = b_ref[:, block(k ^ j, QUART)].T
                gt[block(k, QUART), block(j, ROWS)] = g_ref[:, spot(s_ref[0] ^ k, QUART)].T

    for k in range(4):
        rows = block(k, QUART)
        first = nn(xt[rows, :], dudw[...]).astype(BF16)
        second = (RESIDUAL_SCALE * nn(gt[rows, :], gz[...])).astype(BF16)
        for p in range(PIECES):
            grad_o[p, k, 0, :, 0 : 2 * FSLICE] = first[block(p, PROWS)]
            grad_o[p, k, 0, :, 2 * FSLICE :] = second[block(p, PROWS)]


def expert_grads(place, b_parts, g_parts, dudw, gz):
    return pl.pallas_call(
        expert_grad_kernel,
        name="expert_grads",
        grid=(EXPERTS,),
        in_specs=[SMEM]
        + [pl.BlockSpec((ROWS, BOUT), fixed(2))] * 4
        + [pl.BlockSpec((ROWS, D), fixed(2))] * 4
        + [
            pl.BlockSpec((TOKENS, 2 * FSLICE), lambda e: (0, e)),
            pl.BlockSpec((TOKENS, FSLICE), lambda e: (0, e)),
        ],
        out_specs=pl.BlockSpec((PIECES, 4, 1, PROWS, TILE), lambda e: (0, 0, e, 0, 0)),
        out_shape=shaped((PIECES, 4, EXPERTS, PROWS, TILE), BF16),
        scratch_shapes=[pltpu.VMEM((D, TOKENS), BF16), pltpu.VMEM((D, TOKENS), BF16)],
        compiler_params=pltpu.CompilerParams(vmem_limit_bytes=56 * 1024 * 1024),
        cost_estimate=COST,
    )(place, *b_parts, *g_parts, dudw, gz)


def mixture_kernel(s_ref, gz, w0, w1, w2, w3, keep_o, send_o, wide):
    for k, part in enumerate((w0, w1, w2, w3)):
        for e in range(EXPERTS):
            wide[block(k, QUART), block(e, FSLICE)] = part[e]
    for j in range(4):
        out = (keep_o, send_o)[j % 2]
        total = nt(gz[block(j, ROWS), :], wide[...]).astype(BF16)
        for k in range(4):
            out[j // 2, :, block(k ^ j, QUART)] = total[:, block(k, QUART)]


def mixture(place, gz, w_parts):
    down = pl.BlockSpec((EXPERTS, QUART, FSLICE), lambda i: (0, 0, 2))
    return pl.pallas_call(
        mixture_kernel,
        name="mixture",
        grid=(1,),
        in_specs=[SMEM, pl.BlockSpec((TOKENS, EXPERTS * FSLICE), fixed(2))] + [down] * 4,
        out_specs=[pl.BlockSpec((2, ROWS, D), fixed(3))] * 2,
        out_shape=[shaped((2, ROWS, D), BF16)] * 2,
        scratch_shapes=[pltpu.VMEM((D, EXPERTS * FSLICE), BF16)],
        compiler_params=pltpu.CompilerParams(vmem_limit_bytes=56 * 1024 * 1024),
        cost_estimate=COST,
    )(place, gz, *w_parts)


def attend_back_kernel(
    s_ref, db_keep, db_come, hid, b, gates_ref, gp, gc, gain, rt, mixed, lse,
    q, k0, k1, k2, k3, v0, v1, v2, v3, o0, o1, o2, o3,
    hgrad_o, small_o, dwok_o, dwos_o, dq_o, kvk_o, kvs_o, dk_o, dv_o,
    bias, keys, values, dmix, grow
):
    place = s_ref[0]
    parts = (o0, o1, o2, o3)
    fill_bias(place, bias)
    fill_keys((k0, k1, k2, k3), keys)
    fill_keys((v0, v1, v2, v3), values)
    total = db_keep[...].astype(F32) + db_come[...].astype(F32)
    tail = total[:, D:BOUT]
    dgate = (tail + pltpu.roll(tail, 112, axis=1))[:, 0:16]
    gates = gates_ref[:, 0:16]
    dlog = (gates * (dgate - jnp.sum(gates * dgate, axis=1, keepdims=True))).astype(BF16)
    dbt = total[:, 0:D] + nn(dlog, rt[...])
    small_o[...] = jnp.zeros_like(small_o)
    small_o[16:32, :] = tn(dlog, b[:, 0:D])
    hidden = hid[...]
    inverse = lax.rsqrt(jnp.mean(hidden * hidden, axis=1, keepdims=True) + EPSILON)
    n2 = hidden * inverse
    small_o[1:2, :] = jnp.sum(dbt * n2, axis=0, keepdims=True)
    scaled = dbt * gain[0:1, D : 2 * D]
    for k in range(4):
        there = spot(place ^ k, QUART)
        grow[0:HALF, block(k, QUART)] = gp[:, there]
        grow[HALF:ROWS, block(k, QUART)] = gc[:, there]
    hgrad = grow[...].astype(F32) + inverse * (
        scaled - n2 * jnp.mean(scaled * n2, axis=1, keepdims=True)
    )
    hgrad_o[...] = hgrad
    agrad = (RESIDUAL_SCALE * hgrad).astype(BF16)
    whole = nt(agrad[:, block(0, QUART)], parts[0][...])
    for k in range(1, 4):
        whole = whole + nt(agrad[:, block(k, QUART)], parts[k][...])
    dmix[...] = whole.astype(BF16)
    for g in range(4):
        rows = tn(mixed[:, block(g, QUART)], agrad).astype(BF16)
        for k in range(4):
            out = (dwok_o, dwos_o)[k % 2]
            out[k // 2, :, block(g, QUART)] = rows[:, block(k, QUART)]

    def one_pair(pair, carry):
        dks = []
        dvs = []
        lane = lax.broadcasted_iota(jnp.int32, (ROWS, 128), 1)
        for odd in range(2):
            head = 2 * pair + odd
            kk = doubled(keys, pair, odd)
            vv = doubled(values, pair, odd)
            qs = stacked(q, head, SCORE_SCALE)
            ds_rows = stacked(dmix, head, 1.0)
            probs = jnp.exp(nt(kk, qs) + bias[...] - lse[pl.ds(head, 1), :])
            pgrad = nt(vv, ds_rows)
            inner = jnp.sum(probs * pgrad, axis=0, keepdims=True)
            sgrad = (probs * (pgrad - inner)).astype(BF16)
            dkr = nn(sgrad, qs)
            dvr = nn(probs.astype(BF16), ds_rows)
            dks.append(dkr + pltpu.roll(dkr, HDIM, axis=1))
            dvs.append(dvr + pltpu.roll(dvr, HDIM, axis=1))
            dqt = (SCORE_SCALE * tn(kk, sgrad)).T
            dq_o[:, spot(head, 128)] = jnp.where(lane < HDIM, dqt[0:ROWS], dqt[ROWS : 2 * ROWS])
        low = lax.broadcasted_iota(jnp.int32, (KEYS, 128), 1) < HDIM
        dk = jnp.where(low, dks[0], dks[1])
        dv = jnp.where(low, dvs[0], dvs[1])
        at = spot(pair, 128)
        at_v = spot(pair + 4, 128)
        for j in range(4):
            side = (kvk_o, kvs_o)[j % 2]
            side[j // 2, :, at] = dk[block(j, HALF)].astype(BF16)
            side[j // 2, :, at_v] = dv[block(j, HALF)].astype(BF16)
        dk_o[:, at] = dk[4 * HALF :]
        dv_o[:, at] = dv[4 * HALF :]
        return carry

    lax.fori_loop(0, PAIRS, one_pair, 0)


attend_back = whole_call(
    attend_back_kernel,
    "attend_back",
    [
        shaped((ROWS, D), F32),
        shaped((32, D), F32),
        shaped((2, QUART, D), BF16),
        shaped((2, QUART, D), BF16),
        shaped((ROWS, D), F32),
        shaped((2, HALF, D), BF16),
        shaped((2, HALF, D), BF16),
        shaped((HALF, KVW), F32),
        shaped((HALF, KVW), F32),
    ],
    scratch=[
        pltpu.VMEM((KEYS, 512), F32),
        pltpu.VMEM((KEYS, KVW), BF16),
        pltpu.VMEM((KEYS, KVW), BF16),
        pltpu.VMEM((ROWS, D), BF16),
        pltpu.VMEM((ROWS, D), BF16),
    ],
)


def turn_back(values, cosine, sine):
    return values * cosine - swapped(values) * sine


def query_back_kernel(
    s_ref, dq, nq, inv, gain, cos, sin, ar, a0, a1, a2, a3, dwqk_o, dwqs_o, da_o, qg_o, grads
):
    cosine = cos[...]
    sine = sin[...]
    inv_q = inv[:, 0:1]
    dot = jnp.zeros((ROWS, 1), F32)
    for g in range(8):
        at = block(g, 128)
        back = turn_back(dq[:, at], cosine, sine)
        near = nq[:, at]
        qg_o[0:1, at] = jnp.sum(back * near, axis=0, keepdims=True)
        scaled = back * gain[0:1, 2 * D + g * 128 : 2 * D + (g + 1) * 128]
        dot = dot + jnp.sum(scaled * near, axis=1, keepdims=True)
        grads[:, at] = scaled
    pre = (inv_q * (grads[...] - nq[...] * (dot / D))).astype(BF16)
    for k, part in enumerate((a0, a1, a2, a3)):
        da_o[:, block(k, QUART)] = nt(pre, part[0:QUART, 0:D])
        out = (dwqk_o, dwqs_o)[k % 2]
        out[k // 2] = tn(ar[:, block(k, QUART)], pre).astype(BF16)


query_back = whole_call(
    query_back_kernel,
    "query_back",
    [
        shaped((2, QUART, D), BF16),
        shaped((2, QUART, D), BF16),
        shaped((ROWS, D), F32),
        shaped((8, D), F32),
    ],
    scratch=[pltpu.VMEM((ROWS, D), F32)],
)


def key_back_kernel(
    s_ref, kv_keep, kv_come, dk, dv, nk, inv, gain, cos, sin, ar, xr, hgrad, da_q, qg, small,
    a0, a1, a2, a3, keep_o, send_o, xp_o, xc_o, grads, both, da, cols
):
    place = s_ref[0]
    cosine = cos[...]
    sine = sin[...]
    inv_k = inv[:, 1:2]
    grads[0:HALF, :] = kv_keep[:, 0:KVW].astype(F32) + kv_come[:, 0:KVW].astype(F32)
    grads[HALF:ROWS, :] = dk[...]
    both[0:HALF, KVW:D] = (kv_keep[:, KVW:D].astype(F32) + kv_come[:, KVW:D].astype(F32)).astype(BF16)
    both[HALF:ROWS, KVW:D] = dv[...].astype(BF16)
    cols[...] = jnp.zeros_like(cols)
    dot = jnp.zeros((ROWS, 1), F32)
    for g in range(4):
        at = block(g, 128)
        back = turn_back(grads[:, at], cosine, sine)
        near = nk[:, at]
        kgrad = jnp.sum(back * near, axis=0, keepdims=True)
        cols[3:4, spot(place ^ g, QUART)] = jnp.concatenate([kgrad, jnp.zeros_like(kgrad)], axis=1)
        scaled = back * gain[0:1, 3 * D + g * 128 : 3 * D + (g + 1) * 128]
        dot = dot + jnp.sum(scaled * near, axis=1, keepdims=True)
        grads[:, at] = scaled
    both[:, 0:KVW] = (inv_k * (grads[...] - nk[...] * (dot / KVW))).astype(BF16)
    pre = both[...]
    for k, part in enumerate((a0, a1, a2, a3)):
        da[:, block(k, QUART)] = da_q[:, block(k, QUART)] + nt(pre, part[0:QUART, D:QKVW])
        out = (keep_o, send_o)[k % 2]
        out[k // 2, :, 0:D] = tn(ar[:, block(k, QUART)], pre).astype(BF16)
    x = xr[...].astype(F32)
    inverse = inv[:, 2:3]
    n1 = x * inverse
    grad = da[...]
    cols[0:1, :] = jnp.sum(grad * n1, axis=0, keepdims=True)
    cols[1:2, :] = small[1:2, :]
    cols[16:32, :] = small[16:32, :]
    for k in range(4):
        cols[2:3, block(k, QUART)] = qg[0:1, spot(place ^ k, QUART)]
    for k in range(4):
        out = (keep_o, send_o)[k % 2]
        out[k // 2, :, D:BOUT] = cols[:, block(k, QUART)].T.astype(BF16)
    scaled = grad * gain[0:1, 0:D]
    result = hgrad[...] + inverse * (scaled - n1 * jnp.mean(scaled * n1, axis=1, keepdims=True))
    low = result.astype(BF16)
    for k in range(4):
        there = spot(place ^ k, QUART)
        xp_o[:, there] = low[0:HALF, block(k, QUART)]
        xc_o[:, there] = low[HALF:ROWS, block(k, QUART)]


key_back = whole_call(
    key_back_kernel,
    "key_back",
    [
        shaped((2, QUART, BOUT), BF16),
        shaped((2, QUART, BOUT), BF16),
        shaped((HALF, D), BF16),
        shaped((HALF, D), BF16),
    ],
    scratch=[
        pltpu.VMEM((ROWS, KVW), F32),
        pltpu.VMEM((ROWS, D), BF16),
        pltpu.VMEM((ROWS, D), F32),
        pltpu.VMEM((128, D), F32),
    ],
)


def finish_kernel(s_ref, hid, keep, come, xp_o, xc_o):
    total = hid[...] + RESIDUAL_SCALE * (keep[...].astype(F32) + come[...].astype(F32))
    low = total.astype(BF16)
    for k in range(4):
        there = spot(s_ref[0] ^ k, QUART)
        xp_o[:, there] = low[0:HALF, block(k, QUART)]
        xc_o[:, there] = low[HALF:ROWS, block(k, QUART)]


finish = whole_call(
    finish_kernel,
    "finish",
    [shaped((HALF, D), BF16), shaped((HALF, D), BF16)],
)


def unpack_kernel(s_ref, z_ref, y_ref, a0, a1, a2, a3, b0, b1, b2, b3, gate_o, up_o, down_o, tile):
    for r in range(4):
        z_there = (z_ref[0] + 4 - r) % 4
        for n in range(4):
            y_there = (y_ref[0] + 4 - n) % 4
            rows = spot(z_there * 4 + y_there, PROWS)
            for k in range(2):
                tile[k, rows, :] = (a0, a1, a2, a3)[r][n, k, 0]
                tile[2 + k, rows, :] = (b0, b1, b2, b3)[n][r, k, 0]
    for k in range(4):
        there = spot(s_ref[0] ^ k, FSLICE)
        part = tile[k].astype(F32)
        gate_o[0, :, there] = part[:, 0:FSLICE]
        up_o[0, :, there] = part[:, FSLICE : 2 * FSLICE]
        down_o[0, there, :] = part[:, 2 * FSLICE :].T


def unpack_experts(place, z, y, a_parts, b_parts):
    part = pl.BlockSpec((4, 2, 1, PROWS, TILE), lambda e: (0, 0, e, 0, 0))
    return pl.pallas_call(
        unpack_kernel,
        name="unpack_experts",
        grid=(EXPERTS,),
        in_specs=[SMEM] * 3 + [part] * 8,
        out_specs=[
            pl.BlockSpec((1, QUART, 512), lambda e: (e, 0, 0)),
            pl.BlockSpec((1, QUART, 512), lambda e: (e, 0, 0)),
            pl.BlockSpec((1, 512, QUART), lambda e: (e, 0, 0)),
        ],
        out_shape=[
            shaped((EXPERTS, QUART, 512), F32),
            shaped((EXPERTS, QUART, 512), F32),
            shaped((EXPERTS, 512, QUART), F32),
        ],
        scratch_shapes=[pltpu.VMEM((4, QUART, TILE), BF16)],
        cost_estimate=COST,
    )(place, z, y, *a_parts, *b_parts)


LEFT = D + KVW
RIGHT = ATTW - LEFT


def unpack_attention_kernel(
    z_ref, y_ref, a0, a1, a2, a3, b0, b1, b2, b3, wq_o, wk_o, wv_o, wo_o, small_o, left, right
):
    for r in range(4):
        z_there = (z_ref[0] + 4 - r) % 4
        for n in range(4):
            y_there = (y_ref[0] + 4 - n) % 4
            rows = spot(z_there * 4 + y_there, PROWS)
            left[rows, :] = (a0, a1, a2, a3)[r][n]
            right[rows, :] = (b0, b1, b2, b3)[n][r]
    wq_o[...] = left[:, 0:D].astype(F32)
    wk_o[...] = left[:, D:LEFT].astype(F32)
    wv_o[...] = right[:, 0:KVW].astype(F32)
    for g in range(4):
        wo_o[block(g, QUART), :] = right[:, KVW + g * QUART : KVW + (g + 1) * QUART].astype(F32)
    small_o[...] = right[:, KVW + D :].astype(F32)


def unpack_attention(z, y, a_parts, b_parts):
    return pl.pallas_call(
        unpack_attention_kernel,
        name="unpack_attention",
        in_specs=[SMEM] * 2 + [VMEM] * 8,
        out_specs=[VMEM] * 5,
        out_shape=[
            shaped((QUART, D), F32),
            shaped((QUART, KVW), F32),
            shaped((QUART, KVW), F32),
            shaped((D, QUART), F32),
            shaped((QUART, 128), F32),
        ],
        scratch_shapes=[pltpu.VMEM((QUART, LEFT), BF16), pltpu.VMEM((QUART, RIGHT), BF16)],
        compiler_params=pltpu.CompilerParams(vmem_limit_bytes=32 * 1024 * 1024),
        cost_estimate=COST,
    )(z, y, *a_parts, *b_parts)


def body(
    prompt_x, cont_x, prompt_cot, cont_cot, prompt_routes, cont_routes,
    attn_gain, w_query, w_key, w_value, query_gain, key_gain,
    w_out, ffn_gain, w_router, w_gate, w_up, w_down,
):
    def moved(value, axes, change):
        sizes = [lax.axis_size(a) for a in axes]
        pairs = []
        count = 1
        for size in sizes:
            count *= size
        for index in range(count):
            rest, coords = index, []
            for size in reversed(sizes):
                coords.append(rest % size)
                rest //= size
            to = change(*reversed(coords))
            target = 0
            for size, coord in zip(sizes, to):
                target = target * size + coord
            pairs.append((index, target))
        return lax.ppermute(value, axes, pairs)

    def sib(value):
        return moved(value, ("c",), lambda c: (1 - c,))

    def far(value):
        return moved(value, ("xh",), lambda h: (1 - h,))

    def far_sib(value):
        return moved(value, ("xh", "c"), lambda h, c: (1 - h, 1 - c))

    def cross(value):
        return moved(value, ("xl", "xh"), lambda low, high: (1 - low, 1 - high))

    def cross_sib(value):
        return moved(value, ("xl", "xh", "c"), lambda low, high, c: (1 - low, 1 - high, 1 - c))

    def near(value):
        return moved(value, ("xl",), lambda low: (1 - low,))

    def gathered(value):
        return lax.all_gather(value, ("z", "y"), axis=0, tiled=True)

    def scattered(value):
        return lax.psum_scatter(value, ("z", "y"), scatter_dimension=0, tiled=True)

    def shifted(value, axis, by):
        return moved(value, (axis,), lambda at: ((at + by) % 4,))

    def spread(value, axis):
        return [value] + [shifted(value, axis, by) for by in (1, 2, 3)]

    def collected(blocks, axis):
        total = blocks(0).astype(F32)
        for by in (1, 2, 3):
            total = total + shifted(blocks(by), axis, by).astype(F32)
        return total.astype(BF16)

    after = lax.optimization_barrier

    z = lax.axis_index("z").astype(jnp.int32)
    y = lax.axis_index("y").astype(jnp.int32)
    position = lax.axis_index(("xh", "c")).astype(jnp.int32)
    piece = lax.axis_index(("z", "y"))
    place = position[None]
    cont_in = cont_x.reshape(HALF, D)
    cont_up = cont_cot.reshape(HALF, D)

    gains = jnp.concatenate(
        [attn_gain, ffn_gain, query_gain, key_gain, jnp.zeros((QKVW - 896,), F32)]
    )[None]
    router = jnp.concatenate([w_router.T, jnp.zeros((EXPERTS, QKVW - QUART), F32)], axis=1)
    own_in = jnp.concatenate(
        [
            jnp.concatenate([w_query, w_key, w_value], axis=1),
            gains,
            jnp.zeros((15, QKVW), F32),
            router,
            jnp.zeros((16 - EXPERTS, QKVW), F32),
        ],
        axis=0,
    ).astype(BF16)
    own_in, place = after((own_in, place))
    in_two = cross(own_in)
    packed = pack_experts(place, w_gate, w_up, w_down)
    own_share = lax.dynamic_slice_in_dim(packed[2], piece * PROWS, PROWS, axis=1)
    sib_share = lax.dynamic_slice_in_dim(packed[3], piece * PROWS, PROWS, axis=1)
    share_two = cross(own_share)
    share_three = cross_sib(sib_share)
    w_two = gathered(share_two[None])
    w_three = gathered(share_three[None])
    w_two = w_two.transpose(1, 0, 2, 3).reshape(EXPERTS, QUART, TILE)
    w_three = w_three.transpose(1, 0, 2, 3).reshape(EXPERTS, QUART, TILE)
    w_parts = (packed[0], sib(packed[1]), w_two, w_three)

    own_out, in_two_seen = after((w_out.astype(BF16), in_two))
    in_parts = (own_in, sib(own_in), in_two_seen, sib(in_two_seen))
    out_two = cross(own_out)
    upstream, out_two = after((jnp.concatenate([prompt_cot, cont_up], axis=0), out_two))
    out_parts = (own_out, sib(own_out), out_two, sib(out_two))
    up_two = cross(upstream)
    up_parts = (upstream, sib(upstream), up_two, sib(up_two))

    steps = jnp.arange(HALF, dtype=jnp.int32)
    positions = jnp.concatenate([position * HALF + steps, 4 * HALF + steps]).astype(F32)
    frequency = ROTARY_BASE ** (-jnp.arange(0, HDIM, 2).astype(F32) / HDIM)
    turned = positions[:, None] * frequency[None, :]
    cosine = jnp.tile(jnp.cos(turned), (1, 4))
    sine = jnp.tile(jnp.sin(turned), (1, 4))
    sine = jnp.where(jnp.arange(128)[None, :] % HDIM < HDIM // 2, -sine, sine)

    q, k, v, nq, nk, inv, xr, ar, gain, rt = project(
        place, prompt_x, cont_in, *in_parts, cosine, sine
    )
    kv = jnp.concatenate([k, v], axis=1)[:HALF]
    kv_two = far(kv)
    kv_parts = (sib(kv), kv_two, sib(kv_two))
    k_parts = (k, *(part[:, :KVW] for part in kv_parts))
    v_parts = (v, *(part[:, KVW:] for part in kv_parts))

    mixed, lse, hidden, b, gates = attend(
        place, q, *k_parts, *v_parts, *out_parts, xr, gain, rt,
        prompt_routes, cont_routes.reshape(HALF, 8),
    )
    b_two = cross(b)
    b_parts = (b, sib(b), b_two, sib(b_two))
    dudw, gz, db_keep, db_send = experts(place, b_parts, up_parts, w_parts)

    db_come = sib(db_send)
    db_sum = (db_keep.astype(F32) + db_come.astype(F32)).astype(BF16)
    db_sum, dudw = after((db_sum, dudw))
    db_far = cross(db_sum[1])
    grads = expert_grads(place, b_parts, up_parts, dudw, gz)
    grads, later = after((grads, place))
    summed = scattered(grads.reshape(-1, TILE))

    hgrad, small, dwo_keep, dwo_send, dq, kv_keep, kv_send, dk, dv = attend_back(
        later, db_sum[0], db_far, hidden, b, gates, prompt_cot, cont_up, gain, rt, mixed, lse,
        q, *k_parts, *v_parts, *out_parts,
    )

    kv_come = sib(kv_send)
    kv_sum = (kv_keep.astype(F32) + kv_come.astype(F32)).astype(BF16)
    kv_far = far(kv_sum[1])

    dwq_keep, dwq_send, da_q, qg = query_back(place, dq, nq, inv, gain, cosine, sine, ar, *in_parts)

    mix_keep, mix_send = mixture(place, gz, w_parts)
    mix_come = sib(mix_send)
    mix_sum = (mix_keep.astype(F32) + mix_come.astype(F32)).astype(BF16)
    mix_far = cross(mix_sum[1])
    prompt_out, cont_out = finish(place, hidden, mix_sum[0], mix_far)

    last_keep, last_send, prompt_grad, cont_grad = key_back(
        place, kv_sum[0], kv_far, dk, dv, nk, inv, gain, cosine, sine, ar, xr, hgrad, da_q, qg,
        small, *in_parts,
    )

    summed = summed.reshape(4, EXPERTS, PROWS, TILE)
    turned_parts = jnp.stack(
        [summed[0], sib(summed[1]), far(summed[2]), far_sib(summed[3])], axis=0
    )
    own_sum = (turned_parts.astype(F32) + near(turned_parts).astype(F32)).astype(BF16)
    part_a = spread(jnp.stack(spread(own_sum[0:2], "y")), "z")
    part_b = spread(jnp.stack(spread(own_sum[2:4], "z")), "y")
    gate_grad, up_grad, down_grad = unpack_experts(place, z[None], y[None], part_a, part_b)

    keep = jnp.concatenate([dwq_keep, last_keep[:, :, 0:D], dwo_keep, last_keep[:, :, D:]], axis=2)
    send = [dwq_send, last_send, dwo_send]
    come = [sib(part) for part in send]
    come = jnp.concatenate([come[0], come[1][:, :, 0:D], come[2], come[1][:, :, D:]], axis=2)
    paired = (keep.astype(F32) + come.astype(F32)).astype(BF16).reshape(2, 4, 4, PROWS, ATTW)

    def by_z(value):
        return lambda by: lax.dynamic_index_in_dim(value, (z + by) % 4, 0, keepdims=False)

    def by_y(value):
        return lambda by: lax.dynamic_index_in_dim(value, (y + by) % 4, 1, keepdims=False)

    def by_last(value, at):
        return lambda by: lax.dynamic_index_in_dim(value, (at + by) % 4, 0, keepdims=False)

    near_part = collected(by_last(collected(by_z(paired[0]), "z"), y), "y")
    far_part = collected(by_last(collected(by_y(paired[1]), "y"), z), "z")
    part = (near_part.astype(F32) + far(far_part).astype(F32)).astype(BF16)
    part = (part.astype(F32) + near(part).astype(F32)).astype(BF16)
    left = spread(jnp.stack(spread(part[:, 0:LEFT], "y")), "z")
    right = spread(jnp.stack(spread(part[:, LEFT:], "z")), "y")
    wq_grad, wk_grad, wv_grad, wo_grad, tail = unpack_attention(z[None], y[None], left, right)

    return (
        prompt_out,
        cont_out.reshape(1, HALF, D),
        prompt_grad,
        cont_grad.reshape(1, HALF, D),
        tail[:, 0],
        wq_grad,
        wk_grad,
        wv_grad,
        tail[:, 2],
        tail[0:HALF, 3],
        wo_grad,
        tail[:, 1],
        tail[:, 16 : 16 + EXPERTS],
        gate_grad,
        up_grad,
        down_grad,
    )


def solution(mesh):
    fine = Mesh(mesh.devices.reshape(2, 4, 4, 2, 2), AXES)
    shard = ("xh", "c")
    tokens = P(AXES, None)
    series = P(AXES, None, None)
    weights = (
        P(shard),
        P(shard, None),
        P(shard, None),
        P(shard, None),
        P(shard),
        P(shard),
        P(None, shard),
        P(shard),
        P(shard, None),
        P(None, shard, None),
        P(None, shard, None),
        P(None, None, shard),
    )
    return jax.shard_map(
        body,
        mesh=fine,
        in_specs=(tokens, series, tokens, series, tokens, series, *weights),
        out_specs=(tokens, series, tokens, series, *weights),
        check_vma=False,
    )
```

```python
import jax
import jax.numpy as jnp
import numpy as np
from jax import lax
from jax.experimental import pallas as pl
from jax.experimental.pallas import tpu as pltpu
from jax.sharding import Mesh, PartitionSpec as P

EPSILON = 1e-06
SCORE_SCALE = 0.25
RESIDUAL_SCALE = 0.22
ROTARY_BASE = 10000.0
MASKED = -1e30

D = 1024
HDIM = 64
PAIRS = 4
KVW = 512
QKVW = 2048
ROWS = 256
HALF = 128
QUART = 256
EXPERTS = 9
FSLICE = 128
TILE = 3 * FSLICE
TOKENS = 4 * ROWS
KEYS = 5 * HALF
BOUT = D + 128
ATTW = QKVW + D + 128
PIECES = 16
PROWS = QUART // PIECES

F32 = jnp.float32
BF16 = jnp.bfloat16


def angle_tables():
    frequency = np.float32(ROTARY_BASE) ** (-np.arange(0, HDIM, 2, dtype=np.float32) / HDIM)
    turned = np.arange(KEYS, dtype=np.float32)[:, None] * frequency.astype(np.float32)[None, :]
    cosine = np.tile(np.cos(turned), (1, 4)).astype(np.float32)
    sine = np.sin(turned)
    sine = np.concatenate([-sine, sine, -sine, sine], axis=1).astype(np.float32)
    return cosine, sine


AXES = ("xl", "z", "y", "xh", "c")


def nn(left, right):
    return lax.dot_general(left, right, (((1,), (0,)), ((), ())), preferred_element_type=F32)


def nt(left, right):
    return lax.dot_general(left, right, (((1,), (1,)), ((), ())), preferred_element_type=F32)


def tn(left, right):
    return lax.dot_general(left, right, (((0,), (0,)), ((), ())), preferred_element_type=F32)


def spot(index, width):
    return pl.ds(pl.multiple_of(index * width, width), width)


def block(index, width):
    return slice(index * width, (index + 1) * width)


SMEM = pl.BlockSpec(memory_space=pltpu.SMEM)
VMEM = pl.BlockSpec(memory_space=pltpu.VMEM)


COST = pl.CostEstimate(flops=1_000_000, bytes_accessed=1_000_000, transcendentals=0)


def whole_call(kernel, name, out_shape, scratch=(), limit=56):
    def call(*operands):
        return pl.pallas_call(
            kernel,
            name=name,
            out_shape=out_shape,
            in_specs=[SMEM] + [VMEM] * (len(operands) - 1),
            out_specs=jax.tree.map(lambda _: VMEM, out_shape),
            scratch_shapes=list(scratch),
            compiler_params=pltpu.CompilerParams(vmem_limit_bytes=limit * 1024 * 1024),
            cost_estimate=COST,
        )(*operands)

    return call


def shaped(shape, dtype):
    return jax.ShapeDtypeStruct(shape, dtype)


def pack_kernel(s_ref, gate, up, down, *outs):
    for k in range(2):
        spotted = spot(s_ref[0] ^ k, FSLICE)
        outs[k][0, :, 0:FSLICE] = gate[0, :, spotted].astype(BF16)
        outs[k][0, :, FSLICE : 2 * FSLICE] = up[0, :, spotted].astype(BF16)
        outs[k][0, :, 2 * FSLICE :] = down[0, spotted, :].T.astype(BF16)


def pack_experts(place, w_gate, w_up, w_down):
    return pl.pallas_call(
        pack_kernel,
        name="pack_experts",
        grid=(EXPERTS,),
        in_specs=[
            SMEM,
            pl.BlockSpec((1, QUART, 512), lambda e: (e, 0, 0)),
            pl.BlockSpec((1, QUART, 512), lambda e: (e, 0, 0)),
            pl.BlockSpec((1, 512, QUART), lambda e: (e, 0, 0)),
        ],
        out_specs=[pl.BlockSpec((1, QUART, TILE), lambda e: (e, 0, 0))] * 2,
        out_shape=[shaped((EXPERTS, QUART, TILE), BF16)] * 2,
        cost_estimate=COST,
    )(place, w_gate, w_up, w_down)


def share_kernel(at_ref, gate, up, down, two, three, turned):
    for k, out in ((2, two), (3, three)):
        there = spot(at_ref[1] ^ k, FSLICE)
        out[:, :, 0:FSLICE] = gate[:, :, there].astype(BF16)
        out[:, :, FSLICE : 2 * FSLICE] = up[:, :, there].astype(BF16)
        for e in range(EXPERTS):
            turned[...] = down[e, there, :].T
            out[e, :, 2 * FSLICE :] = turned[spot(at_ref[0] % 8, PROWS), :].astype(BF16)


def share_experts(at, w_gate, w_up, w_down):
    rows = pl.BlockSpec((EXPERTS, PROWS, 512), lambda i, at: (0, at[0], 0))
    out = pl.BlockSpec((EXPERTS, PROWS, TILE), lambda i, at: (0, 0, 0))
    return pl.pallas_call(
        share_kernel,
        name="share_experts",
        grid_spec=pltpu.PrefetchScalarGridSpec(
            num_scalar_prefetch=1,
            grid=(1,),
            in_specs=[
                rows,
                rows,
                pl.BlockSpec((EXPERTS, 512, 128), lambda i, at: (0, 0, at[0] // 8)),
            ],
            out_specs=[out, out],
            scratch_shapes=[pltpu.VMEM((128, FSLICE), F32)],
        ),
        out_shape=[shaped((EXPERTS, PROWS, TILE), BF16)] * 2,
        compiler_params=pltpu.CompilerParams(vmem_limit_bytes=32 * 1024 * 1024),
        cost_estimate=COST,
    )(at, w_gate, w_up, w_down)


def prepare_kernel(s_ref, wk, wv, attn, ffn, query, key, router, kv_o, line, wide):
    kv_o[0:QUART, 0:KVW] = wk[...].astype(BF16)
    kv_o[0:QUART, KVW:D] = wv[...].astype(BF16)
    line[...] = jnp.zeros_like(line)
    line[0:1, 0:256] = attn[...]
    line[0:1, 256:512] = ffn[...]
    line[0:1, 512:768] = query[...]
    line[0:1, 768:896] = key[...]
    kv_o[QUART : QUART + 16, :] = line[...].astype(BF16)
    wide[...] = jnp.zeros_like(wide)
    wide[:, 0:EXPERTS] = router[...]
    line[:, 0:QUART] = wide[...].T[0:16]
    kv_o[QUART + 16 :, :] = line[...].astype(BF16)


prepare = whole_call(
    prepare_kernel,
    "prepare",
    shaped((QUART + 32, D), BF16),
    scratch=[pltpu.VMEM((16, D), F32), pltpu.VMEM((QUART, 128), F32)],
)


def swapped(values):
    lane = lax.broadcasted_iota(jnp.int32, values.shape, 1)
    return jnp.where(
        lane % HDIM < HDIM // 2, pltpu.roll(values, 96, axis=1), pltpu.roll(values, 32, axis=1)
    )


def here(place, table):
    return jnp.concatenate([table[spot(place, HALF), :], table[4 * HALF :, :]], axis=0)


def project_keys_kernel(
    s_ref, xp, xc, a0, a1, a2, a3, cos, sin, kv_o, kvp_o, nk_o, inv_o, xr_o, ar_o, gain_o, rt_o, acc
):
    parts = (a0, a1, a2, a3)
    for k in range(4):
        there = s_ref[0] ^ k
        xr_o[0:HALF, block(k, QUART)] = xp[:, spot(there, QUART)]
        xr_o[HALF:ROWS, block(k, QUART)] = xc[:, spot(there, QUART)]
        small = parts[k][QUART : QUART + 16, :].astype(F32)[0:1]
        gain_o[0:1, block(k, QUART)] = small[:, 0:256]
        gain_o[0:1, slice(D + k * QUART, D + (k + 1) * QUART)] = small[:, 256:512]
        gain_o[0:1, pl.ds(pl.multiple_of(2 * D + there * QUART, 128), QUART)] = small[:, 512:768]
        gain_o[0:1, pl.ds(pl.multiple_of(3 * D + there * HALF, 128), HALF)] = small[:, 768:896]
        rt_o[:, block(k, QUART)] = parts[k][QUART + 16 : QUART + 32, 0:QUART]
    x = xr_o[...].astype(F32)
    inverse = lax.rsqrt(jnp.mean(x * x, axis=1, keepdims=True) + EPSILON)
    ar_o[...] = (x * inverse * gain_o[0:1, 0:D]).astype(BF16)
    total = nn(ar_o[:, block(0, QUART)], parts[0][0:QUART, :])
    for k in range(1, 4):
        total = total + nn(ar_o[:, block(k, QUART)], parts[k][0:QUART, :])
    acc[...] = total
    kp = acc[:, 0:KVW]
    inv_k = lax.rsqrt(jnp.mean(kp * kp, axis=1, keepdims=True) + EPSILON)
    nk_o[...] = kp * inv_k
    lane = lax.broadcasted_iota(jnp.int32, (ROWS, 128), 1)
    inv_o[...] = jnp.where(lane == 1, inv_k, inverse)
    kv_o[:, KVW:D] = acc[:, KVW:D].astype(BF16)
    cosine = here(s_ref[0], cos)
    sine = here(s_ref[0], sin)
    for g in range(4):
        at = block(g, 128)
        u = nk_o[:, at] * gain_o[0:1, 3 * D + g * 128 : 3 * D + (g + 1) * 128]
        kv_o[:, at] = (u * cosine + swapped(u) * sine).astype(BF16)
    kvp_o[...] = kv_o[0:HALF, :]


project_keys = whole_call(
    project_keys_kernel,
    "project_keys",
    [
        shaped((ROWS, D), BF16),
        shaped((HALF, D), BF16),
        shaped((ROWS, KVW), F32),
        shaped((ROWS, 128), F32),
        shaped((ROWS, D), BF16),
        shaped((ROWS, D), BF16),
        shaped((8, 3 * D + KVW), F32),
        shaped((16, D), BF16),
    ],
    scratch=[pltpu.VMEM((ROWS, D), F32)],
)


def project_query_kernel(s_ref, ar, gain, a0, a1, a2, a3, cos, sin, q_o, nq_o, inv_o):
    total = nn(ar[:, block(0, QUART)], a0[...])
    for k, part in ((1, a1), (2, a2), (3, a3)):
        total = total + nn(ar[:, block(k, QUART)], part[...])
    nq_o[...] = total
    inv_q = lax.rsqrt(jnp.mean(total * total, axis=1, keepdims=True) + EPSILON)
    inv_o[...] = jnp.broadcast_to(inv_q, (ROWS, 128))
    cosine = here(s_ref[0], cos)
    sine = here(s_ref[0], sin)
    for g in range(8):
        at = block(g, 128)
        near = nq_o[:, at] * inv_q
        nq_o[:, at] = near
        u = near * gain[0:1, 2 * D + g * 128 : 2 * D + (g + 1) * 128]
        q_o[:, at] = (u * cosine + swapped(u) * sine).astype(BF16)


project_query = whole_call(
    project_query_kernel,
    "project_query",
    [shaped((ROWS, D), BF16), shaped((ROWS, D), F32), shaped((ROWS, 128), F32)],
)


def fill_bias(place, bias):
    row = lax.broadcasted_iota(jnp.int32, (HALF, 512), 0)
    lane = lax.broadcasted_iota(jnp.int32, (HALF, 512), 1)
    causal = jnp.where(row <= lane % HALF, 0.0, MASKED)
    is_prompt = lane % ROWS < HALF
    bias[0:HALF, :] = jnp.where(is_prompt, causal, 0.0)
    for k in range(1, 4):
        level = jnp.where((place ^ k) < place, 0.0, MASKED)
        bias[block(k, HALF), :] = jnp.where(is_prompt, level, 0.0)
    bias[4 * HALF :, :] = jnp.where(is_prompt, MASKED, causal)


def fill_keys(refs, keys, values):
    for j in range(4):
        keys[block(j, HALF), :] = refs[j][0:HALF, 0:KVW]
        values[block(j, HALF), :] = refs[j][0:HALF, KVW:D]
    keys[4 * HALF :, :] = refs[0][HALF:ROWS, 0:KVW]
    values[4 * HALF :, :] = refs[0][HALF:ROWS, KVW:D]


def doubled(ref, pair, odd):
    both = ref[:, spot(pair, 128)]
    other = pltpu.roll(both.astype(F32), HDIM, axis=1).astype(BF16)
    lane = lax.broadcasted_iota(jnp.int32, both.shape, 1)
    return jnp.where((lane < HDIM) == (odd == 0), both, other)


def stacked(ref, head, scale):
    rows = ref[:, spot(head, 128)]
    lane = lax.broadcasted_iota(jnp.int32, rows.shape, 1)
    rows = rows * jnp.asarray(scale, rows.dtype)
    none = jnp.zeros_like(rows)
    return jnp.concatenate(
        [jnp.where(lane < HDIM, rows, none), jnp.where(lane < HDIM, none, rows)], axis=0
    )


def attend_kernel(s_ref, q, kv0, kv1, kv2, kv3, mixed_o, lse_o, bias, keys, values):
    fill_bias(s_ref[0], bias)
    fill_keys((kv0, kv1, kv2, kv3), keys, values)

    def one_pair(pair, carry):
        for odd in range(2):
            head = 2 * pair + odd
            kk = doubled(keys, pair, odd)
            vv = doubled(values, pair, odd)
            scores = nt(kk, stacked(q, head, SCORE_SCALE)) + bias[...]
            highest = jnp.max(scores, axis=0, keepdims=True)
            raised = jnp.exp(scores - highest)
            totals = jnp.sum(raised, axis=0, keepdims=True)
            probs = (raised * (1.0 / totals)).astype(BF16)
            lse_o[pl.ds(head, 1), :] = highest + jnp.log(totals)
            out = tn(vv, probs).T
            lane = lax.broadcasted_iota(jnp.int32, (ROWS, 128), 1)
            mixed_o[:, spot(head, 128)] = jnp.where(
                lane < HDIM, out[0:ROWS], out[ROWS : 2 * ROWS]
            ).astype(BF16)
        return carry

    lax.fori_loop(0, PAIRS, one_pair, 0)


attend = whole_call(
    attend_kernel,
    "attend",
    [shaped((ROWS, D), BF16), shaped((8, 512), F32)],
    scratch=[
        pltpu.VMEM((KEYS, 512), F32),
        pltpu.VMEM((KEYS, KVW), BF16),
        pltpu.VMEM((KEYS, KVW), BF16),
    ],
)


def route_kernel(
    s_ref, mixed_ref, o0, o1, o2, o3, xr, gain, rt, rp, rc, hid_o, b_o, gates_o
):
    mixed = mixed_ref[...]
    for k, part in enumerate((o0, o1, o2, o3)):
        hid_o[:, block(k, QUART)] = xr[:, block(k, QUART)].astype(F32) + RESIDUAL_SCALE * nn(
            mixed, part[...]
        )
    hidden = hid_o[...]
    inverse = lax.rsqrt(jnp.mean(hidden * hidden, axis=1, keepdims=True) + EPSILON)
    b_o[:, 0:D] = (hidden * inverse * gain[0:1, D : 2 * D]).astype(BF16)
    logits = nt(b_o[:, 0:D], rt[...])
    expert = lax.broadcasted_iota(jnp.int32, (HALF, 16), 1)
    for half, routes in enumerate((rp, rc)):
        chosen = routes[:, 0:1] == expert
        for r in range(1, 8):
            chosen = chosen | (routes[:, r : r + 1] == expert)
        level = jnp.where(chosen, logits[block(half, HALF)], MASKED)
        raised = jnp.exp(level - jnp.max(level, axis=1, keepdims=True))
        gates = raised / jnp.sum(raised, axis=1, keepdims=True)
        gates_o[block(half, HALF), 0:16] = gates
        high = gates.astype(BF16).astype(F32)
        b_o[block(half, HALF), D:BOUT] = jnp.concatenate(
            [high, gates - high, jnp.zeros((HALF, 96), F32)], axis=1
        ).astype(BF16)


route = whole_call(
    route_kernel,
    "route",
    [shaped((ROWS, D), F32), shaped((ROWS, BOUT), BF16), shaped((ROWS, 128), F32)],
)


def piece_at(at, r, n):
    return ((at[0] + 4 - r) % 4) * at[2] + ((at[1] + 4 - n) % 4) * at[3]


def fill_weights(at, own, other, far_parts, e, dest, lanes):
    dest[block(0, QUART), lanes] = own[e]
    dest[block(1, QUART), lanes] = other[e]
    for r in range(4):
        for n in range(4):
            piece = piece_at(at, r, n)
            for k in range(2):
                dest[spot((2 + k) * PIECES + piece, PROWS), lanes] = far_parts[r][n, k, e]


def expert_kernel(
    s_ref, at_ref, b0, b1, b2, b3, g0, g1, g2, g3, w0, w1, f0, f1, f2, f3,
    dudw_o, gz_o, dbk_o, dbs_o, xs, gs, gates, dgs, wgu, ws
):
    e = pl.program_id(0)
    place = s_ref[0]

    @pl.when(e == 0)
    def _():
        for j, (b_ref, g_ref) in enumerate(zip((b0, b1, b2, b3), (g0, g1, g2, g3))):
            rows = block(j, ROWS)
            for k in range(4):
                xs[rows, block(k, QUART)] = b_ref[:, block(k ^ j, QUART)]
                gs[rows, block(k, QUART)] = g_ref[:, spot(place ^ k, QUART)]
            both = b_ref[:, D:BOUT].astype(F32)
            gates[rows, :] = both + pltpu.roll(both, 112, axis=1)
        dgs[...] = jnp.zeros_like(dgs)

    fill_weights(at_ref, w0, w1, (f0, f1, f2, f3), 0, ws, slice(None))
    wgu[:, spot(e, 2 * FSLICE)] = ws[:, 0 : 2 * FSLICE]
    both = nn(xs[...], ws[:, 0 : 2 * FSLICE])
    h = RESIDUAL_SCALE * nn(gs[...], ws[:, 2 * FSLICE :])
    u = both[:, 0:FSLICE]
    w = both[:, FSLICE:]
    lane = lax.broadcasted_iota(jnp.int32, (TOKENS, 128), 1)
    gate = jnp.sum(jnp.where(lane == e, gates[...], 0.0), axis=1, keepdims=True)
    sig = jax.nn.sigmoid(u)
    silu = u * sig
    z = (silu * w).astype(BF16).astype(F32)
    gz_o[:, spot(e, FSLICE)] = (gate * z).astype(BF16)
    dgate = jnp.sum(z * h, axis=1, keepdims=True)
    dgs[...] += jnp.where(lane == e, dgate, 0.0)
    dz = gate * h
    du = (dz * w * sig * (1.0 + u * (1.0 - sig))).astype(BF16)
    dw = (dz * silu).astype(BF16)
    dudw_o[:, spot(e, 2 * FSLICE)] = jnp.concatenate([du, dw], axis=1)

    @pl.when(e == EXPERTS - 1)
    def _():
        for j in range(4):
            out = (dbk_o, dbs_o)[j % 2]
            rows = block(j, ROWS)
            total = nt(dudw_o[rows, :], wgu[...]).astype(BF16)
            for k in range(4):
                out[j // 2, :, block(k ^ j, QUART)] = total[:, block(k, QUART)]
            dg = dgs[rows, 0:16]
            high = dg.astype(BF16).astype(F32)
            out[j // 2, :, D:BOUT] = jnp.concatenate(
                [high, dg - high, jnp.zeros((ROWS, 96), F32)], axis=1
            ).astype(BF16)


def fixed(rank):
    return lambda e: (0,) * rank


def experts(place, at, b_parts, g_parts, w_parts):
    return pl.pallas_call(
        expert_kernel,
        name="experts",
        grid=(EXPERTS,),
        in_specs=[SMEM] * 2
        + [pl.BlockSpec((ROWS, BOUT), fixed(2))] * 4
        + [pl.BlockSpec((ROWS, D), fixed(2))] * 4
        + [pl.BlockSpec((1, QUART, TILE), lambda e: (e, 0, 0))] * 2
        + [pl.BlockSpec((4, 2, 1, PROWS, TILE), lambda e: (0, 0, e, 0, 0))] * 4,
        out_specs=[
            pl.BlockSpec((TOKENS, EXPERTS * 2 * FSLICE), fixed(2)),
            pl.BlockSpec((TOKENS, EXPERTS * FSLICE), fixed(2)),
            pl.BlockSpec((2, ROWS, BOUT), fixed(3)),
            pl.BlockSpec((2, ROWS, BOUT), fixed(3)),
        ],
        out_shape=[
            shaped((TOKENS, EXPERTS * 2 * FSLICE), BF16),
            shaped((TOKENS, EXPERTS * FSLICE), BF16),
            shaped((2, ROWS, BOUT), BF16),
            shaped((2, ROWS, BOUT), BF16),
        ],
        scratch_shapes=[
            pltpu.VMEM((TOKENS, D), BF16),
            pltpu.VMEM((TOKENS, D), BF16),
            pltpu.VMEM((TOKENS, 128), F32),
            pltpu.VMEM((TOKENS, 128), F32),
            pltpu.VMEM((D, EXPERTS * 2 * FSLICE), BF16),
            pltpu.VMEM((D, TILE), BF16),
        ],
        compiler_params=pltpu.CompilerParams(vmem_limit_bytes=56 * 1024 * 1024),
        cost_estimate=COST,
    )(place, at, *b_parts, *g_parts, *w_parts)


def piece_to(at, r, v):
    return ((at[0] + r) % 4) * at[2] + v * at[3]


def expert_grad_kernel(
    s_ref, at_ref, b0, b1, b2, b3, g0, g1, g2, g3, dudw, gz, t0, t1, t2, t3, xt, gt, tile
):
    @pl.when(pl.program_id(0) == 0)
    def _():
        for j, (b_ref, g_ref) in enumerate(zip((b0, b1, b2, b3), (g0, g1, g2, g3))):
            for k in range(4):
                xt[block(k, QUART), block(j, ROWS)] = b_ref[:, block(k ^ j, QUART)].T
                gt[block(k, QUART), block(j, ROWS)] = g_ref[:, spot(s_ref[0] ^ k, QUART)].T

    for k in range(4):
        rows = block(k, QUART)
        first = nn(xt[rows, :], dudw[...]).astype(BF16)
        second = (RESIDUAL_SCALE * nn(gt[rows, :], gz[...])).astype(BF16)
        tile[:, 0 : 2 * FSLICE] = first
        tile[:, 2 * FSLICE :] = second
        for r, out in enumerate((t0, t1, t2, t3)):
            for v in range(4):
                out[v, k, 0] = tile[spot(piece_to(at_ref, r, v), PROWS), :]


def expert_grads(place, at, b_parts, g_parts, dudw, gz):
    return pl.pallas_call(
        expert_grad_kernel,
        name="expert_grads",
        grid=(EXPERTS,),
        in_specs=[SMEM] * 2
        + [pl.BlockSpec((ROWS, BOUT), fixed(2))] * 4
        + [pl.BlockSpec((ROWS, D), fixed(2))] * 4
        + [
            pl.BlockSpec((TOKENS, 2 * FSLICE), lambda e: (0, e)),
            pl.BlockSpec((TOKENS, FSLICE), lambda e: (0, e)),
        ],
        out_specs=[pl.BlockSpec((4, 4, 1, PROWS, TILE), lambda e: (0, 0, e, 0, 0))] * 4,
        out_shape=[shaped((4, 4, EXPERTS, PROWS, TILE), BF16)] * 4,
        scratch_shapes=[
            pltpu.VMEM((D, TOKENS), BF16),
            pltpu.VMEM((D, TOKENS), BF16),
            pltpu.VMEM((QUART, TILE), BF16),
        ],
        compiler_params=pltpu.CompilerParams(vmem_limit_bytes=56 * 1024 * 1024),
        cost_estimate=pl.CostEstimate(
            flops=EXPERTS * 2 * TOKENS * D * TILE, bytes_accessed=16_000_000, transcendentals=0
        ),
    )(place, at, *b_parts, *g_parts, dudw, gz)


def mixture_kernel(at_ref, gz, w0, w1, f0, f1, f2, f3, keep_o, send_o, wide):
    for e in range(EXPERTS):
        fill_weights(at_ref, w0, w1, (f0, f1, f2, f3), e, wide, block(e, FSLICE))
    for j in range(4):
        out = (keep_o, send_o)[j % 2]
        total = nt(gz[block(j, ROWS), :], wide[...]).astype(BF16)
        for k in range(4):
            out[j // 2, :, block(k ^ j, QUART)] = total[:, block(k, QUART)]


def mixture(at, gz, w_parts):
    down = [pl.BlockSpec((EXPERTS, QUART, FSLICE), lambda i: (0, 0, 2))] * 2 + [
        pl.BlockSpec((4, 2, EXPERTS, PROWS, FSLICE), lambda i: (0, 0, 0, 0, 2))
    ] * 4
    return pl.pallas_call(
        mixture_kernel,
        name="mixture",
        grid=(1,),
        in_specs=[SMEM, pl.BlockSpec((TOKENS, EXPERTS * FSLICE), fixed(2))] + down,
        out_specs=[pl.BlockSpec((2, ROWS, D), fixed(3))] * 2,
        out_shape=[shaped((2, ROWS, D), BF16)] * 2,
        scratch_shapes=[pltpu.VMEM((D, EXPERTS * FSLICE), BF16)],
        compiler_params=pltpu.CompilerParams(vmem_limit_bytes=56 * 1024 * 1024),
        cost_estimate=COST,
    )(at, gz, *w_parts)


def attend_back_kernel(
    s_ref, db_keep, db_come, hid, b, gates_ref, gp, gc, gain, rt, mixed, lse,
    q, kv0, kv1, kv2, kv3, o0, o1, o2, o3,
    hgrad_o, small_o, dwok_o, dwos_o, dq_o, kvk_o, kvs_o, dk_o, dv_o,
    bias, keys, values, dmix, grow
):
    place = s_ref[0]
    parts = (o0, o1, o2, o3)
    fill_bias(place, bias)
    fill_keys((kv0, kv1, kv2, kv3), keys, values)
    total = db_keep[...].astype(F32) + db_come[...].astype(F32)
    tail = total[:, D:BOUT]
    dgate = (tail + pltpu.roll(tail, 112, axis=1))[:, 0:16]
    gates = gates_ref[:, 0:16]
    dlog = (gates * (dgate - jnp.sum(gates * dgate, axis=1, keepdims=True))).astype(BF16)
    dbt = total[:, 0:D] + nn(dlog, rt[...])
    small_o[...] = jnp.zeros_like(small_o)
    small_o[16:32, :] = tn(dlog, b[:, 0:D])
    hidden = hid[...]
    inverse = lax.rsqrt(jnp.mean(hidden * hidden, axis=1, keepdims=True) + EPSILON)
    n2 = hidden * inverse
    small_o[1:2, :] = jnp.sum(dbt * n2, axis=0, keepdims=True)
    scaled = dbt * gain[0:1, D : 2 * D]
    for k in range(4):
        there = spot(place ^ k, QUART)
        grow[0:HALF, block(k, QUART)] = gp[:, there]
        grow[HALF:ROWS, block(k, QUART)] = gc[:, there]
    hgrad = grow[...].astype(F32) + inverse * (
        scaled - n2 * jnp.mean(scaled * n2, axis=1, keepdims=True)
    )
    hgrad_o[...] = hgrad
    agrad = (RESIDUAL_SCALE * hgrad).astype(BF16)
    whole = nt(agrad[:, block(0, QUART)], parts[0][...])
    for k in range(1, 4):
        whole = whole + nt(agrad[:, block(k, QUART)], parts[k][...])
    dmix[...] = whole.astype(BF16)
    for g in range(4):
        rows = tn(mixed[:, block(g, QUART)], agrad).astype(BF16)
        for k in range(4):
            out = (dwok_o, dwos_o)[k % 2]
            out[k // 2, :, block(g, QUART)] = rows[:, block(k, QUART)]

    def one_pair(pair, carry):
        dks = []
        dvs = []
        lane = lax.broadcasted_iota(jnp.int32, (ROWS, 128), 1)
        for odd in range(2):
            head = 2 * pair + odd
            kk = doubled(keys, pair, odd)
            vv = doubled(values, pair, odd)
            qs = stacked(q, head, SCORE_SCALE)
            ds_rows = stacked(dmix, head, 1.0)
            probs = jnp.exp(nt(kk, qs) + bias[...] - lse[pl.ds(head, 1), :])
            pgrad = nt(vv, ds_rows)
            inner = jnp.sum(probs * pgrad, axis=0, keepdims=True)
            sgrad = (probs * (pgrad - inner)).astype(BF16)
            dkr = nn(sgrad, qs)
            dvr = nn(probs.astype(BF16), ds_rows)
            dks.append(dkr + pltpu.roll(dkr, HDIM, axis=1))
            dvs.append(dvr + pltpu.roll(dvr, HDIM, axis=1))
            dqt = (SCORE_SCALE * tn(kk, sgrad)).T
            dq_o[:, spot(head, 128)] = jnp.where(lane < HDIM, dqt[0:ROWS], dqt[ROWS : 2 * ROWS])
        low = lax.broadcasted_iota(jnp.int32, (KEYS, 128), 1) < HDIM
        dk = jnp.where(low, dks[0], dks[1])
        dv = jnp.where(low, dvs[0], dvs[1])
        at = spot(pair, 128)
        at_v = spot(pair + 4, 128)
        for j in range(4):
            side = (kvk_o, kvs_o)[j % 2]
            side[j // 2, :, at] = dk[block(j, HALF)].astype(BF16)
            side[j // 2, :, at_v] = dv[block(j, HALF)].astype(BF16)
        dk_o[:, at] = dk[4 * HALF :]
        dv_o[:, at] = dv[4 * HALF :]
        return carry

    lax.fori_loop(0, PAIRS, one_pair, 0)


attend_back = whole_call(
    attend_back_kernel,
    "attend_back",
    [
        shaped((ROWS, D), F32),
        shaped((32, D), F32),
        shaped((2, QUART, D), BF16),
        shaped((2, QUART, D), BF16),
        shaped((ROWS, D), F32),
        shaped((2, HALF, D), BF16),
        shaped((2, HALF, D), BF16),
        shaped((HALF, KVW), F32),
        shaped((HALF, KVW), F32),
    ],
    scratch=[
        pltpu.VMEM((KEYS, 512), F32),
        pltpu.VMEM((KEYS, KVW), BF16),
        pltpu.VMEM((KEYS, KVW), BF16),
        pltpu.VMEM((ROWS, D), BF16),
        pltpu.VMEM((ROWS, D), BF16),
    ],
)


def turn_back(values, cosine, sine):
    return values * cosine - swapped(values) * sine


def query_back_kernel(
    s_ref, dq, nq, inv, gain, cos, sin, ar, a0, a1, a2, a3, dwqk_o, dwqs_o, da_o, qg_o, grads
):
    cosine = here(s_ref[0], cos)
    sine = here(s_ref[0], sin)
    inv_q = inv[:, 0:1]
    dot = jnp.zeros((ROWS, 1), F32)
    for g in range(8):
        at = block(g, 128)
        back = turn_back(dq[:, at], cosine, sine)
        near = nq[:, at]
        qg_o[0:1, at] = jnp.sum(back * near, axis=0, keepdims=True)
        scaled = back * gain[0:1, 2 * D + g * 128 : 2 * D + (g + 1) * 128]
        dot = dot + jnp.sum(scaled * near, axis=1, keepdims=True)
        grads[:, at] = scaled
    pre = (inv_q * (grads[...] - nq[...] * (dot / D))).astype(BF16)
    for k, part in enumerate((a0, a1, a2, a3)):
        da_o[:, block(k, QUART)] = nt(pre, part[0:QUART, 0:D])
        out = (dwqk_o, dwqs_o)[k % 2]
        out[k // 2] = tn(ar[:, block(k, QUART)], pre).astype(BF16)


query_back = whole_call(
    query_back_kernel,
    "query_back",
    [
        shaped((2, QUART, D), BF16),
        shaped((2, QUART, D), BF16),
        shaped((ROWS, D), F32),
        shaped((8, D), F32),
    ],
    scratch=[pltpu.VMEM((ROWS, D), F32)],
)


def key_back_kernel(
    s_ref, kv_keep, kv_come, dk, dv, nk, inv, gain, cos, sin, ar, xr, hgrad, da_q, qg, small,
    a0, a1, a2, a3, keep_o, send_o, xp_o, xc_o, grads, both, da, cols
):
    place = s_ref[0]
    cosine = here(s_ref[0], cos)
    sine = here(s_ref[0], sin)
    inv_k = inv[:, 1:2]
    grads[0:HALF, :] = kv_keep[:, 0:KVW].astype(F32) + kv_come[:, 0:KVW].astype(F32)
    grads[HALF:ROWS, :] = dk[...]
    both[0:HALF, KVW:D] = (kv_keep[:, KVW:D].astype(F32) + kv_come[:, KVW:D].astype(F32)).astype(BF16)
    both[HALF:ROWS, KVW:D] = dv[...].astype(BF16)
    cols[...] = jnp.zeros_like(cols)
    dot = jnp.zeros((ROWS, 1), F32)
    for g in range(4):
        at = block(g, 128)
        back = turn_back(grads[:, at], cosine, sine)
        near = nk[:, at]
        kgrad = jnp.sum(back * near, axis=0, keepdims=True)
        cols[3:4, spot(place ^ g, QUART)] = jnp.concatenate([kgrad, jnp.zeros_like(kgrad)], axis=1)
        scaled = back * gain[0:1, 3 * D + g * 128 : 3 * D + (g + 1) * 128]
        dot = dot + jnp.sum(scaled * near, axis=1, keepdims=True)
        grads[:, at] = scaled
    both[:, 0:KVW] = (inv_k * (grads[...] - nk[...] * (dot / KVW))).astype(BF16)
    pre = both[...]
    for k, part in enumerate((a0, a1, a2, a3)):
        da[:, block(k, QUART)] = da_q[:, block(k, QUART)] + nt(pre, part[0:QUART, :])
        out = (keep_o, send_o)[k % 2]
        out[k // 2, :, 0:D] = tn(ar[:, block(k, QUART)], pre).astype(BF16)
    x = xr[...].astype(F32)
    inverse = inv[:, 2:3]
    n1 = x * inverse
    grad = da[...]
    cols[0:1, :] = jnp.sum(grad * n1, axis=0, keepdims=True)
    cols[1:2, :] = small[1:2, :]
    cols[16:32, :] = small[16:32, :]
    for k in range(4):
        cols[2:3, block(k, QUART)] = qg[0:1, spot(place ^ k, QUART)]
    for k in range(4):
        out = (keep_o, send_o)[k % 2]
        out[k // 2, :, D:BOUT] = cols[:, block(k, QUART)].T.astype(BF16)
    scaled = grad * gain[0:1, 0:D]
    result = hgrad[...] + inverse * (scaled - n1 * jnp.mean(scaled * n1, axis=1, keepdims=True))
    low = result.astype(BF16)
    for k in range(4):
        there = spot(place ^ k, QUART)
        xp_o[:, there] = low[0:HALF, block(k, QUART)]
        xc_o[:, there] = low[HALF:ROWS, block(k, QUART)]


key_back = whole_call(
    key_back_kernel,
    "key_back",
    [
        shaped((2, QUART, BOUT), BF16),
        shaped((2, QUART, BOUT), BF16),
        shaped((HALF, D), BF16),
        shaped((HALF, D), BF16),
    ],
    scratch=[
        pltpu.VMEM((ROWS, KVW), F32),
        pltpu.VMEM((ROWS, D), BF16),
        pltpu.VMEM((ROWS, D), F32),
        pltpu.VMEM((128, D), F32),
    ],
)


def finish_kernel(s_ref, hid, keep, come, xp_o, xc_o):
    total = hid[...] + RESIDUAL_SCALE * (keep[...].astype(F32) + come[...].astype(F32))
    low = total.astype(BF16)
    for k in range(4):
        there = spot(s_ref[0] ^ k, QUART)
        xp_o[:, there] = low[0:HALF, block(k, QUART)]
        xc_o[:, there] = low[HALF:ROWS, block(k, QUART)]


finish = whole_call(
    finish_kernel,
    "finish",
    [shaped((HALF, D), BF16), shaped((HALF, D), BF16)],
)


def pair_kernel(at_ref, qk, qc, lk, lc, ok, oc, t0, t1, t2, t3, wide):
    for k in range(2):
        wide[:, 0:D] = qk[k].astype(F32) + qc[k].astype(F32)
        last = lk[k].astype(F32) + lc[k].astype(F32)
        wide[:, D:QKVW] = last[:, 0:D]
        wide[:, QKVW : QKVW + D] = ok[k].astype(F32) + oc[k].astype(F32)
        wide[:, QKVW + D :] = last[:, D:]
        for r, out in enumerate((t0, t1, t2, t3)):
            for v in range(4):
                out[v, k] = wide[spot(piece_to(at_ref, r, v), PROWS), :].astype(BF16)


pair = whole_call(
    pair_kernel,
    "pair",
    [shaped((4, 2, PROWS, ATTW), BF16)] * 4,
    scratch=[pltpu.VMEM((QUART, ATTW), F32)],
)


def fold_kernel(at_ref, i0, i1, i2, i3, o0, o1, o2, o3):
    for r, out in enumerate((o0, o1, o2, o3)):
        there = (at_ref[1] + r) % 4
        total = i0[there].astype(F32) + i1[there].astype(F32)
        out[...] = (total + i2[there].astype(F32) + i3[there].astype(F32)).astype(BF16)


def fold(at, parts, rows, steps):
    shape = parts[0].shape
    width = shape[-1]
    flat = [part.reshape(4, rows, width) for part in parts]
    height = rows // steps
    outs = pl.pallas_call(
        fold_kernel,
        name="fold",
        grid=(steps,),
        in_specs=[SMEM] + [pl.BlockSpec((4, height, width), lambda i: (0, i, 0))] * 4,
        out_specs=[pl.BlockSpec((height, width), lambda i: (i, 0))] * 4,
        out_shape=[shaped((rows, width), BF16)] * 4,
        compiler_params=pltpu.CompilerParams(vmem_limit_bytes=32 * 1024 * 1024),
        cost_estimate=COST,
    )(at, *flat)
    return [out.reshape(shape[1:]) for out in outs]


def unpack_kernel(s_ref, at_ref, p0, p1, p2, p3, gate_o, up_o, down_o, tile):
    for r, part in enumerate((p0, p1, p2, p3)):
        for n in range(4):
            rows = spot(piece_at(at_ref, r, n), PROWS)
            for k in range(4):
                tile[k, rows, :] = part[n, k, 0]
    for k in range(4):
        there = spot(s_ref[0] ^ k, FSLICE)
        part = tile[k].astype(F32)
        gate_o[0, :, there] = part[:, 0:FSLICE]
        up_o[0, :, there] = part[:, FSLICE : 2 * FSLICE]
        down_o[0, there, :] = part[:, 2 * FSLICE :].T


def unpack_experts(place, at, parts):
    part = pl.BlockSpec((4, 4, 1, PROWS, TILE), lambda e: (0, 0, e, 0, 0))
    return pl.pallas_call(
        unpack_kernel,
        name="unpack_experts",
        grid=(EXPERTS,),
        in_specs=[SMEM] * 2 + [part] * 4,
        out_specs=[
            pl.BlockSpec((1, QUART, 512), lambda e: (e, 0, 0)),
            pl.BlockSpec((1, QUART, 512), lambda e: (e, 0, 0)),
            pl.BlockSpec((1, 512, QUART), lambda e: (e, 0, 0)),
        ],
        out_shape=[
            shaped((EXPERTS, QUART, 512), F32),
            shaped((EXPERTS, QUART, 512), F32),
            shaped((EXPERTS, 512, QUART), F32),
        ],
        scratch_shapes=[pltpu.VMEM((4, QUART, TILE), BF16)],
        compiler_params=pltpu.CompilerParams(vmem_limit_bytes=32 * 1024 * 1024),
        cost_estimate=COST,
    )(place, at, *parts)


def unpack_attention_kernel(
    at_ref, p0, p1, p2, p3, wq_o, wk_o, wv_o, wo_o, small_o, wide
):
    for r, part in enumerate((p0, p1, p2, p3)):
        for n in range(4):
            wide[spot(piece_at(at_ref, r, n), PROWS), :] = part[n]
    wq_o[...] = wide[:, 0:D].astype(F32)
    wk_o[...] = wide[:, D : D + KVW].astype(F32)
    wv_o[...] = wide[:, D + KVW : QKVW].astype(F32)
    for g in range(4):
        wo_o[block(g, QUART), :] = wide[:, QKVW + g * QUART : QKVW + (g + 1) * QUART].astype(F32)
    small_o[...] = wide[:, QKVW + D :].astype(F32)


unpack_attention = whole_call(
    unpack_attention_kernel,
    "unpack_attention",
    [
        shaped((QUART, D), F32),
        shaped((QUART, KVW), F32),
        shaped((QUART, KVW), F32),
        shaped((D, QUART), F32),
        shaped((QUART, 128), F32),
    ],
    scratch=[pltpu.VMEM((QUART, ATTW), BF16)],
)


def body(
    prompt_x, cont_x, prompt_cot, cont_cot, prompt_routes, cont_routes,
    attn_gain, w_query, w_key, w_value, query_gain, key_gain,
    w_out, ffn_gain, w_router, w_gate, w_up, w_down,
):
    def moved(value, axes, change):
        sizes = [lax.axis_size(a) for a in axes]
        pairs = []
        count = 1
        for size in sizes:
            count *= size
        for index in range(count):
            rest, coords = index, []
            for size in reversed(sizes):
                coords.append(rest % size)
                rest //= size
            to = change(*reversed(coords))
            target = 0
            for size, coord in zip(sizes, to):
                target = target * size + coord
            pairs.append((index, target))
        return lax.ppermute(value, axes, pairs)

    def sib(value):
        return moved(value, ("c",), lambda c: (1 - c,))

    def far(value):
        return moved(value, ("xh",), lambda h: (1 - h,))

    def far_sib(value):
        return moved(value, ("xh", "c"), lambda h, c: (1 - h, 1 - c))

    def cross(value):
        return moved(value, ("xl", "xh"), lambda low, high: (1 - low, 1 - high))

    def cross_sib(value):
        return moved(value, ("xl", "xh", "c"), lambda low, high, c: (1 - low, 1 - high, 1 - c))

    def near(value):
        return moved(value, ("xl",), lambda low: (1 - low,))

    def along(value, by, core_of_z):
        def change(at_z, at_y, c):
            if c == core_of_z:
                return ((at_z + by) % 4, at_y, c)
            return (at_z, (at_y + by) % 4, c)

        return moved(value, ("z", "y", "c"), change)

    def first(value, by):
        return along(value, by, 1)

    def second(value, by):
        return along(value, by, 0)

    def spread(value, way):
        return [value] + [way(value, by) for by in (1, 2, 3)]

    def added(parts):
        total = parts[0].astype(F32)
        for part in parts[1:]:
            total = total + part.astype(F32)
        return total.astype(BF16)

    after = lax.optimization_barrier

    z = lax.axis_index("z").astype(jnp.int32)
    y = lax.axis_index("y").astype(jnp.int32)
    core = lax.axis_index("c").astype(jnp.int32)
    low_core = core == 0
    at = jnp.stack(
        [
            jnp.where(low_core, y, z),
            jnp.where(low_core, z, y),
            jnp.where(low_core, 1, 4),
            jnp.where(low_core, 4, 1),
        ]
    )
    position = lax.axis_index(("xh", "c")).astype(jnp.int32)
    place = position[None]
    piece = 4 * z + y
    cont_in = cont_x.reshape(HALF, D)
    cont_up = cont_cot.reshape(HALF, D)

    share_two, share_three = share_experts(jnp.stack([piece, position]), w_gate, w_up, w_down)
    place_in, share_two, share_three = after((place, share_two, share_three))
    share_two = cross(share_two)
    share_three = cross_sib(share_three)
    own_keys = prepare(
        place_in, w_key, w_value, attn_gain[None], ffn_gain[None], query_gain[None],
        key_gain[None], w_router,
    )
    w_query, own_keys, share_two, share_three = after((w_query, own_keys, share_two, share_three))
    keys_two = cross(own_keys)
    own_query = w_query.astype(BF16)
    query_two = cross(own_query)
    row = jnp.stack(spread(jnp.stack([share_two, share_three]), second))
    keys_two_in, row = after((keys_two, row))
    key_parts = (own_keys, sib(own_keys), keys_two_in, sib(keys_two_in))
    own_out = w_out.astype(BF16)
    out_two = cross(own_out)
    upstream = jnp.concatenate([prompt_cot, cont_up], axis=0)
    up_two = cross(upstream)

    cosine, sine = (jnp.asarray(table) for table in angle_tables())

    kv, kv_own, nk, inv, xr, ar, gain, rt = project_keys(
        place, prompt_x, cont_in, *key_parts, cosine, sine
    )
    nk, row, place_in = after((nk, row, place))
    packed = pack_experts(place_in, w_gate, w_up, w_down)
    row_one = first(row, 1)
    row_three = first(row, 3)
    kv_two = far(kv_own)
    gain, query_two = after((gain, query_two))
    query_parts = (own_query, sib(own_query), query_two, sib(query_two))
    q, nq, inv_q = project_query(place, ar, gain, *query_parts, cosine, sine)
    kv_parts = (kv, sib(kv_own), kv_two, sib(kv_two))
    q, packed = after((q, packed))
    mixed, lse = attend(place, q, *kv_parts)
    mixed, out_two, row, row_one, row_three = after((mixed, out_two, row, row_one, row_three))
    far_parts = (row, row_one, first(row, 2), row_three)
    out_parts = (own_out, sib(own_out), out_two, sib(out_two))
    hidden, b, gates = route(
        place, mixed, *out_parts, xr, gain, rt, prompt_routes, cont_routes.reshape(HALF, 8)
    )
    b, up_two = after((b, up_two))
    b_two = cross(b)
    w_parts = (packed[0], sib(packed[1]), *far_parts)
    b_parts = (b, sib(b), b_two, sib(b_two))
    up_parts = (upstream, sib(upstream), up_two, sib(up_two))
    dudw, gz, db_keep, db_send = experts(place, at, b_parts, up_parts, w_parts)

    db_come = sib(db_send)
    db_sum = added([db_keep, db_come])
    db_sum, dudw = after((db_sum, dudw))
    db_far = cross(db_sum[1])
    grads = expert_grads(place, at, b_parts, up_parts, dudw, gz)
    grads, db_far, later = after((grads, db_far, place))
    grad_one = first(grads[1], 1)
    grad_three = first(grads[3], 3)

    hgrad, small, dwo_keep, dwo_send, dq, kv_keep, kv_send, dk, dv = attend_back(
        later, db_sum[0], db_far, hidden, b, gates, prompt_cot, cont_up, gain, rt, mixed, lse,
        q, *kv_parts, *out_parts,
    )

    kv_send, grad_one, grad_three, grad_next = after((kv_send, grad_one, grad_three, grads[2]))
    grad_two = first(grad_next, 2)
    kv_come = sib(kv_send)
    kv_sum = added([kv_keep, kv_come])
    kv_far = far(kv_sum[1])
    dwq_keep, dwq_send, da_q, qg = query_back(
        place, dq, nq, inv_q, gain, cosine, sine, ar, *query_parts
    )
    last_keep, last_send, prompt_grad, cont_grad = key_back(
        place, kv_sum[0], kv_far, dk, dv, nk, inv, gain, cosine, sine, ar, xr, hgrad, da_q, qg,
        small, *key_parts,
    )

    grad_rest = fold(at, [grads[0], grad_one, grad_two, grad_three], 4 * EXPERTS * PROWS, 4)
    summed = added([grad_rest[0]] + [second(grad_rest[by], by) for by in (1, 2, 3)])
    paired = pair(
        at, dwq_keep, sib(dwq_send), last_keep, sib(last_send), dwo_keep, sib(dwo_send)
    )
    paired = fold(at, [paired[0]] + [first(paired[by], by) for by in (1, 2, 3)], 2 * PROWS, 1)
    part = added([paired[0]] + [second(paired[by], by) for by in (1, 2, 3)])

    turned_parts = jnp.stack(
        [summed[0], sib(summed[1]), far(summed[2]), far_sib(summed[3])], axis=0
    )
    own_sum = added([turned_parts, near(turned_parts)])
    full_experts = spread(jnp.stack(spread(own_sum, second)), first)
    gate_grad, up_grad, down_grad = unpack_experts(place, at, full_experts)

    part = added([part[0], far(part[1])])
    part = added([part, near(part)])
    full = spread(jnp.stack(spread(part, second)), first)
    wq_grad, wk_grad, wv_grad, wo_grad, tail = unpack_attention(at, *full)

    gz, own_sum = after((gz, own_sum))
    mix_keep, mix_send = mixture(at, gz, w_parts)
    mix_come = sib(mix_send)
    mix_sum = added([mix_keep, mix_come])
    mix_far = cross(mix_sum[1])
    prompt_out, cont_out = finish(place, hidden, mix_sum[0], mix_far)

    return (
        prompt_out,
        cont_out.reshape(1, HALF, D),
        prompt_grad,
        cont_grad.reshape(1, HALF, D),
        tail[:, 0],
        wq_grad,
        wk_grad,
        wv_grad,
        tail[:, 2],
        tail[0:HALF, 3],
        wo_grad,
        tail[:, 1],
        tail[:, 16 : 16 + EXPERTS],
        gate_grad,
        up_grad,
        down_grad,
    )


def solution(mesh):
    fine = Mesh(mesh.devices.reshape(2, 4, 4, 2, 2), AXES)
    shard = ("xh", "c")
    tokens = P(AXES, None)
    series = P(AXES, None, None)
    weights = (
        P(shard),
        P(shard, None),
        P(shard, None),
        P(shard, None),
        P(shard),
        P(shard),
        P(None, shard),
        P(shard),
        P(shard, None),
        P(None, shard, None),
        P(None, shard, None),
        P(None, None, shard),
    )
    return jax.shard_map(
        body,
        mesh=fine,
        in_specs=(tokens, series, tokens, series, tokens, series, *weights),
        out_specs=(tokens, series, tokens, series, *weights),
        check_vma=False,
    )
```

```python
import jax
import jax.numpy as jnp
import numpy as np
from jax import lax
from jax.experimental import pallas as pl
from jax.experimental.pallas import tpu as pltpu
from jax.sharding import Mesh, PartitionSpec as P

EPSILON = 1e-06
SCORE_SCALE = 0.25
RESIDUAL_SCALE = 0.22
ROTARY_BASE = 10000.0
MASKED = -1e30

D = 1024
HDIM = 64
PAIRS = 4
KVW = 512
QKVW = 2048
ROWS = 256
HALF = 128
QUART = 256
EXPERTS = 9
FSLICE = 128
TILE = 3 * FSLICE
TOKENS = 4 * ROWS
KEYS = 5 * HALF
BOUT = D + 128
ATTW = QKVW + D + 128
PIECES = 16
PROWS = QUART // PIECES
SHAREW = 12 * TILE
GROUP = 3
OUT_AT = EXPERTS * TILE

F32 = jnp.float32
BF16 = jnp.bfloat16


def angle_tables():
    frequency = np.float32(ROTARY_BASE) ** (-np.arange(0, HDIM, 2, dtype=np.float32) / HDIM)
    turned = np.arange(KEYS, dtype=np.float32)[:, None] * frequency.astype(np.float32)[None, :]
    cosine = np.tile(np.cos(turned), (1, 4)).astype(np.float32)
    sine = np.sin(turned)
    sine = np.concatenate([-sine, sine, -sine, sine], axis=1).astype(np.float32)
    return cosine, sine


AXES = ("xl", "z", "y", "xh", "c")


def nn(left, right):
    return lax.dot_general(left, right, (((1,), (0,)), ((), ())), preferred_element_type=F32)


def nt(left, right):
    return lax.dot_general(left, right, (((1,), (1,)), ((), ())), preferred_element_type=F32)


def tn(left, right):
    return lax.dot_general(left, right, (((0,), (0,)), ((), ())), preferred_element_type=F32)


def spot(index, width):
    return pl.ds(pl.multiple_of(index * width, width), width)


def block(index, width):
    return slice(index * width, (index + 1) * width)


SMEM = pl.BlockSpec(memory_space=pltpu.SMEM)
VMEM = pl.BlockSpec(memory_space=pltpu.VMEM)


COST = pl.CostEstimate(flops=1_000_000, bytes_accessed=1_000_000, transcendentals=0)


def whole_call(kernel, name, out_shape, scratch=(), limit=56):
    def call(*operands):
        return pl.pallas_call(
            kernel,
            name=name,
            out_shape=out_shape,
            in_specs=[SMEM] + [VMEM] * (len(operands) - 1),
            out_specs=jax.tree.map(lambda _: VMEM, out_shape),
            scratch_shapes=list(scratch),
            compiler_params=pltpu.CompilerParams(vmem_limit_bytes=limit * 1024 * 1024),
            cost_estimate=COST,
        )(*operands)

    return call


def shaped(shape, dtype):
    return jax.ShapeDtypeStruct(shape, dtype)


def pack_kernel(s_ref, gate, up, down, own, other):
    turned = down[0].T
    for k, out in ((0, own), (1, other)):
        low = (s_ref[0] % 2) == k
        for n, part in enumerate((gate[0], up[0], turned)):
            half = jnp.where(low, part[:, 0:FSLICE], part[:, FSLICE:])
            out[0, :, block(n, FSLICE)] = half.astype(BF16)


def pack_experts(place, w_gate, w_up, w_down):
    wide = pl.BlockSpec((1, QUART, 2 * FSLICE), lambda e, s: (e, 0, s[0] // 2))
    out = pl.BlockSpec((1, QUART, TILE), lambda e, s: (e, 0, 0))
    return pl.pallas_call(
        pack_kernel,
        name="pack_experts",
        grid_spec=pltpu.PrefetchScalarGridSpec(
            num_scalar_prefetch=1,
            grid=(EXPERTS,),
            in_specs=[
                wide,
                wide,
                pl.BlockSpec((1, 2 * FSLICE, QUART), lambda e, s: (e, s[0] // 2, 0)),
            ],
            out_specs=[out, out],
        ),
        out_shape=[shaped((EXPERTS, QUART, TILE), BF16)] * 2,
        compiler_params=pltpu.CompilerParams(vmem_limit_bytes=56 * 1024 * 1024),
        cost_estimate=COST,
    )(place, w_gate, w_up, w_down)


def share_kernel(at_ref, gate, up, down, out, two, three, turned):
    for k, dest in ((2, two), (3, three)):
        there = spot(at_ref[1] ^ k, FSLICE)
        for e in range(EXPERTS):
            at = e * TILE
            dest[:, at : at + FSLICE] = gate[e, :, there].astype(BF16)
            dest[:, at + FSLICE : at + 2 * FSLICE] = up[e, :, there].astype(BF16)
            turned[...] = down[e, there, :].T
            dest[:, at + 2 * FSLICE : at + TILE] = turned[
                spot(at_ref[0] % 8, PROWS), :
            ].astype(BF16)
        for g in range(4):
            at = OUT_AT + g * QUART
            dest[:, at : at + QUART] = out[spot(PIECES * g + at_ref[0], PROWS), :].astype(BF16)
        dest[:, OUT_AT + D :] = jnp.zeros((PROWS, SHAREW - OUT_AT - D), BF16)


def share_experts(at, w_gate, w_up, w_down, w_out):
    rows = pl.BlockSpec((EXPERTS, PROWS, 512), lambda i, at: (0, at[0], 0))
    dest = pl.BlockSpec((PROWS, SHAREW), lambda i, at: (0, 0))
    return pl.pallas_call(
        share_kernel,
        name="share_experts",
        grid_spec=pltpu.PrefetchScalarGridSpec(
            num_scalar_prefetch=1,
            grid=(1,),
            in_specs=[
                rows,
                rows,
                pl.BlockSpec((EXPERTS, 512, 128), lambda i, at: (0, 0, at[0] // 8)),
                pl.BlockSpec((D, QUART), lambda i, at: (0, 0)),
            ],
            out_specs=[dest, dest],
            scratch_shapes=[pltpu.VMEM((128, FSLICE), F32)],
        ),
        out_shape=[shaped((PROWS, SHAREW), BF16)] * 2,
        compiler_params=pltpu.CompilerParams(vmem_limit_bytes=56 * 1024 * 1024),
        cost_estimate=COST,
    )(at, w_gate, w_up, w_down, w_out)


def prepare_kernel(s_ref, wq, wk, wv, attn, ffn, query, key, router, kv_o, line):
    kv_o[QUART + 32 :, :] = wq[...].astype(BF16)
    kv_o[0:QUART, 0:KVW] = wk[...].astype(BF16)
    kv_o[0:QUART, KVW:D] = wv[...].astype(BF16)
    line[...] = jnp.zeros_like(line)
    line[0:1, 0:256] = attn[...]
    line[0:1, 256:512] = ffn[...]
    line[0:1, 512:768] = query[...]
    line[0:1, 768:896] = key[...]
    kv_o[QUART : QUART + 16, :] = line[...].astype(BF16)
    line[...] = jnp.zeros_like(line)
    line[0:EXPERTS, 0:QUART] = router[...]
    kv_o[QUART + 16 : QUART + 32, :] = line[...].astype(BF16)


prepare = whole_call(
    prepare_kernel,
    "prepare",
    shaped((2 * QUART + 32, D), BF16),
    scratch=[pltpu.VMEM((16, D), F32)],
)


def swapped(values):
    lane = lax.broadcasted_iota(jnp.int32, values.shape, 1)
    return jnp.where(
        lane % HDIM < HDIM // 2, pltpu.roll(values, 96, axis=1), pltpu.roll(values, 32, axis=1)
    )


def here(place, table):
    return jnp.concatenate([table[spot(place, HALF), :], table[4 * HALF :, :]], axis=0)


def project_keys_kernel(
    s_ref, xp, xc, a0, a1, a2, a3, cos, sin, kv_o, kvp_o, nk_o, inv_o, xr_o, ar_o, gain_o, rt_o, acc
):
    parts = (a0, a1, a2, a3)
    for k in range(4):
        there = s_ref[0] ^ k
        xr_o[0:HALF, block(k, QUART)] = xp[:, spot(there, QUART)]
        xr_o[HALF:ROWS, block(k, QUART)] = xc[:, spot(there, QUART)]
        small = parts[k][QUART : QUART + 16, :].astype(F32)[0:1]
        gain_o[0:1, block(k, QUART)] = small[:, 0:256]
        gain_o[0:1, slice(D + k * QUART, D + (k + 1) * QUART)] = small[:, 256:512]
        gain_o[0:1, pl.ds(pl.multiple_of(2 * D + there * QUART, 128), QUART)] = small[:, 512:768]
        gain_o[0:1, pl.ds(pl.multiple_of(3 * D + there * HALF, 128), HALF)] = small[:, 768:896]
        rt_o[:, block(k, QUART)] = parts[k][QUART + 16 : QUART + 32, 0:QUART]
    x = xr_o[...].astype(F32)
    inverse = lax.rsqrt(jnp.mean(x * x, axis=1, keepdims=True) + EPSILON)
    ar_o[...] = (x * inverse * gain_o[0:1, 0:D]).astype(BF16)
    total = nn(ar_o[:, block(0, QUART)], parts[0][0:QUART, :])
    for k in range(1, 4):
        total = total + nn(ar_o[:, block(k, QUART)], parts[k][0:QUART, :])
    acc[...] = total
    kp = acc[:, 0:KVW]
    inv_k = lax.rsqrt(jnp.mean(kp * kp, axis=1, keepdims=True) + EPSILON)
    nk_o[...] = kp * inv_k
    lane = lax.broadcasted_iota(jnp.int32, (ROWS, 128), 1)
    inv_o[...] = jnp.where(lane == 1, inv_k, inverse)
    kv_o[:, KVW:D] = acc[:, KVW:D].astype(BF16)
    cosine = here(s_ref[0], cos)
    sine = here(s_ref[0], sin)
    for g in range(4):
        at = block(g, 128)
        u = nk_o[:, at] * gain_o[0:1, 3 * D + g * 128 : 3 * D + (g + 1) * 128]
        kv_o[:, at] = (u * cosine + swapped(u) * sine).astype(BF16)
    kvp_o[...] = kv_o[0:HALF, :]


project_keys = whole_call(
    project_keys_kernel,
    "project_keys",
    [
        shaped((ROWS, D), BF16),
        shaped((HALF, D), BF16),
        shaped((ROWS, KVW), F32),
        shaped((ROWS, 128), F32),
        shaped((ROWS, D), BF16),
        shaped((ROWS, D), BF16),
        shaped((8, 3 * D + KVW), F32),
        shaped((16, D), BF16),
    ],
    scratch=[pltpu.VMEM((ROWS, D), F32)],
)


def prepare_out_kernel(s_ref, wo, out):
    for g in range(4):
        out[:, block(g, QUART)] = wo[block(g, QUART), :].astype(BF16)


prepare_out = whole_call(prepare_out_kernel, "prepare_out", shaped((QUART, D), BF16))


def project_query_kernel(s_ref, ar, gain, a0, a1, a2, a3, cos, sin, q_o, nq_o, inv_o):
    total = nn(ar[:, block(0, QUART)], a0[QUART + 32 :, :])
    for k, part in ((1, a1), (2, a2), (3, a3)):
        total = total + nn(ar[:, block(k, QUART)], part[QUART + 32 :, :])
    nq_o[...] = total
    inv_q = lax.rsqrt(jnp.mean(total * total, axis=1, keepdims=True) + EPSILON)
    inv_o[...] = jnp.broadcast_to(inv_q, (ROWS, 128))
    cosine = here(s_ref[0], cos)
    sine = here(s_ref[0], sin)
    for g in range(8):
        at = block(g, 128)
        near = nq_o[:, at] * inv_q
        nq_o[:, at] = near
        u = near * gain[0:1, 2 * D + g * 128 : 2 * D + (g + 1) * 128]
        q_o[:, at] = (u * cosine + swapped(u) * sine).astype(BF16)


project_query = whole_call(
    project_query_kernel,
    "project_query",
    [shaped((ROWS, D), BF16), shaped((ROWS, D), F32), shaped((ROWS, 128), F32)],
)


def fill_bias(place, bias):
    row = lax.broadcasted_iota(jnp.int32, (HALF, 512), 0)
    lane = lax.broadcasted_iota(jnp.int32, (HALF, 512), 1)
    causal = jnp.where(row <= lane % HALF, 0.0, MASKED)
    is_prompt = lane % ROWS < HALF
    bias[0:HALF, :] = jnp.where(is_prompt, causal, 0.0)
    for k in range(1, 4):
        level = jnp.where((place ^ k) < place, 0.0, MASKED)
        bias[block(k, HALF), :] = jnp.where(is_prompt, level, 0.0)
    bias[4 * HALF :, :] = jnp.where(is_prompt, MASKED, causal)


def fill_keys(refs, keys, values):
    for j in range(4):
        keys[block(j, HALF), :] = refs[j][0:HALF, 0:KVW]
        values[block(j, HALF), :] = refs[j][0:HALF, KVW:D]
    keys[4 * HALF :, :] = refs[0][HALF:ROWS, 0:KVW]
    values[4 * HALF :, :] = refs[0][HALF:ROWS, KVW:D]


def doubled(ref, pair, odd):
    both = ref[:, spot(pair, 128)]
    other = pltpu.roll(both.astype(F32), HDIM, axis=1).astype(BF16)
    lane = lax.broadcasted_iota(jnp.int32, both.shape, 1)
    return jnp.where((lane < HDIM) == (odd == 0), both, other)


def stacked(ref, head, scale):
    rows = ref[:, spot(head, 128)]
    lane = lax.broadcasted_iota(jnp.int32, rows.shape, 1)
    rows = rows * jnp.asarray(scale, rows.dtype)
    none = jnp.zeros_like(rows)
    return jnp.concatenate(
        [jnp.where(lane < HDIM, rows, none), jnp.where(lane < HDIM, none, rows)], axis=0
    )


def attend_kernel(s_ref, q, kv0, kv1, kv2, kv3, mixed_o, lse_o, bias, keys, values):
    fill_bias(s_ref[0], bias)
    fill_keys((kv0, kv1, kv2, kv3), keys, values)

    def one_pair(pair, carry):
        for odd in range(2):
            head = 2 * pair + odd
            kk = doubled(keys, pair, odd)
            vv = doubled(values, pair, odd)
            scores = nt(kk, stacked(q, head, SCORE_SCALE)) + bias[...]
            highest = jnp.max(scores, axis=0, keepdims=True)
            raised = jnp.exp(scores - highest)
            totals = jnp.sum(raised, axis=0, keepdims=True)
            probs = (raised * (1.0 / totals)).astype(BF16)
            lse_o[pl.ds(head, 1), :] = highest + jnp.log(totals)
            out = tn(vv, probs).T
            lane = lax.broadcasted_iota(jnp.int32, (ROWS, 128), 1)
            mixed_o[:, spot(head, 128)] = jnp.where(
                lane < HDIM, out[0:ROWS], out[ROWS : 2 * ROWS]
            ).astype(BF16)
        return carry

    lax.fori_loop(0, PAIRS, one_pair, 0)


attend = whole_call(
    attend_kernel,
    "attend",
    [shaped((ROWS, D), BF16), shaped((8, 512), F32)],
    scratch=[
        pltpu.VMEM((KEYS, 512), F32),
        pltpu.VMEM((KEYS, KVW), BF16),
        pltpu.VMEM((KEYS, KVW), BF16),
    ],
)


def route_kernel(
    s_ref, at_ref, mixed_ref, o0, o1, f0, f1, f2, f3, xr, gain, rt, rp, rc, hid_o, b_o, gates_o, out_o
):
    for r, part in enumerate((f0, f1, f2, f3)):
        for n in range(4):
            rows = spot(piece_at(at_ref, r, n), PROWS)
            for k in range(2):
                out_o[k, rows, :] = part[n, k, :, 0:D]
    for k in range(4):
        part = (o0, o1, out_o.at[0], out_o.at[1])[k]
        total = nn(mixed_ref[:, block(0, QUART)], part[:, block(0, QUART)])
        for g in range(1, 4):
            total = total + nn(mixed_ref[:, block(g, QUART)], part[:, block(g, QUART)])
        hid_o[:, block(k, QUART)] = xr[:, block(k, QUART)].astype(F32) + RESIDUAL_SCALE * total
    hidden = hid_o[...]
    inverse = lax.rsqrt(jnp.mean(hidden * hidden, axis=1, keepdims=True) + EPSILON)
    b_o[:, 0:D] = (hidden * inverse * gain[0:1, D : 2 * D]).astype(BF16)
    logits = nt(b_o[:, 0:D], rt[...])
    expert = lax.broadcasted_iota(jnp.int32, (HALF, 16), 1)
    for half, routes in enumerate((rp, rc)):
        chosen = routes[:, 0:1] == expert
        for r in range(1, 8):
            chosen = chosen | (routes[:, r : r + 1] == expert)
        level = jnp.where(chosen, logits[block(half, HALF)], MASKED)
        raised = jnp.exp(level - jnp.max(level, axis=1, keepdims=True))
        gates = raised / jnp.sum(raised, axis=1, keepdims=True)
        gates_o[block(half, HALF), 0:16] = gates
        high = gates.astype(BF16).astype(F32)
        b_o[block(half, HALF), D:BOUT] = jnp.concatenate(
            [high, gates - high, jnp.zeros((HALF, 96), F32)], axis=1
        ).astype(BF16)


def route(place, at, mixed, own, other, far_parts, *rest):
    whole = lambda *shape: pl.BlockSpec(shape, lambda i: (0,) * len(shape))
    tail = pl.BlockSpec((4, 2, PROWS, SHAREW // 4), lambda i: (0, 0, 0, 3))
    return pl.pallas_call(
        route_kernel,
        name="route",
        grid=(1,),
        in_specs=[SMEM, SMEM, whole(ROWS, D), whole(QUART, D), whole(QUART, D)]
        + [tail] * 4
        + [whole(*part.shape) for part in rest],
        out_specs=[whole(ROWS, D), whole(ROWS, BOUT), whole(ROWS, 128), whole(2, QUART, D)],
        out_shape=[
            shaped((ROWS, D), F32),
            shaped((ROWS, BOUT), BF16),
            shaped((ROWS, 128), F32),
            shaped((2, QUART, D), BF16),
        ],
        compiler_params=pltpu.CompilerParams(vmem_limit_bytes=56 * 1024 * 1024),
        cost_estimate=COST,
    )(place, at, mixed, own, other, *far_parts, *rest)


def piece_at(at, r, n):
    return ((at[0] + 4 - r) % 4) * at[2] + ((at[1] + 4 - n) % 4) * at[3]


def piece_at(at, r, n):
    return ((at[0] + 4 - r) % 4) * at[2] + ((at[1] + 4 - n) % 4) * at[3]


def fill_weights(at, own, other, far_parts, dest, lanes):
    dest[block(0, QUART), lanes] = own
    dest[block(1, QUART), lanes] = other
    for r in range(4):
        for n in range(4):
            piece = piece_at(at, r, n)
            for k in range(2):
                dest[spot((2 + k) * PIECES + piece, PROWS), lanes] = far_parts[r][n, k]


def expert_kernel(
    s_ref, at_ref, b0, b1, b2, b3, g0, g1, g2, g3, w0, w1, f0, f1, f2, f3,
    dudw_o, gz_o, dbk_o, dbs_o, xs, gs, gates, dgs, wgu, wd, dudw
):
    step = pl.program_id(0)
    place = s_ref[0]

    @pl.when(step == 0)
    def _():
        for j, (b_ref, g_ref) in enumerate(zip((b0, b1, b2, b3), (g0, g1, g2, g3))):
            rows = block(j, ROWS)
            for k in range(4):
                xs[rows, block(k, QUART)] = b_ref[:, block(k ^ j, QUART)]
                gs[rows, block(k, QUART)] = g_ref[:, spot(place ^ k, QUART)]
            both = b_ref[:, D:BOUT].astype(F32)
            gates[rows, :] = both + pltpu.roll(both, 112, axis=1)
        dgs[...] = jnp.zeros_like(dgs)

    here_gu = spot(step, 2 * GROUP * FSLICE)
    for n in range(GROUP):
        up = slice(n * TILE, n * TILE + 2 * FSLICE)
        down = slice(n * TILE + 2 * FSLICE, (n + 1) * TILE)
        for k, part in enumerate((w0, w1)):
            wgu[step, block(k, QUART), block(n, 2 * FSLICE)] = part[n, :, 0 : 2 * FSLICE]
            wd[block(k, QUART), block(n, FSLICE)] = part[n, :, 2 * FSLICE :]
        for r, part in enumerate((f0, f1, f2, f3)):
            for m in range(4):
                for k in range(2):
                    rows = spot((2 + k) * PIECES + piece_at(at_ref, r, m), PROWS)
                    wgu[step, rows, block(n, 2 * FSLICE)] = part[m, k, :, up]
                    wd[rows, block(n, FSLICE)] = part[m, k, :, down]
    both = nn(xs[...], wgu[step])
    h_all = RESIDUAL_SCALE * nn(gs[...], wd[...])
    lane = lax.broadcasted_iota(jnp.int32, (TOKENS, 128), 1)
    added = jnp.zeros((TOKENS, 128), F32)
    for n in range(GROUP):
        e = step * GROUP + n
        u = both[:, 2 * n * FSLICE : (2 * n + 1) * FSLICE]
        w = both[:, (2 * n + 1) * FSLICE : (2 * n + 2) * FSLICE]
        h = h_all[:, block(n, FSLICE)]
        gate = jnp.sum(jnp.where(lane == e, gates[...], 0.0), axis=1, keepdims=True)
        sig = jax.nn.sigmoid(u)
        silu = u * sig
        z = (silu * w).astype(BF16).astype(F32)
        gz_o[:, block(n, FSLICE)] = (gate * z).astype(BF16)
        added = added + jnp.where(lane == e, jnp.sum(z * h, axis=1, keepdims=True), 0.0)
        dz = gate * h
        du = (dz * w * sig * (1.0 + u * (1.0 - sig))).astype(BF16)
        dw = (dz * silu).astype(BF16)
        dudw_o[:, block(2 * n, FSLICE)] = du
        dudw_o[:, block(2 * n + 1, FSLICE)] = dw
    dgs[...] += added
    dudw[:, here_gu] = dudw_o[...]

    @pl.when(step == EXPERTS // GROUP - 1)
    def _():
        width = 2 * GROUP * FSLICE
        whole = nt(dudw[:, 0:width], wgu[0])
        for n in range(1, EXPERTS // GROUP):
            whole = whole + nt(dudw[:, block(n, width)], wgu[n])
        whole = whole.astype(BF16)
        for j in range(4):
            out = (dbk_o, dbs_o)[j % 2]
            rows = block(j, ROWS)
            for k in range(4):
                out[j // 2, :, block(k ^ j, QUART)] = whole[rows, block(k, QUART)]
            dg = dgs[rows, 0:16]
            high = dg.astype(BF16).astype(F32)
            out[j // 2, :, D:BOUT] = jnp.concatenate(
                [high, dg - high, jnp.zeros((ROWS, 96), F32)], axis=1
            ).astype(BF16)


def fixed(rank):
    return lambda e: (0,) * rank


def experts(place, at, b_parts, g_parts, w_parts):
    return pl.pallas_call(
        expert_kernel,
        name="experts",
        grid=(EXPERTS // GROUP,),
        in_specs=[SMEM] * 2
        + [pl.BlockSpec((ROWS, BOUT), fixed(2))] * 4
        + [pl.BlockSpec((ROWS, D), fixed(2))] * 4
        + [pl.BlockSpec((GROUP, QUART, TILE), lambda e: (e, 0, 0))] * 2
        + [pl.BlockSpec((4, 2, PROWS, GROUP * TILE), lambda e: (0, 0, 0, e))] * 4,
        out_specs=[
            pl.BlockSpec((TOKENS, 2 * GROUP * FSLICE), lambda e: (0, e)),
            pl.BlockSpec((TOKENS, GROUP * FSLICE), lambda e: (0, e)),
            pl.BlockSpec((2, ROWS, BOUT), fixed(3)),
            pl.BlockSpec((2, ROWS, BOUT), fixed(3)),
        ],
        out_shape=[
            shaped((TOKENS, EXPERTS * 2 * FSLICE), BF16),
            shaped((TOKENS, EXPERTS * FSLICE), BF16),
            shaped((2, ROWS, BOUT), BF16),
            shaped((2, ROWS, BOUT), BF16),
        ],
        scratch_shapes=[
            pltpu.VMEM((TOKENS, D), BF16),
            pltpu.VMEM((TOKENS, D), BF16),
            pltpu.VMEM((TOKENS, 128), F32),
            pltpu.VMEM((TOKENS, 128), F32),
            pltpu.VMEM((EXPERTS // GROUP, D, 2 * GROUP * FSLICE), BF16),
            pltpu.VMEM((D, GROUP * FSLICE), BF16),
            pltpu.VMEM((TOKENS, EXPERTS * 2 * FSLICE), BF16),
        ],
        compiler_params=pltpu.CompilerParams(vmem_limit_bytes=58 * 1024 * 1024),
        cost_estimate=COST,
    )(place, at, *b_parts, *g_parts, *w_parts)


def piece_to(at, r, v):
    return ((at[0] + r) % 4) * at[2] + v * at[3]


def expert_grad_kernel(
    s_ref, at_ref, b0, b1, b2, b3, g0, g1, g2, g3, dudw, gz, t0, t1, t2, t3, xt, gt, tile
):
    @pl.when(pl.program_id(0) == 0)
    def _():
        for j, (b_ref, g_ref) in enumerate(zip((b0, b1, b2, b3), (g0, g1, g2, g3))):
            for k in range(4):
                xt[block(k, QUART), block(j, ROWS)] = b_ref[:, block(k ^ j, QUART)].T
                gt[block(k, QUART), block(j, ROWS)] = g_ref[:, spot(s_ref[0] ^ k, QUART)].T

    for k in range(4):
        rows = block(k, QUART)
        first = nn(xt[rows, :], dudw[...]).astype(BF16)
        second = (RESIDUAL_SCALE * nn(gt[rows, :], gz[...])).astype(BF16)
        for n in range(GROUP):
            tile[:, 0 : 2 * FSLICE] = first[:, block(n, 2 * FSLICE)]
            tile[:, 2 * FSLICE :] = second[:, block(n, FSLICE)]
            for r, out in enumerate((t0, t1, t2, t3)):
                for v in range(4):
                    out[v, k, n] = tile[spot(piece_to(at_ref, r, v), PROWS), :]


def expert_grads(place, at, b_parts, g_parts, dudw, gz):
    return pl.pallas_call(
        expert_grad_kernel,
        name="expert_grads",
        grid=(EXPERTS // GROUP,),
        in_specs=[SMEM] * 2
        + [pl.BlockSpec((ROWS, BOUT), fixed(2))] * 4
        + [pl.BlockSpec((ROWS, D), fixed(2))] * 4
        + [
            pl.BlockSpec((TOKENS, 2 * GROUP * FSLICE), lambda e: (0, e)),
            pl.BlockSpec((TOKENS, GROUP * FSLICE), lambda e: (0, e)),
        ],
        out_specs=[pl.BlockSpec((4, 4, GROUP, PROWS, TILE), lambda e: (0, 0, e, 0, 0))] * 4,
        out_shape=[shaped((4, 4, EXPERTS, PROWS, TILE), BF16)] * 4,
        scratch_shapes=[
            pltpu.VMEM((D, TOKENS), BF16),
            pltpu.VMEM((D, TOKENS), BF16),
            pltpu.VMEM((QUART, TILE), BF16),
        ],
        compiler_params=pltpu.CompilerParams(vmem_limit_bytes=56 * 1024 * 1024),
        cost_estimate=COST,
    )(place, at, *b_parts, *g_parts, dudw, gz)


def mixture_kernel(at_ref, gz, w0, w1, f0, f1, f2, f3, keep_o, send_o, wide):
    for e in range(EXPERTS):
        at = slice(e * TILE + 2 * FSLICE, (e + 1) * TILE)
        parts = [part.at[:, :, :, at] for part in (f0, f1, f2, f3)]
        fill_weights(at_ref, w0[e], w1[e], parts, wide, block(e, FSLICE))
    for j in range(4):
        out = (keep_o, send_o)[j % 2]
        total = nt(gz[block(j, ROWS), :], wide[...]).astype(BF16)
        for k in range(4):
            out[j // 2, :, block(k ^ j, QUART)] = total[:, block(k, QUART)]


def mixture(at, gz, w_parts):
    down = [pl.BlockSpec((EXPERTS, QUART, FSLICE), lambda i: (0, 0, 2))] * 2 + [
        pl.BlockSpec((4, 2, PROWS, OUT_AT), lambda i: (0, 0, 0, 0))
    ] * 4
    return pl.pallas_call(
        mixture_kernel,
        name="mixture",
        grid=(1,),
        in_specs=[SMEM, pl.BlockSpec((TOKENS, EXPERTS * FSLICE), fixed(2))] + down,
        out_specs=[pl.BlockSpec((2, ROWS, D), fixed(3))] * 2,
        out_shape=[shaped((2, ROWS, D), BF16)] * 2,
        scratch_shapes=[pltpu.VMEM((D, EXPERTS * FSLICE), BF16)],
        compiler_params=pltpu.CompilerParams(vmem_limit_bytes=56 * 1024 * 1024),
        cost_estimate=COST,
    )(at, gz, *w_parts)


def attend_back_kernel(
    s_ref, db_keep, db_come, hid, b, gates_ref, gp, gc, gain, rt, mixed, lse,
    q, kv0, kv1, kv2, kv3, o0, o1, of,
    hgrad_o, small_o, dwok_o, dwos_o, dq_o, kvk_o, kvs_o, dk_o, dv_o,
    bias, keys, values, dmix, grow
):
    place = s_ref[0]
    parts = (o0, o1, of.at[0], of.at[1])
    fill_bias(place, bias)
    fill_keys((kv0, kv1, kv2, kv3), keys, values)
    total = db_keep[...].astype(F32) + db_come[...].astype(F32)
    tail = total[:, D:BOUT]
    dgate = (tail + pltpu.roll(tail, 112, axis=1))[:, 0:16]
    gates = gates_ref[:, 0:16]
    dlog = (gates * (dgate - jnp.sum(gates * dgate, axis=1, keepdims=True))).astype(BF16)
    dbt = total[:, 0:D] + nn(dlog, rt[...])
    small_o[...] = jnp.zeros_like(small_o)
    small_o[16:32, :] = tn(dlog, b[:, 0:D])
    hidden = hid[...]
    inverse = lax.rsqrt(jnp.mean(hidden * hidden, axis=1, keepdims=True) + EPSILON)
    n2 = hidden * inverse
    small_o[1:2, :] = jnp.sum(dbt * n2, axis=0, keepdims=True)
    scaled = dbt * gain[0:1, D : 2 * D]
    for k in range(4):
        there = spot(place ^ k, QUART)
        grow[0:HALF, block(k, QUART)] = gp[:, there]
        grow[HALF:ROWS, block(k, QUART)] = gc[:, there]
    hgrad = grow[...].astype(F32) + inverse * (
        scaled - n2 * jnp.mean(scaled * n2, axis=1, keepdims=True)
    )
    hgrad_o[...] = hgrad
    agrad = (RESIDUAL_SCALE * hgrad).astype(BF16)
    for g in range(4):
        total = nt(agrad[:, block(0, QUART)], parts[0][:, block(g, QUART)])
        for k in range(1, 4):
            total = total + nt(agrad[:, block(k, QUART)], parts[k][:, block(g, QUART)])
        dmix[:, block(g, QUART)] = total.astype(BF16)
    for g in range(4):
        rows = tn(mixed[:, block(g, QUART)], agrad).astype(BF16)
        for k in range(4):
            out = (dwok_o, dwos_o)[k % 2]
            out[k // 2, :, block(g, QUART)] = rows[:, block(k, QUART)]

    def one_pair(pair, carry):
        dks = []
        dvs = []
        lane = lax.broadcasted_iota(jnp.int32, (ROWS, 128), 1)
        for odd in range(2):
            head = 2 * pair + odd
            kk = doubled(keys, pair, odd)
            vv = doubled(values, pair, odd)
            qs = stacked(q, head, SCORE_SCALE)
            ds_rows = stacked(dmix, head, 1.0)
            probs = jnp.exp(nt(kk, qs) + bias[...] - lse[pl.ds(head, 1), :])
            product = dmix[:, spot(head, 128)].astype(F32) * mixed[:, spot(head, 128)].astype(F32)
            product = product.T
            inner = jnp.concatenate(
                [
                    jnp.sum(product[0:HDIM], axis=0, keepdims=True),
                    jnp.sum(product[HDIM:], axis=0, keepdims=True),
                ],
                axis=1,
            )
            sgrad = (probs * (nt(vv, ds_rows) - inner)).astype(BF16)
            dkr = nn(sgrad, qs)
            dvr = nn(probs.astype(BF16), ds_rows)
            dks.append(dkr + pltpu.roll(dkr, HDIM, axis=1))
            dvs.append(dvr + pltpu.roll(dvr, HDIM, axis=1))
            dqt = (SCORE_SCALE * tn(kk, sgrad)).T
            dq_o[:, spot(head, 128)] = jnp.where(lane < HDIM, dqt[0:ROWS], dqt[ROWS : 2 * ROWS])
        low = lax.broadcasted_iota(jnp.int32, (KEYS, 128), 1) < HDIM
        dk = jnp.where(low, dks[0], dks[1])
        dv = jnp.where(low, dvs[0], dvs[1])
        at = spot(pair, 128)
        at_v = spot(pair + 4, 128)
        for j in range(4):
            side = (kvk_o, kvs_o)[j % 2]
            side[j // 2, :, at] = dk[block(j, HALF)].astype(BF16)
            side[j // 2, :, at_v] = dv[block(j, HALF)].astype(BF16)
        dk_o[:, at] = dk[4 * HALF :]
        dv_o[:, at] = dv[4 * HALF :]
        return carry

    lax.fori_loop(0, PAIRS, one_pair, 0)


attend_back = whole_call(
    attend_back_kernel,
    "attend_back",
    [
        shaped((ROWS, D), F32),
        shaped((32, D), F32),
        shaped((2, QUART, D), BF16),
        shaped((2, QUART, D), BF16),
        shaped((ROWS, D), F32),
        shaped((2, HALF, D), BF16),
        shaped((2, HALF, D), BF16),
        shaped((HALF, KVW), F32),
        shaped((HALF, KVW), F32),
    ],
    scratch=[
        pltpu.VMEM((KEYS, 512), F32),
        pltpu.VMEM((KEYS, KVW), BF16),
        pltpu.VMEM((KEYS, KVW), BF16),
        pltpu.VMEM((ROWS, D), BF16),
        pltpu.VMEM((ROWS, D), BF16),
    ],
)


def turn_back(values, cosine, sine):
    return values * cosine - swapped(values) * sine


def query_back_kernel(
    s_ref, dq, nq, inv, gain, cos, sin, ar, a0, a1, a2, a3, dwqk_o, dwqs_o, da_o, qg_o, grads
):
    cosine = here(s_ref[0], cos)
    sine = here(s_ref[0], sin)
    inv_q = inv[:, 0:1]
    dot = jnp.zeros((ROWS, 1), F32)
    for g in range(8):
        at = block(g, 128)
        back = turn_back(dq[:, at], cosine, sine)
        near = nq[:, at]
        qg_o[0:1, at] = jnp.sum(back * near, axis=0, keepdims=True)
        scaled = back * gain[0:1, 2 * D + g * 128 : 2 * D + (g + 1) * 128]
        dot = dot + jnp.sum(scaled * near, axis=1, keepdims=True)
        grads[:, at] = scaled
    pre = (inv_q * (grads[...] - nq[...] * (dot / D))).astype(BF16)
    for k, part in enumerate((a0, a1, a2, a3)):
        da_o[:, block(k, QUART)] = nt(pre, part[QUART + 32 :, :])
        out = (dwqk_o, dwqs_o)[k % 2]
        out[k // 2] = tn(ar[:, block(k, QUART)], pre).astype(BF16)


query_back = whole_call(
    query_back_kernel,
    "query_back",
    [
        shaped((2, QUART, D), BF16),
        shaped((2, QUART, D), BF16),
        shaped((ROWS, D), F32),
        shaped((8, D), F32),
    ],
    scratch=[pltpu.VMEM((ROWS, D), F32)],
)


def key_back_kernel(
    s_ref, kv_keep, kv_come, dk, dv, nk, inv, gain, cos, sin, ar, xr, hgrad, da_q, qg, small,
    a0, a1, a2, a3, keep_o, send_o, xp_o, xc_o, grads, both, da, cols
):
    place = s_ref[0]
    cosine = here(s_ref[0], cos)
    sine = here(s_ref[0], sin)
    inv_k = inv[:, 1:2]
    grads[0:HALF, :] = kv_keep[:, 0:KVW].astype(F32) + kv_come[:, 0:KVW].astype(F32)
    grads[HALF:ROWS, :] = dk[...]
    both[0:HALF, KVW:D] = (kv_keep[:, KVW:D].astype(F32) + kv_come[:, KVW:D].astype(F32)).astype(BF16)
    both[HALF:ROWS, KVW:D] = dv[...].astype(BF16)
    cols[...] = jnp.zeros_like(cols)
    dot = jnp.zeros((ROWS, 1), F32)
    for g in range(4):
        at = block(g, 128)
        back = turn_back(grads[:, at], cosine, sine)
        near = nk[:, at]
        kgrad = jnp.sum(back * near, axis=0, keepdims=True)
        cols[3:4, spot(place ^ g, QUART)] = jnp.concatenate([kgrad, jnp.zeros_like(kgrad)], axis=1)
        scaled = back * gain[0:1, 3 * D + g * 128 : 3 * D + (g + 1) * 128]
        dot = dot + jnp.sum(scaled * near, axis=1, keepdims=True)
        grads[:, at] = scaled
    both[:, 0:KVW] = (inv_k * (grads[...] - nk[...] * (dot / KVW))).astype(BF16)
    pre = both[...]
    for k, part in enumerate((a0, a1, a2, a3)):
        da[:, block(k, QUART)] = da_q[:, block(k, QUART)] + nt(pre, part[0:QUART, :])
        out = (keep_o, send_o)[k % 2]
        out[k // 2, :, 0:D] = tn(ar[:, block(k, QUART)], pre).astype(BF16)
    x = xr[...].astype(F32)
    inverse = inv[:, 2:3]
    n1 = x * inverse
    grad = da[...]
    cols[0:1, :] = jnp.sum(grad * n1, axis=0, keepdims=True)
    cols[1:2, :] = small[1:2, :]
    cols[16:32, :] = small[16:32, :]
    for k in range(4):
        cols[2:3, block(k, QUART)] = qg[0:1, spot(place ^ k, QUART)]
    for k in range(4):
        out = (keep_o, send_o)[k % 2]
        out[k // 2, :, D:BOUT] = cols[:, block(k, QUART)].T.astype(BF16)
    scaled = grad * gain[0:1, 0:D]
    result = hgrad[...] + inverse * (scaled - n1 * jnp.mean(scaled * n1, axis=1, keepdims=True))
    low = result.astype(BF16)
    for k in range(4):
        there = spot(place ^ k, QUART)
        xp_o[:, there] = low[0:HALF, block(k, QUART)]
        xc_o[:, there] = low[HALF:ROWS, block(k, QUART)]


key_back = whole_call(
    key_back_kernel,
    "key_back",
    [
        shaped((2, QUART, BOUT), BF16),
        shaped((2, QUART, BOUT), BF16),
        shaped((HALF, D), BF16),
        shaped((HALF, D), BF16),
    ],
    scratch=[
        pltpu.VMEM((ROWS, KVW), F32),
        pltpu.VMEM((ROWS, D), BF16),
        pltpu.VMEM((ROWS, D), F32),
        pltpu.VMEM((128, D), F32),
    ],
)


def finish_kernel(s_ref, hid, keep, come, xp_o, xc_o):
    total = hid[...] + RESIDUAL_SCALE * (keep[...].astype(F32) + come[...].astype(F32))
    low = total.astype(BF16)
    for k in range(4):
        there = spot(s_ref[0] ^ k, QUART)
        xp_o[:, there] = low[0:HALF, block(k, QUART)]
        xc_o[:, there] = low[HALF:ROWS, block(k, QUART)]


finish = whole_call(
    finish_kernel,
    "finish",
    [shaped((HALF, D), BF16), shaped((HALF, D), BF16)],
)


def pair_kernel(at_ref, qk, qc, lk, lc, ok, oc, t0, t1, t2, t3):
    for r, out in enumerate((t0, t1, t2, t3)):
        for v in range(4):
            rows = spot(piece_to(at_ref, r, v), PROWS)
            for k in range(2):
                last = (lk[k, rows, :].astype(F32) + lc[k, rows, :].astype(F32)).astype(BF16)
                out[v, k, :, 0:D] = (qk[k, rows, :].astype(F32) + qc[k, rows, :].astype(F32)).astype(BF16)
                out[v, k, :, D:QKVW] = last[:, 0:D]
                out[v, k, :, QKVW : QKVW + D] = (
                    ok[k, rows, :].astype(F32) + oc[k, rows, :].astype(F32)
                ).astype(BF16)
                out[v, k, :, QKVW + D :] = last[:, D:]


pair = whole_call(pair_kernel, "pair", [shaped((4, 2, PROWS, ATTW), BF16)] * 4)


def fold_kernel(at_ref, i0, i1, i2, i3, o0, o1, o2, o3):
    for r, out in enumerate((o0, o1, o2, o3)):
        there = (at_ref[1] + r) % 4
        total = i0[there].astype(F32) + i1[there].astype(F32)
        out[...] = (total + i2[there].astype(F32) + i3[there].astype(F32)).astype(BF16)


def fold(at, parts, rows, steps):
    shape = parts[0].shape
    width = shape[-1]
    flat = [part.reshape(4, rows, width) for part in parts]
    height = rows // steps
    outs = pl.pallas_call(
        fold_kernel,
        name="fold",
        grid=(steps,),
        in_specs=[SMEM] + [pl.BlockSpec((4, height, width), lambda i: (0, i, 0))] * 4,
        out_specs=[pl.BlockSpec((height, width), lambda i: (i, 0))] * 4,
        out_shape=[shaped((rows, width), BF16)] * 4,
        compiler_params=pltpu.CompilerParams(vmem_limit_bytes=56 * 1024 * 1024),
        cost_estimate=COST,
    )(at, *flat)
    return [out.reshape(shape[1:]) for out in outs]


def unpack_kernel(s_ref, at_ref, p0, p1, p2, p3, p4, gate_o, up_o, down_o, tile):
    for r, part, low in ((0, p0, 0), (1, p1, 0), (2, p2, 0), (2, p3, 2), (3, p4, 0)):
        for n in range(part.shape[0]):
            rows = spot(piece_at(at_ref, r, low + n), PROWS)
            for k in range(4):
                tile[k, rows, :] = part[n, k, 0]
    for k in range(4):
        there = spot(s_ref[0] ^ k, FSLICE)
        part = tile[k].astype(F32)
        gate_o[0, :, there] = part[:, 0:FSLICE]
        up_o[0, :, there] = part[:, FSLICE : 2 * FSLICE]
        down_o[0, there, :] = part[:, 2 * FSLICE :].T


def unpack_experts(place, at, parts):
    specs = [
        pl.BlockSpec((part.shape[0], 4, 1, PROWS, TILE), lambda e: (0, 0, e, 0, 0))
        for part in parts
    ]
    return pl.pallas_call(
        unpack_kernel,
        name="unpack_experts",
        grid=(EXPERTS,),
        in_specs=[SMEM] * 2 + specs,
        out_specs=[
            pl.BlockSpec((1, QUART, 512), lambda e: (e, 0, 0)),
            pl.BlockSpec((1, QUART, 512), lambda e: (e, 0, 0)),
            pl.BlockSpec((1, 512, QUART), lambda e: (e, 0, 0)),
        ],
        out_shape=[
            shaped((EXPERTS, QUART, 512), F32),
            shaped((EXPERTS, QUART, 512), F32),
            shaped((EXPERTS, 512, QUART), F32),
        ],
        scratch_shapes=[pltpu.VMEM((4, QUART, TILE), BF16)],
        compiler_params=pltpu.CompilerParams(vmem_limit_bytes=56 * 1024 * 1024),
        cost_estimate=COST,
    )(place, at, *parts)


def unpack_attention_kernel(
    at_ref, p0, p1, p2, p3, wq_o, wk_o, wv_o, wo_o, attn_o, ffn_o, qg_o, kg_o, router_o, wide
):
    for r, part in enumerate((p0, p1, p2, p3)):
        for n in range(4):
            wide[spot(piece_at(at_ref, r, n), PROWS), :] = part[n]
    wq_o[...] = wide[:, 0:D].astype(F32)
    wk_o[...] = wide[:, D : D + KVW].astype(F32)
    wv_o[...] = wide[:, D + KVW : QKVW].astype(F32)
    for g in range(4):
        wo_o[block(g, QUART), :] = wide[:, QKVW + g * QUART : QKVW + (g + 1) * QUART].astype(F32)
    tail = wide[:, QKVW + D :].astype(F32)
    rows = tail.T
    attn_o[...] = rows[0:1]
    ffn_o[...] = rows[1:2]
    qg_o[...] = rows[2:3]
    kg_o[...] = rows[3:4, 0:HALF]
    router_o[...] = rows[16 : 16 + EXPERTS]


unpack_attention = whole_call(
    unpack_attention_kernel,
    "unpack_attention",
    [
        shaped((QUART, D), F32),
        shaped((QUART, KVW), F32),
        shaped((QUART, KVW), F32),
        shaped((D, QUART), F32),
        shaped((1, QUART), F32),
        shaped((1, QUART), F32),
        shaped((1, QUART), F32),
        shaped((1, HALF), F32),
        shaped((EXPERTS, QUART), F32),
    ],
    scratch=[pltpu.VMEM((QUART, ATTW), BF16)],
)


def body(
    prompt_x, cont_x, prompt_cot, cont_cot, prompt_routes, cont_routes,
    attn_gain, w_query, w_key, w_value, query_gain, key_gain,
    w_out, ffn_gain, w_router, w_gate, w_up, w_down,
):
    def moved(value, axes, change):
        sizes = [lax.axis_size(a) for a in axes]
        pairs = []
        count = 1
        for size in sizes:
            count *= size
        for index in range(count):
            rest, coords = index, []
            for size in reversed(sizes):
                coords.append(rest % size)
                rest //= size
            to = change(*reversed(coords))
            target = 0
            for size, coord in zip(sizes, to):
                target = target * size + coord
            pairs.append((index, target))
        return lax.ppermute(value, axes, pairs)

    def sib(value):
        return moved(value, ("c",), lambda c: (1 - c,))

    def far(value):
        return moved(value, ("xh",), lambda h: (1 - h,))

    def far_sib(value):
        return moved(value, ("xh", "c"), lambda h, c: (1 - h, 1 - c))

    def cross(value):
        return moved(value, ("xl", "xh"), lambda low, high: (1 - low, 1 - high))

    def cross_sib(value):
        return moved(value, ("xl", "xh", "c"), lambda low, high, c: (1 - low, 1 - high, 1 - c))

    def near(value):
        return moved(value, ("xl",), lambda low: (1 - low,))

    def along(value, by, core_of_z):
        def change(at_z, at_y, c):
            if c == core_of_z:
                return ((at_z + by) % 4, at_y, c)
            return (at_z, (at_y + by) % 4, c)

        return moved(value, ("z", "y", "c"), change)

    def first(value, by):
        return along(value, by, 1)

    def second(value, by):
        return along(value, by, 0)

    def spread(value, way):
        return [value] + [way(value, by) for by in (1, 2, 3)]

    def added(parts):
        total = parts[0].astype(F32)
        for part in parts[1:]:
            total = total + part.astype(F32)
        return total.astype(BF16)

    after = lax.optimization_barrier

    z = lax.axis_index("z").astype(jnp.int32)
    y = lax.axis_index("y").astype(jnp.int32)
    core = lax.axis_index("c").astype(jnp.int32)
    low_core = core == 0
    at = jnp.stack(
        [
            jnp.where(low_core, y, z),
            jnp.where(low_core, z, y),
            jnp.where(low_core, 1, 4),
            jnp.where(low_core, 4, 1),
        ]
    )
    position = lax.axis_index(("xh", "c")).astype(jnp.int32)
    place = position[None]
    piece = 4 * z + y
    cont_in = cont_x.reshape(HALF, D)
    cont_up = cont_cot.reshape(HALF, D)

    def held(value, *others):
        return after((value, others))[0]

    share_two, share_three = share_experts(
        jnp.concatenate([piece[None], place]), w_gate, w_up, w_down, w_out
    )
    place_in, share_two, share_three = after((place, share_two, share_three))
    share_two = cross(share_two)
    share_three = cross_sib(share_three)
    own_in = prepare(
        place_in, w_query, w_key, w_value, attn_gain[None], ffn_gain[None], query_gain[None],
        key_gain[None], w_router.T,
    )
    place_in, own_in, share_two, share_three = after((place, own_in, share_two, share_three))
    in_two = cross(own_in)
    own_out = prepare_out(place_in, w_out)
    row = jnp.stack(spread(jnp.stack([share_two, share_three]), second))
    packed = pack_experts(place_in, w_gate, w_up, w_down)
    in_two, packed, row, own_in_sib, own_out = after((in_two, packed, row, sib(own_in), own_out))
    row_one = first(row, 1)
    row_three = first(row, 3)
    far_parts = (row, row_one, first(row, 2), row_three)
    in_parts = (own_in, own_in_sib, in_two, sib(in_two))
    out_parts = (own_out, sib(own_out))

    cosine, sine = (jnp.asarray(table) for table in angle_tables())

    kv, kv_own, nk, inv, xr, ar, gain, rt = project_keys(
        place, prompt_x, cont_in, *in_parts, cosine, sine
    )
    kv_two = far(kv_own)
    upstream = held(jnp.concatenate([prompt_cot, cont_up], axis=0), nk)
    up_two = cross(upstream)
    q, nq, inv_q = project_query(place, ar, gain, *in_parts, cosine, sine)
    kv_two, packed = after((kv_two, packed, q, row_one, row_three))[0:2]
    kv_parts = (kv, sib(kv_own), kv_two, sib(kv_two))
    mixed, lse = attend(place, q, *kv_parts)
    hidden, b, gates, out_far = route(
        place, at, mixed, *out_parts, far_parts, xr, gain, rt, prompt_routes,
        cont_routes.reshape(HALF, 8),
    )
    up_sib = sib(upstream)
    w_parts = (packed[0], sib(packed[1]), *far_parts)
    b, up_two, up_sib, w_parts = after((b, up_two, up_sib, w_parts))
    up_parts = (upstream, up_sib, up_two, sib(up_two))
    b_two = cross(b)
    b_parts = (b, sib(b), b_two, sib(b_two))
    dudw, gz, db_keep, db_send = experts(place, at, b_parts, up_parts, w_parts)

    db_come = sib(db_send)
    db_sum = added([db_keep, db_come])
    db_sum, dudw = after((db_sum, dudw))
    db_far = cross(db_sum[1])
    grads = expert_grads(place, at, b_parts, up_parts, dudw, gz)
    grads, db_far, later = after((grads, db_far, place))
    grad_one = first(grads[1], 1)
    grad_three = first(grads[3], 3)

    hgrad, small, dwo_keep, dwo_send, dq, kv_keep, kv_send, dk, dv = attend_back(
        later, db_sum[0], db_far, hidden, b, gates, prompt_cot, cont_up, gain, rt, mixed, lse,
        q, *kv_parts, *out_parts, out_far,
    )

    kv_send, grad_one, grad_three, grad_next = after((kv_send, grad_one, grad_three, grads[2]))
    grad_two = first(grad_next, 2)
    kv_come = sib(kv_send)
    kv_sum = added([kv_keep, kv_come])
    kv_far = far(kv_sum[1])
    dq, kv_sum = after((dq, kv_sum))
    dwq_keep, dwq_send, da_q, qg = query_back(
        place, dq, nq, inv_q, gain, cosine, sine, ar, *in_parts
    )
    last_keep, last_send, prompt_grad, cont_grad = key_back(
        place, kv_sum[0], kv_far, dk, dv, nk, inv, gain, cosine, sine, ar, xr, hgrad, da_q, qg,
        small, *in_parts,
    )

    grad_two, last_keep = after((grad_two, last_keep))
    grad_rest = fold(at, [grads[0], grad_one, grad_two, grad_three], 4 * EXPERTS * PROWS, 4)
    paired = pair(
        held(at, grad_rest), dwq_keep, sib(dwq_send), last_keep, sib(last_send), dwo_keep, sib(dwo_send)
    )
    grad_rest = [grad_rest[0]] + [second(grad_rest[by], by) for by in (1, 2, 3)]
    summed = added(held(grad_rest, paired[0]))
    paired = [paired[0]] + [first(paired[by], by) for by in (1, 2, 3)]

    turned_parts = [summed[0], sib(summed[1]), far(summed[2]), far_sib(summed[3])]
    paired[1], paired[3], turned_parts = after((paired[1], paired[3], turned_parts))
    turned_parts = jnp.stack(turned_parts, axis=0)
    near_parts = near(turned_parts)
    mix_keep, mix_send = mixture(at, held(gz, turned_parts), w_parts)
    own_sum = added([turned_parts, held(near_parts, mix_keep)])
    paired = fold(at, held(paired, turned_parts), 2 * PROWS, 1)
    steps = jnp.stack(spread(own_sum, second))
    steps_one = first(steps, 1)
    steps_three = first(steps, 3)

    mix_sum = added([mix_keep, sib(mix_send)])
    mix_far = cross(mix_sum[1])
    prompt_out, cont_out = finish(place, hidden, mix_sum[0], mix_far)

    paired = held(paired, steps)
    part = added([paired[0]] + [second(paired[by], by) for by in (1, 2, 3)])
    part = added([part[0], near(part[0]), far(part[1]), cross(part[1])])
    part_steps = jnp.stack(spread(part, second))
    steps_one, steps_three, part_steps = after((steps_one, steps_three, part_steps))
    steps_two = (first(steps_one[0:2], 1), first(steps_three[2:4], 3))
    full = spread(part_steps, first)
    gate_grad, up_grad, down_grad = unpack_experts(
        place, at, (steps, steps_one, *steps_two, steps_three)
    )
    wq_grad, wk_grad, wv_grad, wo_grad, attn_grad, ffn_grad, qg_grad, kg_grad, router_grad = (
        unpack_attention(at, *held(full, gate_grad))
    )

    return (
        prompt_out,
        cont_out.reshape(1, HALF, D),
        prompt_grad,
        cont_grad.reshape(1, HALF, D),
        attn_grad[0],
        wq_grad,
        wk_grad,
        wv_grad,
        qg_grad[0],
        kg_grad[0],
        wo_grad,
        ffn_grad[0],
        router_grad.T,
        gate_grad,
        up_grad,
        down_grad,
    )


def solution(mesh):
    fine = Mesh(mesh.devices.reshape(2, 4, 4, 2, 2), AXES)
    shard = ("xh", "c")
    tokens = P(AXES, None)
    series = P(AXES, None, None)
    weights = (
        P(shard),
        P(shard, None),
        P(shard, None),
        P(shard, None),
        P(shard),
        P(shard),
        P(None, shard),
        P(shard),
        P(shard, None),
        P(None, shard, None),
        P(None, shard, None),
        P(None, None, shard),
    )
    return jax.shard_map(
        body,
        mesh=fine,
        in_specs=(tokens, series, tokens, series, tokens, series, *weights),
        out_specs=(tokens, series, tokens, series, *weights),
        check_vma=False,
    )
```

```python
import jax
import jax.numpy as jnp
import numpy as np
from jax import lax
from jax.experimental import pallas as pl
from jax.experimental.pallas import tpu as pltpu
from jax.sharding import Mesh, PartitionSpec as P

EPSILON = 1e-06
SCORE_SCALE = 0.25
RESIDUAL_SCALE = 0.22
ROTARY_BASE = 10000.0
MASKED = -1e30

D = 1024
HDIM = 64
PAIRS = 4
KVW = 512
QKVW = 2048
ROWS = 256
HALF = 128
QUART = 256
EXPERTS = 9
FSLICE = 128
TILE = 3 * FSLICE
TOKENS = 4 * ROWS
KEYS = 5 * HALF
BOUT = D + 128
ATTW = QKVW + D + 128
PIECES = 16
PROWS = QUART // PIECES
SHAREW = EXPERTS * TILE
GROUP = 3

F32 = jnp.float32
BF16 = jnp.bfloat16


def angle_tables():
    frequency = np.float32(ROTARY_BASE) ** (-np.arange(0, HDIM, 2, dtype=np.float32) / HDIM)
    turned = np.arange(KEYS, dtype=np.float32)[:, None] * frequency.astype(np.float32)[None, :]
    cosine = np.tile(np.cos(turned), (1, 4)).astype(np.float32)
    sine = np.sin(turned)
    sine = np.concatenate([-sine, sine, -sine, sine], axis=1).astype(np.float32)
    return cosine, sine


AXES = ("xl", "z", "y", "xh", "c")


def nn(left, right):
    return lax.dot_general(left, right, (((1,), (0,)), ((), ())), preferred_element_type=F32)


def nt(left, right):
    return lax.dot_general(left, right, (((1,), (1,)), ((), ())), preferred_element_type=F32)


def tn(left, right):
    return lax.dot_general(left, right, (((0,), (0,)), ((), ())), preferred_element_type=F32)


def spot(index, width):
    return pl.ds(pl.multiple_of(index * width, width), width)


def block(index, width):
    return slice(index * width, (index + 1) * width)


SMEM = pl.BlockSpec(memory_space=pltpu.SMEM)
VMEM = pl.BlockSpec(memory_space=pltpu.VMEM)


COST = pl.CostEstimate(flops=1_000_000, bytes_accessed=1_000_000, transcendentals=0)


def whole_call(kernel, name, out_shape, scratch=(), limit=24, parts=None):
    def whole(shape, index=None):
        index = index or (0,) * len(shape)
        return pl.BlockSpec(shape, lambda i: index)

    def call(*operands):
        specs = [
            whole(*parts[n]) if parts and n in parts else whole(operand.shape)
            for n, operand in enumerate(operands)
        ]
        return pl.pallas_call(
            kernel,
            name=name,
            out_shape=out_shape,
            grid=(1,),
            in_specs=[SMEM] + specs[1:],
            out_specs=jax.tree.map(lambda out: whole(out.shape), out_shape),
            scratch_shapes=list(scratch),
            compiler_params=pltpu.CompilerParams(vmem_limit_bytes=limit * 1024 * 1024),
            cost_estimate=COST,
        )(*operands)

    return call


def shaped(shape, dtype):
    return jax.ShapeDtypeStruct(shape, dtype)


def pack_kernel(s_ref, gate, up, down, own, other):
    turned = down[0].T
    for k, out in ((0, own), (1, other)):
        low = (s_ref[0] % 2) == k
        for n, part in enumerate((gate[0], up[0], turned)):
            half = jnp.where(low, part[:, 0:FSLICE], part[:, FSLICE:])
            out[0, :, block(n, FSLICE)] = half.astype(BF16)


def pack_experts(place, w_gate, w_up, w_down):
    wide = pl.BlockSpec((1, QUART, 2 * FSLICE), lambda e, s: (e, 0, s[0] // 2))
    out = pl.BlockSpec((1, QUART, TILE), lambda e, s: (e, 0, 0))
    return pl.pallas_call(
        pack_kernel,
        name="pack_experts",
        grid_spec=pltpu.PrefetchScalarGridSpec(
            num_scalar_prefetch=1,
            grid=(EXPERTS,),
            in_specs=[
                wide,
                wide,
                pl.BlockSpec((1, 2 * FSLICE, QUART), lambda e, s: (e, s[0] // 2, 0)),
            ],
            out_specs=[out, out],
        ),
        out_shape=[shaped((EXPERTS, QUART, TILE), BF16)] * 2,
        compiler_params=pltpu.CompilerParams(vmem_limit_bytes=56 * 1024 * 1024),
        cost_estimate=COST,
    )(place, w_gate, w_up, w_down)


def share_kernel(at_ref, gate, up, down, two, three, turned):
    for k, dest in ((2, two), (3, three)):
        there = spot(at_ref[1] ^ k, FSLICE)
        for e in range(EXPERTS):
            at = e * TILE
            dest[:, at : at + FSLICE] = gate[e, :, there].astype(BF16)
            dest[:, at + FSLICE : at + 2 * FSLICE] = up[e, :, there].astype(BF16)
            turned[...] = down[e, there, :].T
            dest[:, at + 2 * FSLICE : at + TILE] = turned[
                spot(at_ref[0] % 8, PROWS), :
            ].astype(BF16)


def share_experts(at, w_gate, w_up, w_down):
    rows = pl.BlockSpec((EXPERTS, PROWS, 512), lambda i, at: (0, at[0], 0))
    dest = pl.BlockSpec((PROWS, SHAREW), lambda i, at: (0, 0))
    return pl.pallas_call(
        share_kernel,
        name="share_experts",
        grid_spec=pltpu.PrefetchScalarGridSpec(
            num_scalar_prefetch=1,
            grid=(1,),
            in_specs=[
                rows,
                rows,
                pl.BlockSpec((EXPERTS, 512, 128), lambda i, at: (0, 0, at[0] // 8)),
            ],
            out_specs=[dest, dest],
            scratch_shapes=[pltpu.VMEM((128, FSLICE), F32)],
        ),
        out_shape=[shaped((PROWS, SHAREW), BF16)] * 2,
        compiler_params=pltpu.CompilerParams(vmem_limit_bytes=56 * 1024 * 1024),
        cost_estimate=COST,
    )(at, w_gate, w_up, w_down)


def prepare_kernel(s_ref, wq, wk, wv, attn, ffn, query, key, router, kv_o, line):
    kv_o[0:QUART, :] = wq[...].astype(BF16)
    kv_o[QUART : 2 * QUART, 0:KVW] = wk[...].astype(BF16)
    kv_o[QUART : 2 * QUART, KVW:D] = wv[...].astype(BF16)
    line[...] = jnp.zeros_like(line)
    line[0:1, 0:256] = attn[...]
    line[0:1, 256:512] = ffn[...]
    line[0:1, 512:768] = query[...]
    line[0:1, 768:896] = key[...]
    kv_o[2 * QUART : 2 * QUART + 16, :] = line[...].astype(BF16)
    line[...] = jnp.zeros_like(line)
    line[0:EXPERTS, 0:QUART] = router[...]
    kv_o[2 * QUART + 16 :, :] = line[...].astype(BF16)


prepare = whole_call(
    prepare_kernel,
    "prepare",
    shaped((2 * QUART + 32, D), BF16),
    scratch=[pltpu.VMEM((16, D), F32)],
    limit=56,
)


def swapped(values):
    lane = lax.broadcasted_iota(jnp.int32, values.shape, 1)
    return jnp.where(
        lane % HDIM < HDIM // 2, pltpu.roll(values, 96, axis=1), pltpu.roll(values, 32, axis=1)
    )


def here(place, table):
    return jnp.concatenate([table[spot(place, HALF), :], table[4 * HALF :, :]], axis=0)


def project_keys_kernel(
    s_ref, xp, xc, a0, a1, a2, a3, cos, sin, kv_o, kvp_o, nk_o, inv_o, xr_o, ar_o, gain_o, rt_o, acc
):
    parts = (a0, a1, a2, a3)
    for k in range(4):
        there = s_ref[0] ^ k
        xr_o[0:HALF, block(k, QUART)] = xp[:, spot(there, QUART)]
        xr_o[HALF:ROWS, block(k, QUART)] = xc[:, spot(there, QUART)]
        small = parts[k][2 * QUART : 2 * QUART + 16, :].astype(F32)[0:1]
        gain_o[0:1, block(k, QUART)] = small[:, 0:256]
        gain_o[0:1, slice(D + k * QUART, D + (k + 1) * QUART)] = small[:, 256:512]
        gain_o[0:1, pl.ds(pl.multiple_of(2 * D + there * QUART, 128), QUART)] = small[:, 512:768]
        gain_o[0:1, pl.ds(pl.multiple_of(3 * D + there * HALF, 128), HALF)] = small[:, 768:896]
        rt_o[:, block(k, QUART)] = parts[k][2 * QUART + 16 :, 0:QUART]
    x = xr_o[...].astype(F32)
    inverse = lax.rsqrt(jnp.mean(x * x, axis=1, keepdims=True) + EPSILON)
    ar_o[...] = (x * inverse * gain_o[0:1, 0:D]).astype(BF16)
    total = nn(ar_o[:, block(0, QUART)], parts[0][QUART : 2 * QUART, :])
    for k in range(1, 4):
        total = total + nn(ar_o[:, block(k, QUART)], parts[k][QUART : 2 * QUART, :])
    acc[...] = total
    kp = acc[:, 0:KVW]
    inv_k = lax.rsqrt(jnp.mean(kp * kp, axis=1, keepdims=True) + EPSILON)
    nk_o[...] = kp * inv_k
    lane = lax.broadcasted_iota(jnp.int32, (ROWS, 128), 1)
    inv_o[...] = jnp.where(lane == 1, inv_k, inverse)
    kv_o[:, KVW:D] = acc[:, KVW:D].astype(BF16)
    cosine = here(s_ref[0], cos)
    sine = here(s_ref[0], sin)
    for g in range(4):
        at = block(g, 128)
        u = nk_o[:, at] * gain_o[0:1, 3 * D + g * 128 : 3 * D + (g + 1) * 128]
        kv_o[:, at] = (u * cosine + swapped(u) * sine).astype(BF16)
    kvp_o[...] = kv_o[0:HALF, :]


project_keys = whole_call(
    project_keys_kernel,
    "project_keys",
    [
        shaped((ROWS, D), BF16),
        shaped((HALF, D), BF16),
        shaped((ROWS, KVW), F32),
        shaped((ROWS, 128), F32),
        shaped((ROWS, D), BF16),
        shaped((ROWS, D), BF16),
        shaped((8, 3 * D + KVW), F32),
        shaped((16, D), BF16),
    ],
    scratch=[pltpu.VMEM((ROWS, D), F32)],
    limit=56,
)


def prepare_out_kernel(s_ref, wo, out):
    for g in range(4):
        out[:, block(g, QUART)] = wo[block(g, QUART), :].astype(BF16)


prepare_out = whole_call(
    prepare_out_kernel, "prepare_out", shaped((QUART, D), BF16), limit=56
)


def project_query_kernel(s_ref, ar, gain, a0, a1, a2, a3, cos, sin, q_o, nq_o, inv_o):
    total = nn(ar[:, block(0, QUART)], a0[...])
    for k, part in ((1, a1), (2, a2), (3, a3)):
        total = total + nn(ar[:, block(k, QUART)], part[...])
    nq_o[...] = total
    inv_q = lax.rsqrt(jnp.mean(total * total, axis=1, keepdims=True) + EPSILON)
    inv_o[...] = jnp.broadcast_to(inv_q, (ROWS, 128))
    cosine = here(s_ref[0], cos)
    sine = here(s_ref[0], sin)
    for g in range(8):
        at = block(g, 128)
        near = nq_o[:, at] * inv_q
        nq_o[:, at] = near
        u = near * gain[0:1, 2 * D + g * 128 : 2 * D + (g + 1) * 128]
        q_o[:, at] = (u * cosine + swapped(u) * sine).astype(BF16)


project_query = whole_call(
    project_query_kernel,
    "project_query",
    [shaped((ROWS, D), BF16), shaped((ROWS, D), F32), shaped((ROWS, 128), F32)],
    parts={n: ((QUART, D), (0, 0)) for n in range(3, 7)},
    limit=56,
)


def fill_bias(place, bias):
    row = lax.broadcasted_iota(jnp.int32, (HALF, 512), 0)
    lane = lax.broadcasted_iota(jnp.int32, (HALF, 512), 1)
    causal = jnp.where(row <= lane % HALF, 0.0, MASKED)
    is_prompt = lane % ROWS < HALF
    bias[0:HALF, :] = jnp.where(is_prompt, causal, 0.0)
    for k in range(1, 4):
        level = jnp.where((place ^ k) < place, 0.0, MASKED)
        bias[block(k, HALF), :] = jnp.where(is_prompt, level, 0.0)
    bias[4 * HALF :, :] = jnp.where(is_prompt, MASKED, causal)


def fill_keys(refs, keys, values):
    for j in range(4):
        keys[block(j, HALF), :] = refs[j][0:HALF, 0:KVW]
        values[block(j, HALF), :] = refs[j][0:HALF, KVW:D]
    keys[4 * HALF :, :] = refs[0][HALF:ROWS, 0:KVW]
    values[4 * HALF :, :] = refs[0][HALF:ROWS, KVW:D]


def doubled(ref, pair, odd):
    both = ref[:, spot(pair, 128)]
    other = pltpu.roll(both.astype(F32), HDIM, axis=1).astype(BF16)
    lane = lax.broadcasted_iota(jnp.int32, both.shape, 1)
    return jnp.where((lane < HDIM) == (odd == 0), both, other)


def stacked(ref, head, scale):
    rows = ref[:, spot(head, 128)]
    lane = lax.broadcasted_iota(jnp.int32, rows.shape, 1)
    rows = rows * jnp.asarray(scale, rows.dtype)
    none = jnp.zeros_like(rows)
    return jnp.concatenate(
        [jnp.where(lane < HDIM, rows, none), jnp.where(lane < HDIM, none, rows)], axis=0
    )


def attend_kernel(s_ref, q, kv0, kv1, kv2, kv3, mixed_o, lse_o, bias, keys, values):
    fill_bias(s_ref[0], bias)
    fill_keys((kv0, kv1, kv2, kv3), keys, values)

    def one_pair(pair, carry):
        for odd in range(2):
            head = 2 * pair + odd
            kk = doubled(keys, pair, odd)
            vv = doubled(values, pair, odd)
            scores = nt(kk, stacked(q, head, SCORE_SCALE)) + bias[...]
            highest = jnp.max(scores, axis=0, keepdims=True)
            raised = jnp.exp(scores - highest)
            totals = jnp.sum(raised, axis=0, keepdims=True)
            probs = (raised * (1.0 / totals)).astype(BF16)
            lse_o[pl.ds(head, 1), :] = highest + jnp.log(totals)
            out = tn(vv, probs).T
            lane = lax.broadcasted_iota(jnp.int32, (ROWS, 128), 1)
            mixed_o[:, spot(head, 128)] = jnp.where(
                lane < HDIM, out[0:ROWS], out[ROWS : 2 * ROWS]
            ).astype(BF16)
        return carry

    lax.fori_loop(0, PAIRS, one_pair, 0)


attend = whole_call(
    attend_kernel,
    "attend",
    [shaped((ROWS, D), BF16), shaped((8, 512), F32)],
    scratch=[
        pltpu.VMEM((KEYS, 512), F32),
        pltpu.VMEM((KEYS, KVW), BF16),
        pltpu.VMEM((KEYS, KVW), BF16),
    ],
    limit=56,
)


def route_kernel(s_ref, mixed_ref, o0, o1, o2, o3, xr, gain, rt, rp, rc, hid_o, b_o, gates_o):
    for k, part in enumerate((o0, o1, o2, o3)):
        total = nn(mixed_ref[:, block(0, QUART)], part[:, block(0, QUART)])
        for g in range(1, 4):
            total = total + nn(mixed_ref[:, block(g, QUART)], part[:, block(g, QUART)])
        hid_o[:, block(k, QUART)] = xr[:, block(k, QUART)].astype(F32) + RESIDUAL_SCALE * total
    hidden = hid_o[...]
    inverse = lax.rsqrt(jnp.mean(hidden * hidden, axis=1, keepdims=True) + EPSILON)
    b_o[:, 0:D] = (hidden * inverse * gain[0:1, D : 2 * D]).astype(BF16)
    logits = nt(rt[...], b_o[:, 0:D])
    expert = lax.broadcasted_iota(jnp.int32, (16, HALF), 0)
    for half, routes in enumerate((rp, rc)):
        chosen = routes[0:1, :] == expert
        for r in range(1, 8):
            chosen = chosen | (routes[r : r + 1, :] == expert)
        level = jnp.where(chosen, logits[:, block(half, HALF)], MASKED)
        raised = jnp.exp(level - jnp.max(level, axis=0, keepdims=True))
        gates = raised / jnp.sum(raised, axis=0, keepdims=True)
        gates = jnp.concatenate([gates, jnp.zeros((112, HALF), F32)], axis=0).T
        gates_o[block(half, HALF), :] = gates
        high = gates.astype(BF16).astype(F32)
        b_o[block(half, HALF), D:BOUT] = (high + pltpu.roll(gates - high, 16, axis=1)).astype(BF16)


route = whole_call(
    route_kernel,
    "route",
    [shaped((ROWS, D), F32), shaped((ROWS, BOUT), BF16), shaped((ROWS, 128), F32)],
    limit=56,
)


def piece_at(at, r, n):
    return ((at[0] + 4 - r) % 4) * at[2] + ((at[1] + 4 - n) % 4) * at[3]


def piece_at(at, r, n):
    return ((at[0] + 4 - r) % 4) * at[2] + ((at[1] + 4 - n) % 4) * at[3]


def fill_weights(at, own, other, far_parts, dest, lanes):
    dest[block(0, QUART), lanes] = own
    dest[block(1, QUART), lanes] = other
    for r in range(4):
        for n in range(4):
            piece = piece_at(at, r, n)
            for k in range(2):
                dest[spot((2 + k) * PIECES + piece, PROWS), lanes] = far_parts[r][n, k]


def expert_kernel(
    s_ref, at_ref, b0, b1, b2, b3, g0, g1, g2, g3, w0, w1, f0, f1, f2, f3,
    dudw_o, gz_o, dbk_o, dbs_o, xs, gs, gates, dgs, wgu, wd, dudw
):
    step = pl.program_id(0)
    place = s_ref[0]

    @pl.when(step == 0)
    def _():
        for j, (b_ref, g_ref) in enumerate(zip((b0, b1, b2, b3), (g0, g1, g2, g3))):
            rows = block(j, ROWS)
            for k in range(4):
                xs[rows, block(k, QUART)] = b_ref[:, block(k ^ j, QUART)]
                gs[rows, block(k, QUART)] = g_ref[:, spot(place ^ k, QUART)]
            both = b_ref[:, D:BOUT].astype(F32)
            gates[rows, :] = both + pltpu.roll(both, 112, axis=1)
        dgs[...] = jnp.zeros_like(dgs)

    here_gu = spot(step, 2 * GROUP * FSLICE)
    for n in range(GROUP):
        up = slice(n * TILE, n * TILE + 2 * FSLICE)
        down = slice(n * TILE + 2 * FSLICE, (n + 1) * TILE)
        for k, part in enumerate((w0, w1)):
            wgu[step, block(k, QUART), block(n, 2 * FSLICE)] = part[n, :, 0 : 2 * FSLICE]
            wd[block(k, QUART), block(n, FSLICE)] = part[n, :, 2 * FSLICE :]
        for r, part in enumerate((f0, f1, f2, f3)):
            for m in range(4):
                for k in range(2):
                    rows = spot((2 + k) * PIECES + piece_at(at_ref, r, m), PROWS)
                    wgu[step, rows, block(n, 2 * FSLICE)] = part[m, k, :, up]
                    wd[rows, block(n, FSLICE)] = part[m, k, :, down]
    both = nn(xs[...], wgu[step])
    h_all = RESIDUAL_SCALE * nn(gs[...], wd[...])
    lane = lax.broadcasted_iota(jnp.int32, (TOKENS, 128), 1)
    added = jnp.zeros((TOKENS, 128), F32)
    for n in range(GROUP):
        e = step * GROUP + n
        u = both[:, 2 * n * FSLICE : (2 * n + 1) * FSLICE]
        w = both[:, (2 * n + 1) * FSLICE : (2 * n + 2) * FSLICE]
        h = h_all[:, block(n, FSLICE)]
        gate = jnp.sum(jnp.where(lane == e, gates[...], 0.0), axis=1, keepdims=True)
        sig = jax.nn.sigmoid(u)
        silu = u * sig
        z = (silu * w).astype(BF16).astype(F32)
        gz_o[:, block(n, FSLICE)] = (gate * z).astype(BF16)
        added = added + jnp.where(lane == e, jnp.sum(z * h, axis=1, keepdims=True), 0.0)
        dz = gate * h
        du = (dz * w * sig * (1.0 + u * (1.0 - sig))).astype(BF16)
        dw = (dz * silu).astype(BF16)
        dudw_o[:, block(2 * n, FSLICE)] = du
        dudw_o[:, block(2 * n + 1, FSLICE)] = dw
    dgs[...] += added
    dudw[:, here_gu] = dudw_o[...]

    @pl.when(step == EXPERTS // GROUP - 1)
    def _():
        width = 2 * GROUP * FSLICE
        whole = nt(dudw[:, 0:width], wgu[0])
        for n in range(1, EXPERTS // GROUP):
            whole = whole + nt(dudw[:, block(n, width)], wgu[n])
        whole = whole.astype(BF16)
        for j in range(4):
            out = (dbk_o, dbs_o)[j % 2]
            rows = block(j, ROWS)
            for k in range(4):
                out[j // 2, :, block(k ^ j, QUART)] = whole[rows, block(k, QUART)]
            dg = dgs[rows, 0:16]
            high = dg.astype(BF16).astype(F32)
            out[j // 2, :, D:BOUT] = jnp.concatenate(
                [high, dg - high, jnp.zeros((ROWS, 96), F32)], axis=1
            ).astype(BF16)


def fixed(rank):
    return lambda e: (0,) * rank


def experts(place, at, b_parts, g_parts, w_parts):
    return pl.pallas_call(
        expert_kernel,
        name="experts",
        grid=(EXPERTS // GROUP,),
        in_specs=[SMEM] * 2
        + [pl.BlockSpec((ROWS, BOUT), fixed(2))] * 4
        + [pl.BlockSpec((ROWS, D), fixed(2))] * 4
        + [pl.BlockSpec((GROUP, QUART, TILE), lambda e: (e, 0, 0))] * 2
        + [pl.BlockSpec((4, 2, PROWS, GROUP * TILE), lambda e: (0, 0, 0, e))] * 4,
        out_specs=[
            pl.BlockSpec((TOKENS, 2 * GROUP * FSLICE), lambda e: (0, e)),
            pl.BlockSpec((TOKENS, GROUP * FSLICE), lambda e: (0, e)),
            pl.BlockSpec((2, ROWS, BOUT), fixed(3)),
            pl.BlockSpec((2, ROWS, BOUT), fixed(3)),
        ],
        out_shape=[
            shaped((TOKENS, EXPERTS * 2 * FSLICE), BF16),
            shaped((TOKENS, EXPERTS * FSLICE), BF16),
            shaped((2, ROWS, BOUT), BF16),
            shaped((2, ROWS, BOUT), BF16),
        ],
        scratch_shapes=[
            pltpu.VMEM((TOKENS, D), BF16),
            pltpu.VMEM((TOKENS, D), BF16),
            pltpu.VMEM((TOKENS, 128), F32),
            pltpu.VMEM((TOKENS, 128), F32),
            pltpu.VMEM((EXPERTS // GROUP, D, 2 * GROUP * FSLICE), BF16),
            pltpu.VMEM((D, GROUP * FSLICE), BF16),
            pltpu.VMEM((TOKENS, EXPERTS * 2 * FSLICE), BF16),
        ],
        compiler_params=pltpu.CompilerParams(vmem_limit_bytes=58 * 1024 * 1024),
        cost_estimate=COST,
    )(place, at, *b_parts, *g_parts, *w_parts)


def piece_to(at, r, v):
    return ((at[0] + r) % 4) * at[2] + v * at[3]


def grad_rows(at_ref, steps, source, dest):
    for i, r in enumerate(steps):
        for v in range(4):
            for k in range(4):
                rows = spot(PIECES * k + piece_to(at_ref, r, v), PROWS)
                dest[block(PIECES * i + 4 * v + k, PROWS), :] = source[rows, :]


def grad_blocks(outs, x_rows, g_rows, dudw, gz):
    first = nn(x_rows[...], dudw[...]).astype(BF16)
    second = (RESIDUAL_SCALE * nn(g_rows[...], gz[...])).astype(BF16)
    for i, out in enumerate(outs):
        for v in range(4):
            for k in range(4):
                rows = block(PIECES * i + 4 * v + k, PROWS)
                for n in range(GROUP):
                    out[v, k, n, :, 0 : 2 * FSLICE] = first[rows, block(n, 2 * FSLICE)]
                    out[v, k, n, :, 2 * FSLICE :] = second[rows, block(n, FSLICE)]


def near_grad_kernel(
    s_ref, at_ref, b0, b1, b2, b3, g0, g1, g2, g3, dudw, gz, t1, t3, xt, gt, x_rows, g_rows
):
    @pl.when(pl.program_id(0) == 0)
    def _():
        for j, (b_ref, g_ref) in enumerate(zip((b0, b1, b2, b3), (g0, g1, g2, g3))):
            for k in range(4):
                xt[block(k, QUART), block(j, ROWS)] = b_ref[:, block(k ^ j, QUART)].T
                gt[block(k, QUART), block(j, ROWS)] = g_ref[:, spot(s_ref[0] ^ k, QUART)].T
        grad_rows(at_ref, (1, 3), xt, x_rows)
        grad_rows(at_ref, (1, 3), gt, g_rows)

    grad_blocks((t1, t3), x_rows, g_rows, dudw, gz)


def rest_grad_kernel(s_ref, at_ref, xt, gt, dudw, gz, t0, t2, x_rows, g_rows):
    @pl.when(pl.program_id(0) == 0)
    def _():
        grad_rows(at_ref, (0, 2), xt, x_rows)
        grad_rows(at_ref, (0, 2), gt, g_rows)

    grad_blocks((t0, t2), x_rows, g_rows, dudw, gz)


def expert_grads(kernel, place, at, inputs, outputs, dudw, gz):
    block_out = pl.BlockSpec((4, 4, GROUP, PROWS, TILE), lambda e: (0, 0, e, 0, 0))
    return pl.pallas_call(
        kernel,
        name=kernel.__name__,
        grid=(EXPERTS // GROUP,),
        in_specs=[SMEM] * 2
        + [pl.BlockSpec(part.shape, fixed(2)) for part in inputs]
        + [
            pl.BlockSpec((TOKENS, 2 * GROUP * FSLICE), lambda e: (0, e)),
            pl.BlockSpec((TOKENS, GROUP * FSLICE), lambda e: (0, e)),
        ],
        out_specs=[block_out] * 2 + [pl.BlockSpec(out.shape, fixed(2)) for out in outputs],
        out_shape=[shaped((4, 4, EXPERTS, PROWS, TILE), BF16)] * 2 + outputs,
        scratch_shapes=[pltpu.VMEM((2 * QUART, TOKENS), BF16)] * 2,
        compiler_params=pltpu.CompilerParams(vmem_limit_bytes=56 * 1024 * 1024),
        cost_estimate=COST,
    )(place, at, *inputs, dudw, gz)


def mixture_kernel(at_ref, gz, w0, w1, f0, f1, f2, f3, keep_o, send_o, wide):
    for e in range(EXPERTS):
        at = slice(e * TILE + 2 * FSLICE, (e + 1) * TILE)
        parts = [part.at[:, :, :, at] for part in (f0, f1, f2, f3)]
        fill_weights(at_ref, w0[e], w1[e], parts, wide, block(e, FSLICE))
    for j in range(4):
        out = (keep_o, send_o)[j % 2]
        total = nt(gz[block(j, ROWS), :], wide[...]).astype(BF16)
        for k in range(4):
            out[j // 2, :, block(k ^ j, QUART)] = total[:, block(k, QUART)]


def mixture(at, gz, w_parts):
    down = [pl.BlockSpec((EXPERTS, QUART, FSLICE), lambda i: (0, 0, 2))] * 2 + [
        pl.BlockSpec((4, 2, PROWS, SHAREW), lambda i: (0, 0, 0, 0))
    ] * 4
    return pl.pallas_call(
        mixture_kernel,
        name="mixture",
        grid=(1,),
        in_specs=[SMEM, pl.BlockSpec((TOKENS, EXPERTS * FSLICE), fixed(2))] + down,
        out_specs=[pl.BlockSpec((2, ROWS, D), fixed(3))] * 2,
        out_shape=[shaped((2, ROWS, D), BF16)] * 2,
        scratch_shapes=[pltpu.VMEM((D, EXPERTS * FSLICE), BF16)],
        compiler_params=pltpu.CompilerParams(vmem_limit_bytes=56 * 1024 * 1024),
        cost_estimate=COST,
    )(at, gz, *w_parts)


def attend_back_kernel(
    s_ref, db_keep, db_come, db_far, hid, b, gates_ref, gp, gc, gain, rt, mixed, lse,
    q, kv0, kv1, kv2, kv3, o0, o1, o2, o3,
    hgrad_o, small_o, dwok_o, dwos_o, dq_o, kvk_o, kvs_o, dk_o, dv_o,
    bias, keys, values, dmix, grow
):
    place = s_ref[0]
    parts = (o0, o1, o2, o3)
    fill_bias(place, bias)
    fill_keys((kv0, kv1, kv2, kv3), keys, values)
    total = db_keep[0].astype(F32) + db_come[0].astype(F32) + db_far[...].astype(F32)
    tail = total[:, D:BOUT]
    dgate = (tail + pltpu.roll(tail, 112, axis=1))[:, 0:16]
    gates = gates_ref[:, 0:16]
    dlog = (gates * (dgate - jnp.sum(gates * dgate, axis=1, keepdims=True))).astype(BF16)
    dbt = total[:, 0:D] + nn(dlog, rt[...])
    small_o[...] = jnp.zeros_like(small_o)
    small_o[16:32, :] = tn(dlog, b[:, 0:D])
    hidden = hid[...]
    inverse = lax.rsqrt(jnp.mean(hidden * hidden, axis=1, keepdims=True) + EPSILON)
    n2 = hidden * inverse
    small_o[1:2, :] = jnp.sum(dbt * n2, axis=0, keepdims=True)
    scaled = dbt * gain[0:1, D : 2 * D]
    for k in range(4):
        there = spot(place ^ k, QUART)
        grow[0:HALF, block(k, QUART)] = gp[:, there]
        grow[HALF:ROWS, block(k, QUART)] = gc[:, there]
    hgrad = grow[...].astype(F32) + inverse * (
        scaled - n2 * jnp.mean(scaled * n2, axis=1, keepdims=True)
    )
    hgrad_o[...] = hgrad
    agrad = (RESIDUAL_SCALE * hgrad).astype(BF16)
    for g in range(4):
        total = nt(agrad[:, block(0, QUART)], parts[0][:, block(g, QUART)])
        for k in range(1, 4):
            total = total + nt(agrad[:, block(k, QUART)], parts[k][:, block(g, QUART)])
        dmix[:, block(g, QUART)] = total.astype(BF16)
    for g in range(4):
        rows = tn(mixed[:, block(g, QUART)], agrad).astype(BF16)
        for k in range(4):
            out = (dwok_o, dwos_o)[k % 2]
            out[k // 2, :, block(g, QUART)] = rows[:, block(k, QUART)]

    def one_pair(pair, carry):
        dks = []
        dvs = []
        lane = lax.broadcasted_iota(jnp.int32, (ROWS, 128), 1)
        for odd in range(2):
            head = 2 * pair + odd
            kk = doubled(keys, pair, odd)
            vv = doubled(values, pair, odd)
            qs = stacked(q, head, SCORE_SCALE)
            ds_rows = stacked(dmix, head, 1.0)
            probs = jnp.exp(nt(kk, qs) + bias[...] - lse[pl.ds(head, 1), :])
            product = dmix[:, spot(head, 128)].astype(F32) * mixed[:, spot(head, 128)].astype(F32)
            product = product.T
            inner = jnp.concatenate(
                [
                    jnp.sum(product[0:HDIM], axis=0, keepdims=True),
                    jnp.sum(product[HDIM:], axis=0, keepdims=True),
                ],
                axis=1,
            )
            sgrad = (probs * (nt(vv, ds_rows) - inner)).astype(BF16)
            dkr = nn(sgrad, qs)
            dvr = nn(probs.astype(BF16), ds_rows)
            dks.append(dkr + pltpu.roll(dkr, HDIM, axis=1))
            dvs.append(dvr + pltpu.roll(dvr, HDIM, axis=1))
            dqt = (SCORE_SCALE * tn(kk, sgrad)).T
            dq_o[:, spot(head, 128)] = jnp.where(lane < HDIM, dqt[0:ROWS], dqt[ROWS : 2 * ROWS])
        low = lax.broadcasted_iota(jnp.int32, (KEYS, 128), 1) < HDIM
        dk = jnp.where(low, dks[0], dks[1])
        dv = jnp.where(low, dvs[0], dvs[1])
        at = spot(pair, 128)
        at_v = spot(pair + 4, 128)
        for j in range(4):
            side = (kvk_o, kvs_o)[j % 2]
            side[j // 2, :, at] = dk[block(j, HALF)].astype(BF16)
            side[j // 2, :, at_v] = dv[block(j, HALF)].astype(BF16)
        dk_o[:, at] = dk[4 * HALF :]
        dv_o[:, at] = dv[4 * HALF :]
        return carry

    lax.fori_loop(0, PAIRS, one_pair, 0)


attend_back = whole_call(
    attend_back_kernel,
    "attend_back",
    [
        shaped((ROWS, D), F32),
        shaped((32, D), F32),
        shaped((2, QUART, D), BF16),
        shaped((2, QUART, D), BF16),
        shaped((ROWS, D), F32),
        shaped((2, HALF, D), BF16),
        shaped((2, HALF, D), BF16),
        shaped((HALF, KVW), F32),
        shaped((HALF, KVW), F32),
    ],
    scratch=[
        pltpu.VMEM((KEYS, 512), F32),
        pltpu.VMEM((KEYS, KVW), BF16),
        pltpu.VMEM((KEYS, KVW), BF16),
        pltpu.VMEM((ROWS, D), BF16),
        pltpu.VMEM((ROWS, D), BF16),
    ],
    limit=36,
    parts={n: ((1, ROWS, BOUT), (0, 0, 0)) for n in (1, 2)},
)


def turn_back(values, cosine, sine):
    return values * cosine - swapped(values) * sine


def query_back_kernel(
    s_ref, dq, nq, inv, gain, cos, sin, ar, a0, a1, a2, a3, dwqk_o, dwqs_o, da_o, qg_o, grads
):
    cosine = here(s_ref[0], cos)
    sine = here(s_ref[0], sin)
    inv_q = inv[:, 0:1]
    dot = jnp.zeros((ROWS, 1), F32)
    for g in range(8):
        at = block(g, 128)
        back = turn_back(dq[:, at], cosine, sine)
        near = nq[:, at]
        qg_o[0:1, at] = jnp.sum(back * near, axis=0, keepdims=True)
        scaled = back * gain[0:1, 2 * D + g * 128 : 2 * D + (g + 1) * 128]
        dot = dot + jnp.sum(scaled * near, axis=1, keepdims=True)
        grads[:, at] = scaled
    pre = (inv_q * (grads[...] - nq[...] * (dot / D))).astype(BF16)
    for k, part in enumerate((a0, a1, a2, a3)):
        da_o[:, block(k, QUART)] = nt(pre, part[...])
        out = (dwqk_o, dwqs_o)[k % 2]
        out[k // 2] = tn(ar[:, block(k, QUART)], pre).astype(BF16)


query_back = whole_call(
    query_back_kernel,
    "query_back",
    [
        shaped((2, QUART, D), BF16),
        shaped((2, QUART, D), BF16),
        shaped((ROWS, D), F32),
        shaped((8, D), F32),
    ],
    scratch=[pltpu.VMEM((ROWS, D), F32)],
    parts={n: ((QUART, D), (0, 0)) for n in range(8, 12)},
)


def key_back_kernel(
    s_ref, kv_keep, kv_come, dk, dv, nk, inv, gain, cos, sin, ar, xr, hgrad, da_q, qg, small,
    a0, a1, a2, a3, keep_o, send_o, xp_o, xc_o, grads, both, da, cols
):
    place = s_ref[0]
    cosine = here(s_ref[0], cos)
    sine = here(s_ref[0], sin)
    inv_k = inv[:, 1:2]
    grads[0:HALF, :] = kv_keep[:, 0:KVW].astype(F32) + kv_come[:, 0:KVW].astype(F32)
    grads[HALF:ROWS, :] = dk[...]
    both[0:HALF, KVW:D] = (kv_keep[:, KVW:D].astype(F32) + kv_come[:, KVW:D].astype(F32)).astype(BF16)
    both[HALF:ROWS, KVW:D] = dv[...].astype(BF16)
    cols[...] = jnp.zeros_like(cols)
    dot = jnp.zeros((ROWS, 1), F32)
    for g in range(4):
        at = block(g, 128)
        back = turn_back(grads[:, at], cosine, sine)
        near = nk[:, at]
        kgrad = jnp.sum(back * near, axis=0, keepdims=True)
        cols[3:4, spot(place ^ g, QUART)] = jnp.concatenate([kgrad, jnp.zeros_like(kgrad)], axis=1)
        scaled = back * gain[0:1, 3 * D + g * 128 : 3 * D + (g + 1) * 128]
        dot = dot + jnp.sum(scaled * near, axis=1, keepdims=True)
        grads[:, at] = scaled
    both[:, 0:KVW] = (inv_k * (grads[...] - nk[...] * (dot / KVW))).astype(BF16)
    pre = both[...]
    for k, part in enumerate((a0, a1, a2, a3)):
        da[:, block(k, QUART)] = da_q[:, block(k, QUART)] + nt(pre, part[...])
        out = (keep_o, send_o)[k % 2]
        out[k // 2, :, 0:D] = tn(ar[:, block(k, QUART)], pre).astype(BF16)
    x = xr[...].astype(F32)
    inverse = inv[:, 2:3]
    n1 = x * inverse
    grad = da[...]
    cols[0:1, :] = jnp.sum(grad * n1, axis=0, keepdims=True)
    cols[1:2, :] = small[1:2, :]
    cols[16:32, :] = small[16:32, :]
    for k in range(4):
        cols[2:3, block(k, QUART)] = qg[0:1, spot(place ^ k, QUART)]
    for k in range(4):
        out = (keep_o, send_o)[k % 2]
        out[k // 2, :, D:BOUT] = cols[:, block(k, QUART)].T.astype(BF16)
    scaled = grad * gain[0:1, 0:D]
    result = hgrad[...] + inverse * (scaled - n1 * jnp.mean(scaled * n1, axis=1, keepdims=True))
    low = result.astype(BF16)
    for k in range(4):
        there = spot(place ^ k, QUART)
        xp_o[:, there] = low[0:HALF, block(k, QUART)]
        xc_o[:, there] = low[HALF:ROWS, block(k, QUART)]


key_back = whole_call(
    key_back_kernel,
    "key_back",
    [
        shaped((2, QUART, BOUT), BF16),
        shaped((2, QUART, BOUT), BF16),
        shaped((HALF, D), BF16),
        shaped((HALF, D), BF16),
    ],
    scratch=[
        pltpu.VMEM((ROWS, KVW), F32),
        pltpu.VMEM((ROWS, D), BF16),
        pltpu.VMEM((ROWS, D), F32),
        pltpu.VMEM((128, D), F32),
    ],
    parts={n: ((QUART, D), (1, 0)) for n in range(16, 20)},
)


def finish_kernel(s_ref, hid, keep, come, xp_o, xc_o):
    total = hid[...] + RESIDUAL_SCALE * (keep[...].astype(F32) + come[...].astype(F32))
    low = total.astype(BF16)
    for k in range(4):
        there = spot(s_ref[0] ^ k, QUART)
        xp_o[:, there] = low[0:HALF, block(k, QUART)]
        xc_o[:, there] = low[HALF:ROWS, block(k, QUART)]


finish = whole_call(
    finish_kernel,
    "finish",
    [shaped((HALF, D), BF16), shaped((HALF, D), BF16)],
)


def pair_kernel(at_ref, qk, qc, lk, lc, ok, oc, t0, t1, t2, t3):
    for r, out in enumerate((t0, t1, t2, t3)):
        for v in range(4):
            rows = spot(piece_to(at_ref, r, v), PROWS)
            last = (lk[0, rows, :].astype(F32) + lc[0, rows, :].astype(F32)).astype(BF16)
            out[v, 0, :, 0:D] = (qk[0, rows, :].astype(F32) + qc[0, rows, :].astype(F32)).astype(BF16)
            out[v, 0, :, D:QKVW] = last[:, 0:D]
            out[v, 0, :, QKVW : QKVW + D] = (
                ok[0, rows, :].astype(F32) + oc[0, rows, :].astype(F32)
            ).astype(BF16)
            out[v, 0, :, QKVW + D :] = last[:, D:]


def pair(at, *parts):
    return pl.pallas_call(
        pair_kernel,
        name="pair",
        grid=(2,),
        in_specs=[SMEM]
        + [pl.BlockSpec((1, QUART, part.shape[2]), lambda k: (k, 0, 0)) for part in parts],
        out_specs=[pl.BlockSpec((4, 1, PROWS, ATTW), lambda k: (0, k, 0, 0))] * 4,
        out_shape=[shaped((4, 2, PROWS, ATTW), BF16)] * 4,
        compiler_params=pltpu.CompilerParams(vmem_limit_bytes=24 * 1024 * 1024),
        cost_estimate=COST,
    )(at, *parts)


def fold_kernel(at_ref, i0, i1, i2, i3, o0, o1, o2, o3):
    for r, out in enumerate((o0, o1, o2, o3)):
        there = (at_ref[1] + r) % 4
        total = i0[there].astype(F32) + i1[there].astype(F32)
        out[...] = (total + i2[there].astype(F32) + i3[there].astype(F32)).astype(BF16)


def fold(at, parts, rows, steps):
    shape = parts[0].shape
    width = shape[-1]
    flat = [part.reshape(4, rows, width) for part in parts]
    height = rows // steps
    outs = pl.pallas_call(
        fold_kernel,
        name="fold",
        grid=(steps,),
        in_specs=[SMEM] + [pl.BlockSpec((4, height, width), lambda i: (0, i, 0))] * 4,
        out_specs=[pl.BlockSpec((height, width), lambda i: (i, 0))] * 4,
        out_shape=[shaped((rows, width), BF16)] * 4,
        compiler_params=pltpu.CompilerParams(vmem_limit_bytes=24 * 1024 * 1024),
        cost_estimate=COST,
    )(at, *flat)
    return [out.reshape(shape[1:]) for out in outs]


def unpack_kernel(s_ref, at_ref, p0, p1, p2, p3, p4, gate_o, up_o, down_o, tile):
    for r, part, low in ((0, p0, 0), (1, p1, 0), (2, p2, 0), (2, p3, 2), (3, p4, 0)):
        for n in range(part.shape[0]):
            rows = spot(piece_at(at_ref, r, low + n), PROWS)
            for k in range(4):
                there = spot(s_ref[0] ^ k, FSLICE)
                gate_o[0, rows, there] = part[n, k, 0, :, 0:FSLICE].astype(F32)
                up_o[0, rows, there] = part[n, k, 0, :, FSLICE : 2 * FSLICE].astype(F32)
                tile[rows, block(k, FSLICE)] = part[n, k, 0, :, 2 * FSLICE :].astype(F32)
    for k in range(4):
        down_o[0, spot(s_ref[0] ^ k, FSLICE), :] = tile[:, block(k, FSLICE)].T


def unpack_experts(place, at, parts):
    specs = [
        pl.BlockSpec((part.shape[0], 4, 1, PROWS, TILE), lambda e: (0, 0, e, 0, 0))
        for part in parts
    ]
    return pl.pallas_call(
        unpack_kernel,
        name="unpack_experts",
        grid=(EXPERTS,),
        in_specs=[SMEM] * 2 + specs,
        out_specs=[
            pl.BlockSpec((1, QUART, 512), lambda e: (e, 0, 0)),
            pl.BlockSpec((1, QUART, 512), lambda e: (e, 0, 0)),
            pl.BlockSpec((1, 512, QUART), lambda e: (e, 0, 0)),
        ],
        out_shape=[
            shaped((EXPERTS, QUART, 512), F32),
            shaped((EXPERTS, QUART, 512), F32),
            shaped((EXPERTS, 512, QUART), F32),
        ],
        scratch_shapes=[pltpu.VMEM((QUART, 512), F32)],
        compiler_params=pltpu.CompilerParams(vmem_limit_bytes=24 * 1024 * 1024),
        cost_estimate=COST,
    )(place, at, *parts)


def unpack_attention_kernel(
    at_ref, p0, p1, p2, p3, wq_o, wk_o, wv_o, wo_o, attn_o, ffn_o, qg_o, kg_o, router_o, wide
):
    for r, part in enumerate((p0, p1, p2, p3)):
        for n in range(4):
            wide[spot(piece_at(at_ref, r, n), PROWS), :] = part[n]
    wq_o[...] = wide[:, 0:D].astype(F32)
    wk_o[...] = wide[:, D : D + KVW].astype(F32)
    wv_o[...] = wide[:, D + KVW : QKVW].astype(F32)
    for g in range(4):
        wo_o[block(g, QUART), :] = wide[:, QKVW + g * QUART : QKVW + (g + 1) * QUART].astype(F32)
    tail = wide[:, QKVW + D :].astype(F32)
    rows = tail.T
    attn_o[...] = rows[0:1]
    ffn_o[...] = rows[1:2]
    qg_o[...] = rows[2:3]
    kg_o[...] = rows[3:4, 0:HALF]
    router_o[...] = rows[16 : 16 + EXPERTS]


unpack_attention = whole_call(
    unpack_attention_kernel,
    "unpack_attention",
    [
        shaped((QUART, D), F32),
        shaped((QUART, KVW), F32),
        shaped((QUART, KVW), F32),
        shaped((D, QUART), F32),
        shaped((1, QUART), F32),
        shaped((1, QUART), F32),
        shaped((1, QUART), F32),
        shaped((1, HALF), F32),
        shaped((EXPERTS, QUART), F32),
    ],
    scratch=[pltpu.VMEM((QUART, ATTW), BF16)],
)


def body(
    prompt_x, cont_x, prompt_cot, cont_cot, prompt_routes, cont_routes,
    attn_gain, w_query, w_key, w_value, query_gain, key_gain,
    w_out, ffn_gain, w_router, w_gate, w_up, w_down,
):
    def moved(value, axes, change):
        sizes = [lax.axis_size(a) for a in axes]
        pairs = []
        count = 1
        for size in sizes:
            count *= size
        for index in range(count):
            rest, coords = index, []
            for size in reversed(sizes):
                coords.append(rest % size)
                rest //= size
            to = change(*reversed(coords))
            target = 0
            for size, coord in zip(sizes, to):
                target = target * size + coord
            pairs.append((index, target))
        return lax.ppermute(value, axes, pairs)

    def sib(value):
        return moved(value, ("c",), lambda c: (1 - c,))

    def far(value):
        return moved(value, ("xh",), lambda h: (1 - h,))

    def far_sib(value):
        return moved(value, ("xh", "c"), lambda h, c: (1 - h, 1 - c))

    def cross(value):
        return moved(value, ("xl", "xh"), lambda low, high: (1 - low, 1 - high))

    def cross_sib(value):
        return moved(value, ("xl", "xh", "c"), lambda low, high, c: (1 - low, 1 - high, 1 - c))

    def near(value):
        return moved(value, ("xl",), lambda low: (1 - low,))

    def along(value, by, core_of_z):
        def change(at_z, at_y, c):
            if c == core_of_z:
                return ((at_z + by) % 4, at_y, c)
            return (at_z, (at_y + by) % 4, c)

        return moved(value, ("z", "y", "c"), change)

    def first(value, by):
        return along(value, by, 1)

    def second(value, by):
        return along(value, by, 0)

    def spread(value, way):
        return [value] + [way(value, by) for by in (1, 2, 3)]

    def added(parts):
        total = parts[0].astype(F32)
        for part in parts[1:]:
            total = total + part.astype(F32)
        return total.astype(BF16)

    after = lax.optimization_barrier

    z = lax.axis_index("z").astype(jnp.int32)
    y = lax.axis_index("y").astype(jnp.int32)
    core = lax.axis_index("c").astype(jnp.int32)
    low_core = core == 0
    at = jnp.stack(
        [
            jnp.where(low_core, y, z),
            jnp.where(low_core, z, y),
            jnp.where(low_core, 1, 4),
            jnp.where(low_core, 4, 1),
        ]
    )
    position = lax.axis_index(("xh", "c")).astype(jnp.int32)
    place = position[None]
    piece = 4 * z + y
    cont_in = cont_x.reshape(HALF, D)
    cont_up = cont_cot.reshape(HALF, D)

    def held(value, *others):
        return after((value, others))[0]

    own_in = prepare(
        place, w_query, w_key, w_value, attn_gain[None], ffn_gain[None], query_gain[None],
        key_gain[None], w_router.T,
    )
    in_two = cross(own_in)
    place_in, own_in = after((place, own_in))
    share_two, share_three = share_experts(
        jnp.concatenate([piece[None], place_in]), w_gate, w_up, w_down
    )
    place_in, share_two, share_three = after((place, share_two, share_three))
    share_two = cross(share_two)
    share_three = cross_sib(share_three)
    own_out = prepare_out(place_in, w_out)
    packed = pack_experts(place_in, w_gate, w_up, w_down)
    out_sib = sib(own_out)
    in_two, packed, own_in_sib, own_out, out_sib, share_two, share_three = after(
        (in_two, packed, sib(own_in), own_out, out_sib, share_two, share_three)
    )
    in_parts = (own_in, own_in_sib, in_two, sib(in_two))

    cosine, sine = (jnp.asarray(table) for table in angle_tables())

    kv, kv_own, nk, inv, xr, ar, gain, rt = project_keys(
        place, prompt_x, cont_in, *in_parts, cosine, sine
    )
    kv_two = far(kv_own)
    upstream = held(jnp.concatenate([prompt_cot, cont_up], axis=0), nk)
    up_two = cross(upstream)
    shares = held(jnp.stack([share_two, share_three]), nk)
    out_two = cross(own_out)
    row = jnp.stack(held(spread(shares, second), kv_two))
    ar, row, out_two = after((ar, row, out_two))
    q, nq, inv_q = project_query(place, ar, gain, *in_parts, cosine, sine)
    row = held(row, q)
    row_one = first(row, 1)
    row_three = first(row, 3)
    packed = held(packed, q)
    kv_parts = (kv, sib(kv_own), kv_two, sib(kv_two))
    mixed, lse = attend(place, q, *kv_parts)
    row_two = first(held(row, mixed), 2)
    out_parts = (own_out, out_sib, out_two, sib(out_two))
    hidden, b, gates = route(
        place, mixed, *out_parts, xr, gain, rt, prompt_routes.T, cont_routes.reshape(HALF, 8).T
    )
    up_sib = sib(upstream)
    packed_sib = sib(packed[1])
    b, up_two, up_sib, packed_sib, row_one, row_three = after(
        (b, up_two, up_sib, packed_sib, row_one, row_three)
    )
    w_parts = (packed[0], packed_sib, row, row_one, row_two, row_three)
    b_two, up_sib_two = after((cross(b), sib(up_two)))
    up_parts = (upstream, up_sib, up_two, up_sib_two)
    b_parts = (b, sib(b), b_two, sib(b_two))
    dudw, gz, db_keep, db_send = experts(place, at, b_parts, up_parts, w_parts)

    db_come = sib(db_send)
    db_sum = added([db_keep[1], db_come[1]])
    db_sum, dudw = after((db_sum, dudw))
    db_far = cross(db_sum)
    turned = [shaped((D, TOKENS), BF16)] * 2
    grad_one, grad_three, xt, gt = expert_grads(
        near_grad_kernel, place, at, [*b_parts, *up_parts], turned, dudw, gz
    )
    place_in, xt, db_far = after((place, xt, db_far))
    grad_own, grad_next = expert_grads(rest_grad_kernel, place_in, at, [xt, gt], [], dudw, gz)
    grad_one = first(grad_one, 1)
    grad_three = first(grad_three, 3)
    grad_two = first(grad_next, 2)
    later = held(place, grad_own)

    hgrad, small, dwo_keep, dwo_send, dq, kv_keep, kv_send, dk, dv = attend_back(
        later, db_keep, db_come, db_far, hidden, b, gates, prompt_cot, cont_up, gain, rt, mixed, lse,
        q, *kv_parts, *out_parts,
    )

    kv_come = sib(kv_send)
    kv_sum = added([kv_keep, kv_come])
    kv_far = far(kv_sum[1])
    dq, kv_sum = after((dq, kv_sum))
    dwq_keep, dwq_send, da_q, qg = query_back(
        place, dq, nq, inv_q, gain, cosine, sine, ar, *in_parts
    )
    grad_one, grad_two, grad_three, da_q = after((grad_one, grad_two, grad_three, da_q))
    grad_rest = fold(at, [grad_own, grad_one, grad_two, grad_three], 4 * EXPERTS * PROWS, 2)
    da_q, grad_rest = after((da_q, grad_rest))
    last_keep, last_send, prompt_grad, cont_grad = key_back(
        place, kv_sum[0], kv_far, dk, dv, nk, inv, gain, cosine, sine, ar, xr, hgrad, da_q, qg,
        small, *in_parts,
    )

    paired = pair(
        held(at, grad_rest), dwq_keep, sib(dwq_send), last_keep, sib(last_send), dwo_keep, sib(dwo_send)
    )
    grad_rest = [grad_rest[0]] + [second(grad_rest[by], by) for by in (1, 2, 3)]
    summed = added(held(grad_rest, paired[0]))
    paired = [paired[0]] + [first(paired[by], by) for by in (1, 2, 3)]

    turned_parts = [summed[0], sib(summed[1]), far(summed[2]), far_sib(summed[3])]
    paired[1], paired[3], turned_parts = after((paired[1], paired[3], turned_parts))
    turned_parts = jnp.stack(turned_parts, axis=0)
    near_parts = near(turned_parts)
    mix_keep, mix_send = mixture(at, held(gz, turned_parts), w_parts)
    own_sum = added([turned_parts, held(near_parts, mix_keep)])
    steps = jnp.stack(spread(own_sum, second))
    paired = held(fold(at, held(paired, turned_parts), 2 * PROWS, 1), steps)
    steps_one = first(steps, 1)
    steps_three = first(steps, 3)

    mix_sum = added([mix_keep, sib(mix_send)])
    mix_far = cross(mix_sum[1])
    prompt_out, cont_out = finish(place, hidden, mix_sum[0], mix_far)

    part = added([paired[0]] + [second(paired[by], by) for by in (1, 2, 3)])
    part = added([part[0], near(part[0]), far(part[1]), cross(part[1])])
    part_steps = jnp.stack(spread(part, second))
    steps_one, steps_three, part_steps = after((steps_one, steps_three, part_steps))
    steps_two = (first(steps_one[0:2], 1), first(steps_three[2:4], 3))
    full = spread(part_steps, first)
    gate_grad, up_grad, down_grad = unpack_experts(
        place, at, (steps, steps_one, *steps_two, steps_three)
    )
    wq_grad, wk_grad, wv_grad, wo_grad, attn_grad, ffn_grad, qg_grad, kg_grad, router_grad = (
        unpack_attention(at, *held(full, gate_grad))
    )

    return (
        prompt_out,
        cont_out.reshape(1, HALF, D),
        prompt_grad,
        cont_grad.reshape(1, HALF, D),
        attn_grad[0],
        wq_grad,
        wk_grad,
        wv_grad,
        qg_grad[0],
        kg_grad[0],
        wo_grad,
        ffn_grad[0],
        router_grad.T,
        gate_grad,
        up_grad,
        down_grad,
    )


def solution(mesh):
    fine = Mesh(mesh.devices.reshape(2, 4, 4, 2, 2), AXES)
    shard = ("xh", "c")
    tokens = P(AXES, None)
    series = P(AXES, None, None)
    weights = (
        P(shard),
        P(shard, None),
        P(shard, None),
        P(shard, None),
        P(shard),
        P(shard),
        P(None, shard),
        P(shard),
        P(shard, None),
        P(None, shard, None),
        P(None, shard, None),
        P(None, None, shard),
    )
    return jax.shard_map(
        body,
        mesh=fine,
        in_specs=(tokens, series, tokens, series, tokens, series, *weights),
        out_specs=(tokens, series, tokens, series, *weights),
        check_vma=False,
    )
```

```python
import jax
import jax.numpy as jnp
import numpy as np
from jax import lax
from jax.experimental import pallas as pl
from jax.experimental.pallas import tpu as pltpu
from jax.sharding import Mesh, PartitionSpec as P

EPSILON = 1e-06
SCORE_SCALE = 0.25
RESIDUAL_SCALE = 0.22
ROTARY_BASE = 10000.0
MASKED = -1e30

D = 1024
HDIM = 64
PAIRS = 4
KVW = 512
QKVW = 2048
ROWS = 256
HALF = 128
QUART = 256
EXPERTS = 9
FSLICE = 128
TILE = 3 * FSLICE
TOKENS = 4 * ROWS
KEYS = 5 * HALF
BOUT = D + 128
ATTW = QKVW + D + 128
PIECES = 16
PROWS = QUART // PIECES
SHAREW = EXPERTS * TILE
GROUP = 3

F32 = jnp.float32
BF16 = jnp.bfloat16


def angle_tables():
    frequency = np.float32(ROTARY_BASE) ** (-np.arange(0, HDIM, 2, dtype=np.float32) / HDIM)
    turned = np.arange(KEYS, dtype=np.float32)[:, None] * frequency.astype(np.float32)[None, :]
    cosine = np.tile(np.cos(turned), (1, 4)).astype(np.float32)
    sine = np.sin(turned)
    sine = np.concatenate([-sine, sine, -sine, sine], axis=1).astype(np.float32)
    return cosine, sine


AXES = ("xl", "z", "y", "xh", "c")


def nn(left, right):
    return lax.dot_general(left, right, (((1,), (0,)), ((), ())), preferred_element_type=F32)


def nt(left, right):
    return lax.dot_general(left, right, (((1,), (1,)), ((), ())), preferred_element_type=F32)


def tn(left, right):
    return lax.dot_general(left, right, (((0,), (0,)), ((), ())), preferred_element_type=F32)


def spot(index, width):
    return pl.ds(pl.multiple_of(index * width, width), width)


def block(index, width):
    return slice(index * width, (index + 1) * width)


SMEM = pl.BlockSpec(memory_space=pltpu.SMEM)
VMEM = pl.BlockSpec(memory_space=pltpu.VMEM)


COST = pl.CostEstimate(flops=1_000_000, bytes_accessed=1_000_000, transcendentals=0)


def whole_call(kernel, name, out_shape, scratch=(), limit=24, parts=None):
    def whole(shape, index=None):
        index = index or (0,) * len(shape)
        return pl.BlockSpec(shape, lambda i: index)

    def call(*operands):
        specs = [
            whole(*parts[n]) if parts and n in parts else whole(operand.shape)
            for n, operand in enumerate(operands)
        ]
        return pl.pallas_call(
            kernel,
            name=name,
            out_shape=out_shape,
            grid=(1,),
            in_specs=[SMEM] + specs[1:],
            out_specs=jax.tree.map(lambda out: whole(out.shape), out_shape),
            scratch_shapes=list(scratch),
            compiler_params=pltpu.CompilerParams(vmem_limit_bytes=limit * 1024 * 1024),
            cost_estimate=COST,
        )(*operands)

    return call


def shaped(shape, dtype):
    return jax.ShapeDtypeStruct(shape, dtype)


def pack_kernel(s_ref, gate, up, down, own, other):
    turned = down[0].T
    for k, out in ((0, own), (1, other)):
        low = (s_ref[0] % 2) == k
        for n, part in enumerate((gate[0], up[0], turned)):
            half = jnp.where(low, part[:, 0:FSLICE], part[:, FSLICE:])
            out[0, :, block(n, FSLICE)] = half.astype(BF16)


def pack_experts(place, w_gate, w_up, w_down):
    wide = pl.BlockSpec((1, QUART, 2 * FSLICE), lambda e, s: (e, 0, s[0] // 2))
    out = pl.BlockSpec((1, QUART, TILE), lambda e, s: (e, 0, 0))
    return pl.pallas_call(
        pack_kernel,
        name="pack_experts",
        grid_spec=pltpu.PrefetchScalarGridSpec(
            num_scalar_prefetch=1,
            grid=(EXPERTS,),
            in_specs=[
                wide,
                wide,
                pl.BlockSpec((1, 2 * FSLICE, QUART), lambda e, s: (e, s[0] // 2, 0)),
            ],
            out_specs=[out, out],
        ),
        out_shape=[shaped((EXPERTS, QUART, TILE), BF16)] * 2,
        compiler_params=pltpu.CompilerParams(vmem_limit_bytes=56 * 1024 * 1024),
        cost_estimate=COST,
    )(place, w_gate, w_up, w_down)


def share_kernel(at_ref, gate, up, down, two, three, turned):
    for k, dest in ((2, two), (3, three)):
        there = spot(at_ref[1] ^ k, FSLICE)
        for e in range(EXPERTS):
            at = e * TILE
            dest[:, at : at + FSLICE] = gate[e, :, there].astype(BF16)
            dest[:, at + FSLICE : at + 2 * FSLICE] = up[e, :, there].astype(BF16)
            turned[...] = down[e, there, :].T
            dest[:, at + 2 * FSLICE : at + TILE] = turned[
                spot(at_ref[0] % 8, PROWS), :
            ].astype(BF16)


def share_experts(at, w_gate, w_up, w_down):
    rows = pl.BlockSpec((EXPERTS, PROWS, 512), lambda i, at: (0, at[0], 0))
    dest = pl.BlockSpec((PROWS, SHAREW), lambda i, at: (0, 0))
    return pl.pallas_call(
        share_kernel,
        name="share_experts",
        grid_spec=pltpu.PrefetchScalarGridSpec(
            num_scalar_prefetch=1,
            grid=(1,),
            in_specs=[
                rows,
                rows,
                pl.BlockSpec((EXPERTS, 512, 128), lambda i, at: (0, 0, at[0] // 8)),
            ],
            out_specs=[dest, dest],
            scratch_shapes=[pltpu.VMEM((128, FSLICE), F32)],
        ),
        out_shape=[shaped((PROWS, SHAREW), BF16)] * 2,
        compiler_params=pltpu.CompilerParams(vmem_limit_bytes=56 * 1024 * 1024),
        cost_estimate=COST,
    )(at, w_gate, w_up, w_down)


def prepare_kernel(s_ref, wq, wk, wv, attn, ffn, query, key, router, kv_o, line):
    kv_o[0:QUART, :] = wq[...].astype(BF16)
    kv_o[QUART : 2 * QUART, 0:KVW] = wk[...].astype(BF16)
    kv_o[QUART : 2 * QUART, KVW:D] = wv[...].astype(BF16)
    line[...] = jnp.zeros_like(line)
    line[0:1, 0:256] = attn[...]
    line[0:1, 256:512] = ffn[...]
    line[0:1, 512:768] = query[...]
    line[0:1, 768:896] = key[...]
    kv_o[2 * QUART : 2 * QUART + 16, :] = line[...].astype(BF16)
    line[...] = jnp.zeros_like(line)
    line[0:EXPERTS, 0:QUART] = router[...]
    kv_o[2 * QUART + 16 :, :] = line[...].astype(BF16)


prepare = whole_call(
    prepare_kernel,
    "prepare",
    shaped((2 * QUART + 32, D), BF16),
    scratch=[pltpu.VMEM((16, D), F32)],
    limit=56,
)


def swapped(values):
    lane = lax.broadcasted_iota(jnp.int32, values.shape, 1)
    return jnp.where(
        lane % HDIM < HDIM // 2, pltpu.roll(values, 96, axis=1), pltpu.roll(values, 32, axis=1)
    )


def here(place, table):
    return jnp.concatenate([table[spot(place, HALF), :], table[4 * HALF :, :]], axis=0)


def project_keys_kernel(
    s_ref, xp, xc, a0, a1, a2, a3, cos, sin, kv_o, kvp_o, nk_o, inv_o, xr_o, ar_o, gain_o, rt_o, acc
):
    parts = (a0, a1, a2, a3)
    for k in range(4):
        there = s_ref[0] ^ k
        xr_o[0:HALF, block(k, QUART)] = xp[:, spot(there, QUART)]
        xr_o[HALF:ROWS, block(k, QUART)] = xc[:, spot(there, QUART)]
        small = parts[k][2 * QUART : 2 * QUART + 16, :].astype(F32)[0:1]
        gain_o[0:1, block(k, QUART)] = small[:, 0:256]
        gain_o[0:1, slice(D + k * QUART, D + (k + 1) * QUART)] = small[:, 256:512]
        gain_o[0:1, pl.ds(pl.multiple_of(2 * D + there * QUART, 128), QUART)] = small[:, 512:768]
        gain_o[0:1, pl.ds(pl.multiple_of(3 * D + there * HALF, 128), HALF)] = small[:, 768:896]
        rt_o[:, block(k, QUART)] = parts[k][2 * QUART + 16 :, 0:QUART]
    x = xr_o[...].astype(F32)
    inverse = lax.rsqrt(jnp.mean(x * x, axis=1, keepdims=True) + EPSILON)
    ar_o[...] = (x * inverse * gain_o[0:1, 0:D]).astype(BF16)
    total = nn(ar_o[:, block(0, QUART)], parts[0][QUART : 2 * QUART, :])
    for k in range(1, 4):
        total = total + nn(ar_o[:, block(k, QUART)], parts[k][QUART : 2 * QUART, :])
    acc[...] = total
    kp = acc[:, 0:KVW]
    inv_k = lax.rsqrt(jnp.mean(kp * kp, axis=1, keepdims=True) + EPSILON)
    nk_o[...] = kp * inv_k
    lane = lax.broadcasted_iota(jnp.int32, (ROWS, 128), 1)
    inv_o[...] = jnp.where(lane == 1, inv_k, inverse)
    kv_o[:, KVW:D] = acc[:, KVW:D].astype(BF16)
    cosine = here(s_ref[0], cos)
    sine = here(s_ref[0], sin)
    for g in range(4):
        at = block(g, 128)
        u = nk_o[:, at] * gain_o[0:1, 3 * D + g * 128 : 3 * D + (g + 1) * 128]
        kv_o[:, at] = (u * cosine + swapped(u) * sine).astype(BF16)
    kvp_o[...] = kv_o[0:HALF, :]


project_keys = whole_call(
    project_keys_kernel,
    "project_keys",
    [
        shaped((ROWS, D), BF16),
        shaped((HALF, D), BF16),
        shaped((ROWS, KVW), F32),
        shaped((ROWS, 128), F32),
        shaped((ROWS, D), BF16),
        shaped((ROWS, D), BF16),
        shaped((8, 3 * D + KVW), F32),
        shaped((16, D), BF16),
    ],
    scratch=[pltpu.VMEM((ROWS, D), F32)],
    limit=56,
)


def prepare_out_kernel(s_ref, wo, out):
    for g in range(4):
        out[:, block(g, QUART)] = wo[block(g, QUART), :].astype(BF16)


prepare_out = whole_call(
    prepare_out_kernel, "prepare_out", shaped((QUART, D), BF16), limit=56
)


def project_query_kernel(s_ref, ar, gain, a0, a1, a2, a3, cos, sin, q_o, nq_o, inv_o):
    total = nn(ar[:, block(0, QUART)], a0[...])
    for k, part in ((1, a1), (2, a2), (3, a3)):
        total = total + nn(ar[:, block(k, QUART)], part[...])
    nq_o[...] = total
    inv_q = lax.rsqrt(jnp.mean(total * total, axis=1, keepdims=True) + EPSILON)
    inv_o[...] = jnp.broadcast_to(inv_q, (ROWS, 128))
    cosine = here(s_ref[0], cos)
    sine = here(s_ref[0], sin)
    for g in range(8):
        at = block(g, 128)
        near = nq_o[:, at] * inv_q
        nq_o[:, at] = near
        u = near * gain[0:1, 2 * D + g * 128 : 2 * D + (g + 1) * 128]
        q_o[:, at] = (u * cosine + swapped(u) * sine).astype(BF16)


project_query = whole_call(
    project_query_kernel,
    "project_query",
    [shaped((ROWS, D), BF16), shaped((ROWS, D), F32), shaped((ROWS, 128), F32)],
    parts={n: ((QUART, D), (0, 0)) for n in range(3, 7)},
    limit=56,
)


def fill_bias(place, bias):
    row = lax.broadcasted_iota(jnp.int32, (HALF, 512), 0)
    lane = lax.broadcasted_iota(jnp.int32, (HALF, 512), 1)
    causal = jnp.where(row <= lane % HALF, 0.0, MASKED)
    is_prompt = lane % ROWS < HALF
    bias[0:HALF, :] = jnp.where(is_prompt, causal, 0.0)
    for k in range(1, 4):
        level = jnp.where((place ^ k) < place, 0.0, MASKED)
        bias[block(k, HALF), :] = jnp.where(is_prompt, level, 0.0)
    bias[4 * HALF :, :] = jnp.where(is_prompt, MASKED, causal)


def fill_keys(refs, keys, values):
    for j in range(4):
        keys[block(j, HALF), :] = refs[j][0:HALF, 0:KVW]
        values[block(j, HALF), :] = refs[j][0:HALF, KVW:D]
    keys[4 * HALF :, :] = refs[0][HALF:ROWS, 0:KVW]
    values[4 * HALF :, :] = refs[0][HALF:ROWS, KVW:D]


def doubled(ref, pair, odd):
    both = ref[:, spot(pair, 128)]
    other = pltpu.roll(both.astype(F32), HDIM, axis=1).astype(BF16)
    lane = lax.broadcasted_iota(jnp.int32, both.shape, 1)
    return jnp.where((lane < HDIM) == (odd == 0), both, other)


def stacked(ref, head, scale):
    rows = ref[:, spot(head, 128)]
    lane = lax.broadcasted_iota(jnp.int32, rows.shape, 1)
    rows = rows * jnp.asarray(scale, rows.dtype)
    none = jnp.zeros_like(rows)
    return jnp.concatenate(
        [jnp.where(lane < HDIM, rows, none), jnp.where(lane < HDIM, none, rows)], axis=0
    )


def attend_kernel(s_ref, q, kv0, kv1, kv2, kv3, mixed_o, lse_o, bias, keys, values):
    fill_bias(s_ref[0], bias)
    fill_keys((kv0, kv1, kv2, kv3), keys, values)

    def one_pair(pair, carry):
        for odd in range(2):
            head = 2 * pair + odd
            kk = doubled(keys, pair, odd)
            vv = doubled(values, pair, odd)
            scores = nt(kk, stacked(q, head, SCORE_SCALE)) + bias[...]
            highest = jnp.max(scores, axis=0, keepdims=True)
            raised = jnp.exp(scores - highest)
            totals = jnp.sum(raised, axis=0, keepdims=True)
            probs = (raised * (1.0 / totals)).astype(BF16)
            lse_o[pl.ds(head, 1), :] = highest + jnp.log(totals)
            out = tn(vv, probs).T
            lane = lax.broadcasted_iota(jnp.int32, (ROWS, 128), 1)
            mixed_o[:, spot(head, 128)] = jnp.where(
                lane < HDIM, out[0:ROWS], out[ROWS : 2 * ROWS]
            ).astype(BF16)
        return carry

    lax.fori_loop(0, PAIRS, one_pair, 0)


attend = whole_call(
    attend_kernel,
    "attend",
    [shaped((ROWS, D), BF16), shaped((8, 512), F32)],
    scratch=[
        pltpu.VMEM((KEYS, 512), F32),
        pltpu.VMEM((KEYS, KVW), BF16),
        pltpu.VMEM((KEYS, KVW), BF16),
    ],
    limit=56,
)


def route_kernel(s_ref, mixed_ref, o0, o1, o2, o3, xr, gain, rt, rp, rc, hid_o, b_o, gates_o):
    for k, part in enumerate((o0, o1, o2, o3)):
        total = nn(mixed_ref[:, block(0, QUART)], part[:, block(0, QUART)])
        for g in range(1, 4):
            total = total + nn(mixed_ref[:, block(g, QUART)], part[:, block(g, QUART)])
        hid_o[:, block(k, QUART)] = xr[:, block(k, QUART)].astype(F32) + RESIDUAL_SCALE * total
    hidden = hid_o[...]
    inverse = lax.rsqrt(jnp.mean(hidden * hidden, axis=1, keepdims=True) + EPSILON)
    b_o[:, 0:D] = (hidden * inverse * gain[0:1, D : 2 * D]).astype(BF16)
    logits = nt(rt[...], b_o[:, 0:D])
    expert = lax.broadcasted_iota(jnp.int32, (16, HALF), 0)
    for half, routes in enumerate((rp, rc)):
        chosen = routes[0:1, :] == expert
        for r in range(1, 8):
            chosen = chosen | (routes[r : r + 1, :] == expert)
        level = jnp.where(chosen, logits[:, block(half, HALF)], MASKED)
        raised = jnp.exp(level - jnp.max(level, axis=0, keepdims=True))
        gates = raised / jnp.sum(raised, axis=0, keepdims=True)
        gates = jnp.concatenate([gates, jnp.zeros((112, HALF), F32)], axis=0).T
        gates_o[block(half, HALF), :] = gates
        high = gates.astype(BF16).astype(F32)
        b_o[block(half, HALF), D:BOUT] = (high + pltpu.roll(gates - high, 16, axis=1)).astype(BF16)


route = whole_call(
    route_kernel,
    "route",
    [shaped((ROWS, D), F32), shaped((ROWS, BOUT), BF16), shaped((ROWS, 128), F32)],
    limit=56,
)


def piece_at(at, r, n):
    return ((at[0] + 4 - r) % 4) * at[2] + ((at[1] + 4 - n) % 4) * at[3]


def piece_at(at, r, n):
    return ((at[0] + 4 - r) % 4) * at[2] + ((at[1] + 4 - n) % 4) * at[3]


def fill_weights(at, own, other, far_parts, dest, lanes):
    dest[block(0, QUART), lanes] = own
    dest[block(1, QUART), lanes] = other
    for r in range(4):
        for n in range(4):
            piece = piece_at(at, r, n)
            for k in range(2):
                dest[spot((2 + k) * PIECES + piece, PROWS), lanes] = far_parts[r][n, k]


def expert_kernel(
    s_ref, at_ref, b0, b1, b2, b3, g0, g1, g2, g3, w0, w1, f0, f1, f2, f3,
    dudw_o, gz_o, dbk_o, dbs_o, xs, gs, gates, dgs, wgu, wd, dudw
):
    step = pl.program_id(0)
    place = s_ref[0]

    @pl.when(step == 0)
    def _():
        for j, (b_ref, g_ref) in enumerate(zip((b0, b1, b2, b3), (g0, g1, g2, g3))):
            rows = block(j, ROWS)
            for k in range(4):
                xs[rows, block(k, QUART)] = b_ref[:, block(k ^ j, QUART)]
                gs[rows, block(k, QUART)] = g_ref[:, spot(place ^ k, QUART)]
            both = b_ref[:, D:BOUT].astype(F32)
            gates[rows, :] = both + pltpu.roll(both, 112, axis=1)
        dgs[...] = jnp.zeros_like(dgs)

    here_gu = spot(step, 2 * GROUP * FSLICE)
    for n in range(GROUP):
        up = slice(n * TILE, n * TILE + 2 * FSLICE)
        down = slice(n * TILE + 2 * FSLICE, (n + 1) * TILE)
        for k, part in enumerate((w0, w1)):
            wgu[step, block(k, QUART), block(n, 2 * FSLICE)] = part[n, :, 0 : 2 * FSLICE]
            wd[block(k, QUART), block(n, FSLICE)] = part[n, :, 2 * FSLICE :]
        for r, part in enumerate((f0, f1, f2, f3)):
            for m in range(4):
                for k in range(2):
                    rows = spot((2 + k) * PIECES + piece_at(at_ref, r, m), PROWS)
                    wgu[step, rows, block(n, 2 * FSLICE)] = part[m, k, :, up]
                    wd[rows, block(n, FSLICE)] = part[m, k, :, down]
    both = nn(xs[...], wgu[step])
    h_all = RESIDUAL_SCALE * nn(gs[...], wd[...])
    lane = lax.broadcasted_iota(jnp.int32, (TOKENS, 128), 1)
    added = jnp.zeros((TOKENS, 128), F32)
    for n in range(GROUP):
        e = step * GROUP + n
        u = both[:, 2 * n * FSLICE : (2 * n + 1) * FSLICE]
        w = both[:, (2 * n + 1) * FSLICE : (2 * n + 2) * FSLICE]
        h = h_all[:, block(n, FSLICE)]
        gate = jnp.sum(jnp.where(lane == e, gates[...], 0.0), axis=1, keepdims=True)
        sig = jax.nn.sigmoid(u)
        silu = u * sig
        z = (silu * w).astype(BF16).astype(F32)
        gz_o[:, block(n, FSLICE)] = (gate * z).astype(BF16)
        added = added + jnp.where(lane == e, jnp.sum(z * h, axis=1, keepdims=True), 0.0)
        dz = gate * h
        du = (dz * w * sig * (1.0 + u * (1.0 - sig))).astype(BF16)
        dw = (dz * silu).astype(BF16)
        dudw_o[:, block(2 * n, FSLICE)] = du
        dudw_o[:, block(2 * n + 1, FSLICE)] = dw
    dgs[...] += added
    dudw[:, here_gu] = dudw_o[...]

    @pl.when(step == EXPERTS // GROUP - 1)
    def _():
        width = 2 * GROUP * FSLICE
        whole = nt(dudw[:, 0:width], wgu[0])
        for n in range(1, EXPERTS // GROUP):
            whole = whole + nt(dudw[:, block(n, width)], wgu[n])
        whole = whole.astype(BF16)
        for j in range(4):
            out = (dbk_o, dbs_o)[j % 2]
            rows = block(j, ROWS)
            for k in range(4):
                out[j // 2, :, block(k ^ j, QUART)] = whole[rows, block(k, QUART)]
            dg = dgs[rows, 0:16]
            high = dg.astype(BF16).astype(F32)
            out[j // 2, :, D:BOUT] = jnp.concatenate(
                [high, dg - high, jnp.zeros((ROWS, 96), F32)], axis=1
            ).astype(BF16)


def fixed(rank):
    return lambda e: (0,) * rank


def experts(place, at, b_parts, g_parts, w_parts):
    return pl.pallas_call(
        expert_kernel,
        name="experts",
        grid=(EXPERTS // GROUP,),
        in_specs=[SMEM] * 2
        + [pl.BlockSpec((ROWS, BOUT), fixed(2))] * 4
        + [pl.BlockSpec((ROWS, D), fixed(2))] * 4
        + [pl.BlockSpec((GROUP, QUART, TILE), lambda e: (e, 0, 0))] * 2
        + [pl.BlockSpec((4, 2, PROWS, GROUP * TILE), lambda e: (0, 0, 0, e))] * 4,
        out_specs=[
            pl.BlockSpec((TOKENS, 2 * GROUP * FSLICE), lambda e: (0, e)),
            pl.BlockSpec((TOKENS, GROUP * FSLICE), lambda e: (0, e)),
            pl.BlockSpec((2, ROWS, BOUT), fixed(3)),
            pl.BlockSpec((2, ROWS, BOUT), fixed(3)),
        ],
        out_shape=[
            shaped((TOKENS, EXPERTS * 2 * FSLICE), BF16),
            shaped((TOKENS, EXPERTS * FSLICE), BF16),
            shaped((2, ROWS, BOUT), BF16),
            shaped((2, ROWS, BOUT), BF16),
        ],
        scratch_shapes=[
            pltpu.VMEM((TOKENS, D), BF16),
            pltpu.VMEM((TOKENS, D), BF16),
            pltpu.VMEM((TOKENS, 128), F32),
            pltpu.VMEM((TOKENS, 128), F32),
            pltpu.VMEM((EXPERTS // GROUP, D, 2 * GROUP * FSLICE), BF16),
            pltpu.VMEM((D, GROUP * FSLICE), BF16),
            pltpu.VMEM((TOKENS, EXPERTS * 2 * FSLICE), BF16),
        ],
        compiler_params=pltpu.CompilerParams(vmem_limit_bytes=58 * 1024 * 1024),
        cost_estimate=COST,
    )(place, at, *b_parts, *g_parts, *w_parts)


def piece_to(at, r, v):
    return ((at[0] + r) % 4) * at[2] + v * at[3]


def grad_rows(at_ref, steps, source, dest):
    for i, r in enumerate(steps):
        for v in range(4):
            for k in range(4):
                rows = spot(PIECES * k + piece_to(at_ref, r, v), PROWS)
                dest[block(PIECES * i + 4 * v + k, PROWS), :] = source[rows, :]


def grad_blocks(outs, x_rows, g_rows, dudw, gz):
    first = nn(x_rows[...], dudw[...]).astype(BF16)
    second = (RESIDUAL_SCALE * nn(g_rows[...], gz[...])).astype(BF16)
    for i, out in enumerate(outs):
        for v in range(4):
            for k in range(4):
                rows = block(PIECES * i + 4 * v + k, PROWS)
                for n in range(GROUP):
                    out[v, k, n, :, 0 : 2 * FSLICE] = first[rows, block(n, 2 * FSLICE)]
                    out[v, k, n, :, 2 * FSLICE :] = second[rows, block(n, FSLICE)]


def near_grad_kernel(
    s_ref, at_ref, b0, b1, b2, b3, g0, g1, g2, g3, dudw, gz, t1, t3, xt, gt, x_rows, g_rows
):
    @pl.when(pl.program_id(0) == 0)
    def _():
        for j, (b_ref, g_ref) in enumerate(zip((b0, b1, b2, b3), (g0, g1, g2, g3))):
            for k in range(4):
                xt[block(k, QUART), block(j, ROWS)] = b_ref[:, block(k ^ j, QUART)].T
                gt[block(k, QUART), block(j, ROWS)] = g_ref[:, spot(s_ref[0] ^ k, QUART)].T
        grad_rows(at_ref, (1, 3), xt, x_rows)
        grad_rows(at_ref, (1, 3), gt, g_rows)

    grad_blocks((t1, t3), x_rows, g_rows, dudw, gz)


def rest_grad_kernel(s_ref, at_ref, xt, gt, dudw, gz, t0, t2, x_rows, g_rows):
    @pl.when(pl.program_id(0) == 0)
    def _():
        grad_rows(at_ref, (0, 2), xt, x_rows)
        grad_rows(at_ref, (0, 2), gt, g_rows)

    grad_blocks((t0, t2), x_rows, g_rows, dudw, gz)


def expert_grads(kernel, place, at, inputs, outputs, dudw, gz):
    block_out = pl.BlockSpec((4, 4, GROUP, PROWS, TILE), lambda e: (0, 0, e, 0, 0))
    return pl.pallas_call(
        kernel,
        name=kernel.__name__,
        grid=(EXPERTS // GROUP,),
        in_specs=[SMEM] * 2
        + [pl.BlockSpec(part.shape, fixed(2)) for part in inputs]
        + [
            pl.BlockSpec((TOKENS, 2 * GROUP * FSLICE), lambda e: (0, e)),
            pl.BlockSpec((TOKENS, GROUP * FSLICE), lambda e: (0, e)),
        ],
        out_specs=[block_out] * 2 + [pl.BlockSpec(out.shape, fixed(2)) for out in outputs],
        out_shape=[shaped((4, 4, EXPERTS, PROWS, TILE), BF16)] * 2 + outputs,
        scratch_shapes=[pltpu.VMEM((2 * QUART, TOKENS), BF16)] * 2,
        compiler_params=pltpu.CompilerParams(vmem_limit_bytes=56 * 1024 * 1024),
        cost_estimate=COST,
    )(place, at, *inputs, dudw, gz)


def mixture_kernel(at_ref, gz, w0, w1, f0, f1, f2, f3, keep_o, send_o, wide):
    for e in range(EXPERTS):
        at = slice(e * TILE + 2 * FSLICE, (e + 1) * TILE)
        parts = [part.at[:, :, :, at] for part in (f0, f1, f2, f3)]
        fill_weights(at_ref, w0[e], w1[e], parts, wide, block(e, FSLICE))
    for j in range(4):
        out = (keep_o, send_o)[j % 2]
        total = nt(gz[block(j, ROWS), :], wide[...]).astype(BF16)
        for k in range(4):
            out[j // 2, :, block(k ^ j, QUART)] = total[:, block(k, QUART)]


def mixture(at, gz, w_parts):
    down = [pl.BlockSpec((EXPERTS, QUART, FSLICE), lambda i: (0, 0, 2))] * 2 + [
        pl.BlockSpec((4, 2, PROWS, SHAREW), lambda i: (0, 0, 0, 0))
    ] * 4
    return pl.pallas_call(
        mixture_kernel,
        name="mixture",
        grid=(1,),
        in_specs=[SMEM, pl.BlockSpec((TOKENS, EXPERTS * FSLICE), fixed(2))] + down,
        out_specs=[pl.BlockSpec((2, ROWS, D), fixed(3))] * 2,
        out_shape=[shaped((2, ROWS, D), BF16)] * 2,
        scratch_shapes=[pltpu.VMEM((D, EXPERTS * FSLICE), BF16)],
        compiler_params=pltpu.CompilerParams(vmem_limit_bytes=56 * 1024 * 1024),
        cost_estimate=COST,
    )(at, gz, *w_parts)


def attend_back_kernel(
    s_ref, db_keep, db_come, db_far, hid, b, gates_ref, gp, gc, gain, rt, mixed, lse,
    q, kv0, kv1, kv2, kv3, o0, o1, o2, o3,
    hgrad_o, small_o, dwok_o, dwos_o, dq_o, kvk_o, kvs_o, dk_o, dv_o,
    bias, keys, values, dmix, grow
):
    place = s_ref[0]
    parts = (o0, o1, o2, o3)
    fill_bias(place, bias)
    fill_keys((kv0, kv1, kv2, kv3), keys, values)
    total = db_keep[0].astype(F32) + db_come[0].astype(F32) + db_far[...].astype(F32)
    tail = total[:, D:BOUT]
    dgate = (tail + pltpu.roll(tail, 112, axis=1))[:, 0:16]
    gates = gates_ref[:, 0:16]
    dlog = (gates * (dgate - jnp.sum(gates * dgate, axis=1, keepdims=True))).astype(BF16)
    dbt = total[:, 0:D] + nn(dlog, rt[...])
    small_o[...] = jnp.zeros_like(small_o)
    small_o[16:32, :] = tn(dlog, b[:, 0:D])
    hidden = hid[...]
    inverse = lax.rsqrt(jnp.mean(hidden * hidden, axis=1, keepdims=True) + EPSILON)
    n2 = hidden * inverse
    small_o[1:2, :] = jnp.sum(dbt * n2, axis=0, keepdims=True)
    scaled = dbt * gain[0:1, D : 2 * D]
    for k in range(4):
        there = spot(place ^ k, QUART)
        grow[0:HALF, block(k, QUART)] = gp[:, there]
        grow[HALF:ROWS, block(k, QUART)] = gc[:, there]
    hgrad = grow[...].astype(F32) + inverse * (
        scaled - n2 * jnp.mean(scaled * n2, axis=1, keepdims=True)
    )
    hgrad_o[...] = hgrad
    agrad = (RESIDUAL_SCALE * hgrad).astype(BF16)
    for g in range(4):
        total = nt(agrad[:, block(0, QUART)], parts[0][:, block(g, QUART)])
        for k in range(1, 4):
            total = total + nt(agrad[:, block(k, QUART)], parts[k][:, block(g, QUART)])
        dmix[:, block(g, QUART)] = total.astype(BF16)
    for g in range(4):
        rows = tn(mixed[:, block(g, QUART)], agrad).astype(BF16)
        for k in range(4):
            out = (dwok_o, dwos_o)[k % 2]
            out[k // 2, :, block(g, QUART)] = rows[:, block(k, QUART)]

    def one_pair(pair, carry):
        dks = []
        dvs = []
        lane = lax.broadcasted_iota(jnp.int32, (ROWS, 128), 1)
        for odd in range(2):
            head = 2 * pair + odd
            kk = doubled(keys, pair, odd)
            vv = doubled(values, pair, odd)
            qs = stacked(q, head, SCORE_SCALE)
            ds_rows = stacked(dmix, head, 1.0)
            probs = jnp.exp(nt(kk, qs) + bias[...] - lse[pl.ds(head, 1), :])
            product = dmix[:, spot(head, 128)].astype(F32) * mixed[:, spot(head, 128)].astype(F32)
            product = product.T
            inner = jnp.concatenate(
                [
                    jnp.sum(product[0:HDIM], axis=0, keepdims=True),
                    jnp.sum(product[HDIM:], axis=0, keepdims=True),
                ],
                axis=1,
            )
            sgrad = (probs * (nt(vv, ds_rows) - inner)).astype(BF16)
            dkr = nn(sgrad, qs)
            dvr = nn(probs.astype(BF16), ds_rows)
            dks.append(dkr + pltpu.roll(dkr, HDIM, axis=1))
            dvs.append(dvr + pltpu.roll(dvr, HDIM, axis=1))
            dqt = (SCORE_SCALE * tn(kk, sgrad)).T
            dq_o[:, spot(head, 128)] = jnp.where(lane < HDIM, dqt[0:ROWS], dqt[ROWS : 2 * ROWS])
        low = lax.broadcasted_iota(jnp.int32, (KEYS, 128), 1) < HDIM
        dk = jnp.where(low, dks[0], dks[1])
        dv = jnp.where(low, dvs[0], dvs[1])
        at = spot(pair, 128)
        at_v = spot(pair + 4, 128)
        for j in range(4):
            side = (kvk_o, kvs_o)[j % 2]
            side[j // 2, :, at] = dk[block(j, HALF)].astype(BF16)
            side[j // 2, :, at_v] = dv[block(j, HALF)].astype(BF16)
        dk_o[:, at] = dk[4 * HALF :]
        dv_o[:, at] = dv[4 * HALF :]
        return carry

    lax.fori_loop(0, PAIRS, one_pair, 0)


attend_back = whole_call(
    attend_back_kernel,
    "attend_back",
    [
        shaped((ROWS, D), F32),
        shaped((32, D), F32),
        shaped((2, QUART, D), BF16),
        shaped((2, QUART, D), BF16),
        shaped((ROWS, D), F32),
        shaped((2, HALF, D), BF16),
        shaped((2, HALF, D), BF16),
        shaped((HALF, KVW), F32),
        shaped((HALF, KVW), F32),
    ],
    scratch=[
        pltpu.VMEM((KEYS, 512), F32),
        pltpu.VMEM((KEYS, KVW), BF16),
        pltpu.VMEM((KEYS, KVW), BF16),
        pltpu.VMEM((ROWS, D), BF16),
        pltpu.VMEM((ROWS, D), BF16),
    ],
    limit=36,
    parts={n: ((1, ROWS, BOUT), (0, 0, 0)) for n in (1, 2)},
)


def turn_back(values, cosine, sine):
    return values * cosine - swapped(values) * sine


def query_back_kernel(
    s_ref, dq, nq, inv, gain, cos, sin, ar, a0, a1, a2, a3, dwqk_o, dwqs_o, da_o, qg_o, grads
):
    cosine = here(s_ref[0], cos)
    sine = here(s_ref[0], sin)
    inv_q = inv[:, 0:1]
    dot = jnp.zeros((ROWS, 1), F32)
    for g in range(8):
        at = block(g, 128)
        back = turn_back(dq[:, at], cosine, sine)
        near = nq[:, at]
        qg_o[0:1, at] = jnp.sum(back * near, axis=0, keepdims=True)
        scaled = back * gain[0:1, 2 * D + g * 128 : 2 * D + (g + 1) * 128]
        dot = dot + jnp.sum(scaled * near, axis=1, keepdims=True)
        grads[:, at] = scaled
    pre = (inv_q * (grads[...] - nq[...] * (dot / D))).astype(BF16)
    for k, part in enumerate((a0, a1, a2, a3)):
        da_o[:, block(k, QUART)] = nt(pre, part[...])
        out = (dwqk_o, dwqs_o)[k % 2]
        out[k // 2] = tn(ar[:, block(k, QUART)], pre).astype(BF16)


query_back = whole_call(
    query_back_kernel,
    "query_back",
    [
        shaped((2, QUART, D), BF16),
        shaped((2, QUART, D), BF16),
        shaped((ROWS, D), F32),
        shaped((8, D), F32),
    ],
    scratch=[pltpu.VMEM((ROWS, D), F32)],
    parts={n: ((QUART, D), (0, 0)) for n in range(8, 12)},
)


def key_back_kernel(
    s_ref, kv_keep, kv_come, dk, dv, nk, inv, gain, cos, sin, ar, xr, hgrad, da_q, qg, small,
    a0, a1, a2, a3, keep_o, send_o, xp_o, xc_o, grads, both, da, cols
):
    place = s_ref[0]
    cosine = here(s_ref[0], cos)
    sine = here(s_ref[0], sin)
    inv_k = inv[:, 1:2]
    grads[0:HALF, :] = kv_keep[:, 0:KVW].astype(F32) + kv_come[:, 0:KVW].astype(F32)
    grads[HALF:ROWS, :] = dk[...]
    both[0:HALF, KVW:D] = (kv_keep[:, KVW:D].astype(F32) + kv_come[:, KVW:D].astype(F32)).astype(BF16)
    both[HALF:ROWS, KVW:D] = dv[...].astype(BF16)
    cols[...] = jnp.zeros_like(cols)
    dot = jnp.zeros((ROWS, 1), F32)
    for g in range(4):
        at = block(g, 128)
        back = turn_back(grads[:, at], cosine, sine)
        near = nk[:, at]
        kgrad = jnp.sum(back * near, axis=0, keepdims=True)
        cols[3:4, spot(place ^ g, QUART)] = jnp.concatenate([kgrad, jnp.zeros_like(kgrad)], axis=1)
        scaled = back * gain[0:1, 3 * D + g * 128 : 3 * D + (g + 1) * 128]
        dot = dot + jnp.sum(scaled * near, axis=1, keepdims=True)
        grads[:, at] = scaled
    both[:, 0:KVW] = (inv_k * (grads[...] - nk[...] * (dot / KVW))).astype(BF16)
    pre = both[...]
    for k, part in enumerate((a0, a1, a2, a3)):
        da[:, block(k, QUART)] = da_q[:, block(k, QUART)] + nt(pre, part[...])
        out = (keep_o, send_o)[k % 2]
        out[k // 2, :, 0:D] = tn(ar[:, block(k, QUART)], pre).astype(BF16)
    x = xr[...].astype(F32)
    inverse = inv[:, 2:3]
    n1 = x * inverse
    grad = da[...]
    cols[0:1, :] = jnp.sum(grad * n1, axis=0, keepdims=True)
    cols[1:2, :] = small[1:2, :]
    cols[16:32, :] = small[16:32, :]
    for k in range(4):
        cols[2:3, block(k, QUART)] = qg[0:1, spot(place ^ k, QUART)]
    for k in range(4):
        out = (keep_o, send_o)[k % 2]
        out[k // 2, :, D:BOUT] = cols[:, block(k, QUART)].T.astype(BF16)
    scaled = grad * gain[0:1, 0:D]
    result = hgrad[...] + inverse * (scaled - n1 * jnp.mean(scaled * n1, axis=1, keepdims=True))
    low = result.astype(BF16)
    for k in range(4):
        there = spot(place ^ k, QUART)
        xp_o[:, there] = low[0:HALF, block(k, QUART)]
        xc_o[:, there] = low[HALF:ROWS, block(k, QUART)]


key_back = whole_call(
    key_back_kernel,
    "key_back",
    [
        shaped((2, QUART, BOUT), BF16),
        shaped((2, QUART, BOUT), BF16),
        shaped((HALF, D), BF16),
        shaped((HALF, D), BF16),
    ],
    scratch=[
        pltpu.VMEM((ROWS, KVW), F32),
        pltpu.VMEM((ROWS, D), BF16),
        pltpu.VMEM((ROWS, D), F32),
        pltpu.VMEM((128, D), F32),
    ],
    parts={n: ((QUART, D), (1, 0)) for n in range(16, 20)},
)


def finish_kernel(s_ref, hid, keep, come, xp_o, xc_o):
    total = hid[...] + RESIDUAL_SCALE * (keep[...].astype(F32) + come[...].astype(F32))
    low = total.astype(BF16)
    for k in range(4):
        there = spot(s_ref[0] ^ k, QUART)
        xp_o[:, there] = low[0:HALF, block(k, QUART)]
        xc_o[:, there] = low[HALF:ROWS, block(k, QUART)]


finish = whole_call(
    finish_kernel,
    "finish",
    [shaped((HALF, D), BF16), shaped((HALF, D), BF16)],
)


def pair_kernel(at_ref, qk, qc, lk, lc, ok, oc, t0, t1, t2, t3):
    for r, out in enumerate((t0, t1, t2, t3)):
        for v in range(4):
            rows = spot(piece_to(at_ref, r, v), PROWS)
            last = (lk[0, rows, :].astype(F32) + lc[0, rows, :].astype(F32)).astype(BF16)
            out[v, 0, :, 0:D] = (qk[0, rows, :].astype(F32) + qc[0, rows, :].astype(F32)).astype(BF16)
            out[v, 0, :, D:QKVW] = last[:, 0:D]
            out[v, 0, :, QKVW : QKVW + D] = (
                ok[0, rows, :].astype(F32) + oc[0, rows, :].astype(F32)
            ).astype(BF16)
            out[v, 0, :, QKVW + D :] = last[:, D:]


def pair(at, *parts):
    return pl.pallas_call(
        pair_kernel,
        name="pair",
        grid=(2,),
        in_specs=[SMEM]
        + [pl.BlockSpec((1, QUART, part.shape[2]), lambda k: (k, 0, 0)) for part in parts],
        out_specs=[pl.BlockSpec((4, 1, PROWS, ATTW), lambda k: (0, k, 0, 0))] * 4,
        out_shape=[shaped((4, 2, PROWS, ATTW), BF16)] * 4,
        compiler_params=pltpu.CompilerParams(vmem_limit_bytes=24 * 1024 * 1024),
        cost_estimate=COST,
    )(at, *parts)


def fold_kernel(at_ref, i0, i1, i2, i3, o0, o1, o2, o3):
    for r, out in enumerate((o0, o1, o2, o3)):
        there = (at_ref[1] + r) % 4
        total = i0[there].astype(F32) + i1[there].astype(F32)
        out[...] = (total + i2[there].astype(F32) + i3[there].astype(F32)).astype(BF16)


def fold(at, parts, rows, steps):
    shape = parts[0].shape
    width = shape[-1]
    flat = [part.reshape(4, rows, width) for part in parts]
    height = rows // steps
    outs = pl.pallas_call(
        fold_kernel,
        name="fold",
        grid=(steps,),
        in_specs=[SMEM] + [pl.BlockSpec((4, height, width), lambda i: (0, i, 0))] * 4,
        out_specs=[pl.BlockSpec((height, width), lambda i: (i, 0))] * 4,
        out_shape=[shaped((rows, width), BF16)] * 4,
        compiler_params=pltpu.CompilerParams(vmem_limit_bytes=24 * 1024 * 1024),
        cost_estimate=COST,
    )(at, *flat)
    return [out.reshape(shape[1:]) for out in outs]


def unpack_kernel(s_ref, at_ref, p0, p1, p2, p3, p4, gate_o, up_o, down_o, tile):
    for r, part, low in ((0, p0, 0), (1, p1, 0), (2, p2, 0), (2, p3, 2), (3, p4, 0)):
        for n in range(part.shape[0]):
            rows = spot(piece_at(at_ref, r, low + n), PROWS)
            for k in range(4):
                there = spot(s_ref[0] ^ k, FSLICE)
                gate_o[0, rows, there] = part[n, k, 0, :, 0:FSLICE].astype(F32)
                up_o[0, rows, there] = part[n, k, 0, :, FSLICE : 2 * FSLICE].astype(F32)
                tile[rows, block(k, FSLICE)] = part[n, k, 0, :, 2 * FSLICE :].astype(F32)
    for k in range(4):
        down_o[0, spot(s_ref[0] ^ k, FSLICE), :] = tile[:, block(k, FSLICE)].T


def unpack_experts(place, at, parts):
    specs = [
        pl.BlockSpec((part.shape[0], 4, 1, PROWS, TILE), lambda e: (0, 0, e, 0, 0))
        for part in parts
    ]
    return pl.pallas_call(
        unpack_kernel,
        name="unpack_experts",
        grid=(EXPERTS,),
        in_specs=[SMEM] * 2 + specs,
        out_specs=[
            pl.BlockSpec((1, QUART, 512), lambda e: (e, 0, 0)),
            pl.BlockSpec((1, QUART, 512), lambda e: (e, 0, 0)),
            pl.BlockSpec((1, 512, QUART), lambda e: (e, 0, 0)),
        ],
        out_shape=[
            shaped((EXPERTS, QUART, 512), F32),
            shaped((EXPERTS, QUART, 512), F32),
            shaped((EXPERTS, 512, QUART), F32),
        ],
        scratch_shapes=[pltpu.VMEM((QUART, 512), F32)],
        compiler_params=pltpu.CompilerParams(vmem_limit_bytes=24 * 1024 * 1024),
        cost_estimate=COST,
    )(place, at, *parts)


def unpack_attention_kernel(
    at_ref, p0, p1, p2, p3, wq_o, wk_o, wv_o, wo_o, attn_o, ffn_o, qg_o, kg_o, router_o, wide
):
    for r, part in enumerate((p0, p1, p2, p3)):
        for n in range(4):
            wide[spot(piece_at(at_ref, r, n), PROWS), :] = part[n]
    wq_o[...] = wide[:, 0:D].astype(F32)
    wk_o[...] = wide[:, D : D + KVW].astype(F32)
    wv_o[...] = wide[:, D + KVW : QKVW].astype(F32)
    for g in range(4):
        wo_o[block(g, QUART), :] = wide[:, QKVW + g * QUART : QKVW + (g + 1) * QUART].astype(F32)
    tail = wide[:, QKVW + D :].astype(F32)
    rows = tail.T
    attn_o[...] = rows[0:1]
    ffn_o[...] = rows[1:2]
    qg_o[...] = rows[2:3]
    kg_o[...] = rows[3:4, 0:HALF]
    router_o[...] = rows[16 : 16 + EXPERTS]


unpack_attention = whole_call(
    unpack_attention_kernel,
    "unpack_attention",
    [
        shaped((QUART, D), F32),
        shaped((QUART, KVW), F32),
        shaped((QUART, KVW), F32),
        shaped((D, QUART), F32),
        shaped((1, QUART), F32),
        shaped((1, QUART), F32),
        shaped((1, QUART), F32),
        shaped((1, HALF), F32),
        shaped((EXPERTS, QUART), F32),
    ],
    scratch=[pltpu.VMEM((QUART, ATTW), BF16)],
)


def body(
    prompt_x, cont_x, prompt_cot, cont_cot, prompt_routes, cont_routes,
    attn_gain, w_query, w_key, w_value, query_gain, key_gain,
    w_out, ffn_gain, w_router, w_gate, w_up, w_down,
):
    def moved(value, axes, change):
        sizes = [lax.axis_size(a) for a in axes]
        pairs = []
        count = 1
        for size in sizes:
            count *= size
        for index in range(count):
            rest, coords = index, []
            for size in reversed(sizes):
                coords.append(rest % size)
                rest //= size
            to = change(*reversed(coords))
            target = 0
            for size, coord in zip(sizes, to):
                target = target * size + coord
            pairs.append((index, target))
        return lax.ppermute(value, axes, pairs)

    def sib(value):
        return moved(value, ("c",), lambda c: (1 - c,))

    def far(value):
        return moved(value, ("xh",), lambda h: (1 - h,))

    def far_sib(value):
        return moved(value, ("xh", "c"), lambda h, c: (1 - h, 1 - c))

    def cross(value):
        return moved(value, ("xl", "xh"), lambda low, high: (1 - low, 1 - high))

    def cross_sib(value):
        return moved(value, ("xl", "xh", "c"), lambda low, high, c: (1 - low, 1 - high, 1 - c))

    def near(value):
        return moved(value, ("xl",), lambda low: (1 - low,))

    def along(value, by, core_of_z):
        def change(at_z, at_y, c):
            if c == core_of_z:
                return ((at_z + by) % 4, at_y, c)
            return (at_z, (at_y + by) % 4, c)

        return moved(value, ("z", "y", "c"), change)

    def first(value, by):
        return along(value, by, 1)

    def second(value, by):
        return along(value, by, 0)

    def spread(value, way):
        return [value] + [way(value, by) for by in (1, 2, 3)]

    def added(parts):
        total = parts[0].astype(F32)
        for part in parts[1:]:
            total = total + part.astype(F32)
        return total.astype(BF16)

    after = lax.optimization_barrier

    z = lax.axis_index("z").astype(jnp.int32)
    y = lax.axis_index("y").astype(jnp.int32)
    core = lax.axis_index("c").astype(jnp.int32)
    low_core = core == 0
    at = jnp.stack(
        [
            jnp.where(low_core, y, z),
            jnp.where(low_core, z, y),
            jnp.where(low_core, 1, 4),
            jnp.where(low_core, 4, 1),
        ]
    )
    position = lax.axis_index(("xh", "c")).astype(jnp.int32)
    place = position[None]
    piece = 4 * z + y
    cont_in = cont_x.reshape(HALF, D)
    cont_up = cont_cot.reshape(HALF, D)

    def held(value, *others):
        return after((value, others))[0]

    share_two, share_three = share_experts(
        jnp.concatenate([piece[None], place]), w_gate, w_up, w_down
    )
    place_in, share_two, share_three = after((place, share_two, share_three))
    share_two = cross(share_two)
    share_three = cross_sib(share_three)
    own_in = prepare(
        place_in, w_query, w_key, w_value, attn_gain[None], ffn_gain[None], query_gain[None],
        key_gain[None], w_router.T,
    )
    place_in, own_in, share_two, share_three = after((place, own_in, share_two, share_three))
    in_two = cross(own_in)
    row = jnp.stack(spread(jnp.stack([share_two, share_three]), second))
    own_out = prepare_out(place_in, w_out)
    packed = pack_experts(place_in, w_gate, w_up, w_down)
    in_two, packed, row, own_in_sib, own_out, out_sib = after(
        (in_two, packed, row, sib(own_in), own_out, sib(own_out))
    )
    in_parts = (own_in, own_in_sib, in_two, sib(in_two))

    cosine, sine = (jnp.asarray(table) for table in angle_tables())

    kv, kv_own, nk, inv, xr, ar, gain, rt = project_keys(
        place, prompt_x, cont_in, *in_parts, cosine, sine
    )
    kv_two = far(kv_own)
    row_one = first(row, 1)
    row_three = first(row, 3)
    q, nq, inv_q = project_query(place, ar, gain, *in_parts, cosine, sine)
    kv_two = held(kv_two, q)
    out_two = cross(own_out)
    upstream = jnp.concatenate([prompt_cot, cont_up], axis=0)
    up_two = cross(upstream)
    kv_parts = (kv, sib(held(kv_own, q)), kv_two, sib(kv_two))
    kv_parts, out_two = after((kv_parts, out_two))
    mixed, lse = attend(place, q, *kv_parts)
    row, row_one, row_three, packed, upstream, up_two = after(
        (row, row_one, row_three, packed, upstream, up_two, mixed)
    )[0:6]
    row_two = first(row, 2)
    out_parts = (own_out, out_sib, out_two, sib(out_two))
    hidden, b, gates = route(
        place, mixed, *out_parts, xr, gain, rt, prompt_routes.T, cont_routes.reshape(HALF, 8).T
    )
    up_sib = sib(upstream)
    packed_sib = sib(packed[1])
    b, up_sib, packed_sib = after((b, up_sib, packed_sib))
    w_parts = (packed[0], packed_sib, row, row_one, row_two, row_three)
    b_two, up_sib_two = after((cross(b), sib(up_two)))
    up_parts = (upstream, up_sib, up_two, up_sib_two)
    b_parts = (b, sib(b), b_two, sib(b_two))
    dudw, gz, db_keep, db_send = experts(place, at, b_parts, up_parts, w_parts)

    db_come = sib(db_send)
    db_sum = added([db_keep[1], db_come[1]])
    db_sum, dudw = after((db_sum, dudw))
    db_far = cross(db_sum)
    turned = [shaped((D, TOKENS), BF16)] * 2
    grad_one, grad_three, xt, gt = expert_grads(
        near_grad_kernel, place, at, [*b_parts, *up_parts], turned, dudw, gz
    )
    place_in, xt, db_far = after((place, xt, db_far))
    grad_own, grad_next = expert_grads(rest_grad_kernel, place_in, at, [xt, gt], [], dudw, gz)
    grad_one = first(grad_one, 1)
    grad_three = first(grad_three, 3)
    grad_two = first(grad_next, 2)
    later = held(place, grad_own)

    hgrad, small, dwo_keep, dwo_send, dq, kv_keep, kv_send, dk, dv = attend_back(
        later, db_keep, db_come, db_far, hidden, b, gates, prompt_cot, cont_up, gain, rt, mixed, lse,
        q, *kv_parts, *out_parts,
    )

    kv_come = sib(kv_send)
    kv_sum = added([kv_keep, kv_come])
    kv_far = far(kv_sum[1])
    dq, kv_sum = after((dq, kv_sum))
    dwq_keep, dwq_send, da_q, qg = query_back(
        place, dq, nq, inv_q, gain, cosine, sine, ar, *in_parts
    )
    grad_one, grad_two, grad_three, da_q = after((grad_one, grad_two, grad_three, da_q))
    grad_rest = fold(at, [grad_own, grad_one, grad_two, grad_three], 4 * EXPERTS * PROWS, 2)
    da_q, grad_rest = after((da_q, grad_rest))
    last_keep, last_send, prompt_grad, cont_grad = key_back(
        place, kv_sum[0], kv_far, dk, dv, nk, inv, gain, cosine, sine, ar, xr, hgrad, da_q, qg,
        small, *in_parts,
    )

    paired = pair(
        held(at, grad_rest), dwq_keep, sib(dwq_send), last_keep, sib(last_send), dwo_keep, sib(dwo_send)
    )
    grad_rest = [grad_rest[0]] + [second(grad_rest[by], by) for by in (1, 2, 3)]
    summed = added(held(grad_rest, paired[0]))
    paired = [paired[0]] + [first(paired[by], by) for by in (1, 2, 3)]

    turned_parts = [summed[0], sib(summed[1]), far(summed[2]), far_sib(summed[3])]
    paired[1], paired[3], turned_parts = after((paired[1], paired[3], turned_parts))
    turned_parts = jnp.stack(turned_parts, axis=0)
    near_parts = near(turned_parts)
    mix_keep, mix_send = mixture(at, held(gz, turned_parts), w_parts)
    own_sum = added([turned_parts, held(near_parts, mix_keep)])
    steps = jnp.stack(spread(own_sum, second))
    paired = held(fold(at, held(paired, turned_parts), 2 * PROWS, 1), steps)
    steps_one = first(steps, 1)
    steps_three = first(steps, 3)

    mix_sum = added([mix_keep, sib(mix_send)])
    mix_far = cross(mix_sum[1])
    prompt_out, cont_out = finish(place, hidden, mix_sum[0], mix_far)

    part = added([paired[0]] + [second(paired[by], by) for by in (1, 2, 3)])
    part = added([part[0], near(part[0]), far(part[1]), cross(part[1])])
    part_steps = jnp.stack(spread(part, second))
    steps_one, steps_three, part_steps = after((steps_one, steps_three, part_steps))
    steps_two = (first(steps_one[0:2], 1), first(steps_three[2:4], 3))
    full = spread(part_steps, first)
    gate_grad, up_grad, down_grad = unpack_experts(
        place, at, (steps, steps_one, *steps_two, steps_three)
    )
    wq_grad, wk_grad, wv_grad, wo_grad, attn_grad, ffn_grad, qg_grad, kg_grad, router_grad = (
        unpack_attention(at, *held(full, gate_grad))
    )

    return (
        prompt_out,
        cont_out.reshape(1, HALF, D),
        prompt_grad,
        cont_grad.reshape(1, HALF, D),
        attn_grad[0],
        wq_grad,
        wk_grad,
        wv_grad,
        qg_grad[0],
        kg_grad[0],
        wo_grad,
        ffn_grad[0],
        router_grad.T,
        gate_grad,
        up_grad,
        down_grad,
    )


def solution(mesh):
    fine = Mesh(mesh.devices.reshape(2, 4, 4, 2, 2), AXES)
    shard = ("xh", "c")
    tokens = P(AXES, None)
    series = P(AXES, None, None)
    weights = (
        P(shard),
        P(shard, None),
        P(shard, None),
        P(shard, None),
        P(shard),
        P(shard),
        P(None, shard),
        P(shard),
        P(shard, None),
        P(None, shard, None),
        P(None, shard, None),
        P(None, None, shard),
    )
    return jax.shard_map(
        body,
        mesh=fine,
        in_specs=(tokens, series, tokens, series, tokens, series, *weights),
        out_specs=(tokens, series, tokens, series, *weights),
        check_vma=False,
    )
```

```python
import jax
import jax.numpy as jnp
import numpy as np
from jax import lax
from jax.experimental import pallas as pl
from jax.experimental.pallas import tpu as pltpu
from jax.sharding import Mesh, PartitionSpec as P

EPSILON = 1e-06
SCORE_SCALE = 0.25
RESIDUAL_SCALE = 0.22
ROTARY_BASE = 10000.0
MASKED = -1e30

D = 1024
HDIM = 64
PAIRS = 4
KVW = 512
QKVW = 2048
ROWS = 256
HALF = 128
QUART = 256
EXPERTS = 9
FSLICE = 128
TILE = 3 * FSLICE
TOKENS = 4 * ROWS
KEYS = 5 * HALF
BOUT = D + 128
ATTW = QKVW + D + 128
PIECES = 16
PROWS = QUART // PIECES
SHAREW = EXPERTS * TILE
GROUP = 3

F32 = jnp.float32
BF16 = jnp.bfloat16


def angle_tables():
    frequency = np.float32(ROTARY_BASE) ** (-np.arange(0, HDIM, 2, dtype=np.float32) / HDIM)
    turned = np.arange(KEYS, dtype=np.float32)[:, None] * frequency.astype(np.float32)[None, :]
    cosine = np.tile(np.cos(turned), (1, 4)).astype(np.float32)
    sine = np.sin(turned)
    sine = np.concatenate([-sine, sine, -sine, sine], axis=1).astype(np.float32)
    return cosine, sine


AXES = ("xl", "z", "y", "xh", "c")


def nn(left, right):
    return lax.dot_general(left, right, (((1,), (0,)), ((), ())), preferred_element_type=F32)


def nt(left, right):
    return lax.dot_general(left, right, (((1,), (1,)), ((), ())), preferred_element_type=F32)


def tn(left, right):
    return lax.dot_general(left, right, (((0,), (0,)), ((), ())), preferred_element_type=F32)


def spot(index, width):
    return pl.ds(pl.multiple_of(index * width, width), width)


def block(index, width):
    return slice(index * width, (index + 1) * width)


SMEM = pl.BlockSpec(memory_space=pltpu.SMEM)
VMEM = pl.BlockSpec(memory_space=pltpu.VMEM)


COST = pl.CostEstimate(flops=1_000_000, bytes_accessed=1_000_000, transcendentals=0)


def whole_call(kernel, name, out_shape, scratch=(), limit=24, parts=None):
    def whole(shape, index=None):
        index = index or (0,) * len(shape)
        return pl.BlockSpec(shape, lambda i: index)

    def call(*operands):
        specs = [
            whole(*parts[n]) if parts and n in parts else whole(operand.shape)
            for n, operand in enumerate(operands)
        ]
        return pl.pallas_call(
            kernel,
            name=name,
            out_shape=out_shape,
            grid=(1,),
            in_specs=[SMEM] + specs[1:],
            out_specs=jax.tree.map(lambda out: whole(out.shape), out_shape),
            scratch_shapes=list(scratch),
            compiler_params=pltpu.CompilerParams(vmem_limit_bytes=limit * 1024 * 1024),
            cost_estimate=COST,
        )(*operands)

    return call


def shaped(shape, dtype):
    return jax.ShapeDtypeStruct(shape, dtype)


def pack_kernel(s_ref, gate, up, down, own, other):
    turned = down[0].T
    for k, out in ((0, own), (1, other)):
        low = (s_ref[0] % 2) == k
        for n, part in enumerate((gate[0], up[0], turned)):
            half = jnp.where(low, part[:, 0:FSLICE], part[:, FSLICE:])
            out[0, :, block(n, FSLICE)] = half.astype(BF16)


def pack_experts(place, w_gate, w_up, w_down):
    wide = pl.BlockSpec((1, QUART, 2 * FSLICE), lambda e, s: (e, 0, s[0] // 2))
    out = pl.BlockSpec((1, QUART, TILE), lambda e, s: (e, 0, 0))
    return pl.pallas_call(
        pack_kernel,
        name="pack_experts",
        grid_spec=pltpu.PrefetchScalarGridSpec(
            num_scalar_prefetch=1,
            grid=(EXPERTS,),
            in_specs=[
                wide,
                wide,
                pl.BlockSpec((1, 2 * FSLICE, QUART), lambda e, s: (e, s[0] // 2, 0)),
            ],
            out_specs=[out, out],
        ),
        out_shape=[shaped((EXPERTS, QUART, TILE), BF16)] * 2,
        compiler_params=pltpu.CompilerParams(vmem_limit_bytes=56 * 1024 * 1024),
        cost_estimate=COST,
    )(place, w_gate, w_up, w_down)


def share_kernel(at_ref, gate, up, down, two, three, turned):
    for k, dest in ((2, two), (3, three)):
        there = spot(at_ref[1] ^ k, FSLICE)
        for e in range(EXPERTS):
            at = e * TILE
            dest[:, at : at + FSLICE] = gate[e, :, there].astype(BF16)
            dest[:, at + FSLICE : at + 2 * FSLICE] = up[e, :, there].astype(BF16)
            turned[...] = down[e, there, :].T
            dest[:, at + 2 * FSLICE : at + TILE] = turned[
                spot(at_ref[0] % 8, PROWS), :
            ].astype(BF16)


def share_experts(at, w_gate, w_up, w_down):
    rows = pl.BlockSpec((EXPERTS, PROWS, 512), lambda i, at: (0, at[0], 0))
    dest = pl.BlockSpec((PROWS, SHAREW), lambda i, at: (0, 0))
    return pl.pallas_call(
        share_kernel,
        name="share_experts",
        grid_spec=pltpu.PrefetchScalarGridSpec(
            num_scalar_prefetch=1,
            grid=(1,),
            in_specs=[
                rows,
                rows,
                pl.BlockSpec((EXPERTS, 512, 128), lambda i, at: (0, 0, at[0] // 8)),
            ],
            out_specs=[dest, dest],
            scratch_shapes=[pltpu.VMEM((128, FSLICE), F32)],
        ),
        out_shape=[shaped((PROWS, SHAREW), BF16)] * 2,
        compiler_params=pltpu.CompilerParams(vmem_limit_bytes=56 * 1024 * 1024),
        cost_estimate=COST,
    )(at, w_gate, w_up, w_down)


def prepare_kernel(s_ref, wq, wk, wv, attn, ffn, query, key, router, kv_o, line):
    kv_o[0:QUART, :] = wq[...].astype(BF16)
    kv_o[QUART : 2 * QUART, 0:KVW] = wk[...].astype(BF16)
    kv_o[QUART : 2 * QUART, KVW:D] = wv[...].astype(BF16)
    line[...] = jnp.zeros_like(line)
    line[0:1, 0:256] = attn[...]
    line[0:1, 256:512] = ffn[...]
    line[0:1, 512:768] = query[...]
    line[0:1, 768:896] = key[...]
    kv_o[2 * QUART : 2 * QUART + 16, :] = line[...].astype(BF16)
    line[...] = jnp.zeros_like(line)
    line[0:EXPERTS, 0:QUART] = router[...]
    kv_o[2 * QUART + 16 :, :] = line[...].astype(BF16)


prepare = whole_call(
    prepare_kernel,
    "prepare",
    shaped((2 * QUART + 32, D), BF16),
    scratch=[pltpu.VMEM((16, D), F32)],
    limit=56,
)


def swapped(values):
    lane = lax.broadcasted_iota(jnp.int32, values.shape, 1)
    return jnp.where(
        lane % HDIM < HDIM // 2, pltpu.roll(values, 96, axis=1), pltpu.roll(values, 32, axis=1)
    )


def here(place, table):
    return jnp.concatenate([table[spot(place, HALF), :], table[4 * HALF :, :]], axis=0)


def project_keys_kernel(
    s_ref, xp, xc, a0, a1, a2, a3, cos, sin, kv_o, kvp_o, nk_o, inv_o, xr_o, ar_o, gain_o, rt_o, acc
):
    parts = (a0, a1, a2, a3)
    for k in range(4):
        there = s_ref[0] ^ k
        xr_o[0:HALF, block(k, QUART)] = xp[:, spot(there, QUART)]
        xr_o[HALF:ROWS, block(k, QUART)] = xc[:, spot(there, QUART)]
        small = parts[k][2 * QUART : 2 * QUART + 16, :].astype(F32)[0:1]
        gain_o[0:1, block(k, QUART)] = small[:, 0:256]
        gain_o[0:1, slice(D + k * QUART, D + (k + 1) * QUART)] = small[:, 256:512]
        gain_o[0:1, pl.ds(pl.multiple_of(2 * D + there * QUART, 128), QUART)] = small[:, 512:768]
        gain_o[0:1, pl.ds(pl.multiple_of(3 * D + there * HALF, 128), HALF)] = small[:, 768:896]
        rt_o[:, block(k, QUART)] = parts[k][2 * QUART + 16 :, 0:QUART]
    x = xr_o[...].astype(F32)
    inverse = lax.rsqrt(jnp.mean(x * x, axis=1, keepdims=True) + EPSILON)
    ar_o[...] = (x * inverse * gain_o[0:1, 0:D]).astype(BF16)
    total = nn(ar_o[:, block(0, QUART)], parts[0][QUART : 2 * QUART, :])
    for k in range(1, 4):
        total = total + nn(ar_o[:, block(k, QUART)], parts[k][QUART : 2 * QUART, :])
    acc[...] = total
    kp = acc[:, 0:KVW]
    inv_k = lax.rsqrt(jnp.mean(kp * kp, axis=1, keepdims=True) + EPSILON)
    nk_o[...] = kp * inv_k
    lane = lax.broadcasted_iota(jnp.int32, (ROWS, 128), 1)
    inv_o[...] = jnp.where(lane == 1, inv_k, inverse)
    kv_o[:, KVW:D] = acc[:, KVW:D].astype(BF16)
    cosine = here(s_ref[0], cos)
    sine = here(s_ref[0], sin)
    for g in range(4):
        at = block(g, 128)
        u = nk_o[:, at] * gain_o[0:1, 3 * D + g * 128 : 3 * D + (g + 1) * 128]
        kv_o[:, at] = (u * cosine + swapped(u) * sine).astype(BF16)
    kvp_o[...] = kv_o[0:HALF, :]


project_keys = whole_call(
    project_keys_kernel,
    "project_keys",
    [
        shaped((ROWS, D), BF16),
        shaped((HALF, D), BF16),
        shaped((ROWS, KVW), F32),
        shaped((ROWS, 128), F32),
        shaped((ROWS, D), BF16),
        shaped((ROWS, D), BF16),
        shaped((8, 3 * D + KVW), F32),
        shaped((16, D), BF16),
    ],
    scratch=[pltpu.VMEM((ROWS, D), F32)],
    limit=56,
)


def prepare_out_kernel(s_ref, wo, out):
    for g in range(4):
        out[:, block(g, QUART)] = wo[block(g, QUART), :].astype(BF16)


prepare_out = whole_call(
    prepare_out_kernel, "prepare_out", shaped((QUART, D), BF16), limit=56
)


def project_query_kernel(s_ref, ar, gain, a0, a1, a2, a3, cos, sin, q_o, nq_o, inv_o):
    total = nn(ar[:, block(0, QUART)], a0[...])
    for k, part in ((1, a1), (2, a2), (3, a3)):
        total = total + nn(ar[:, block(k, QUART)], part[...])
    nq_o[...] = total
    inv_q = lax.rsqrt(jnp.mean(total * total, axis=1, keepdims=True) + EPSILON)
    inv_o[...] = jnp.broadcast_to(inv_q, (ROWS, 128))
    cosine = here(s_ref[0], cos)
    sine = here(s_ref[0], sin)
    for g in range(8):
        at = block(g, 128)
        near = nq_o[:, at] * inv_q
        nq_o[:, at] = near
        u = near * gain[0:1, 2 * D + g * 128 : 2 * D + (g + 1) * 128]
        q_o[:, at] = (u * cosine + swapped(u) * sine).astype(BF16)


project_query = whole_call(
    project_query_kernel,
    "project_query",
    [shaped((ROWS, D), BF16), shaped((ROWS, D), F32), shaped((ROWS, 128), F32)],
    parts={n: ((QUART, D), (0, 0)) for n in range(3, 7)},
    limit=56,
)


def fill_bias(place, bias):
    row = lax.broadcasted_iota(jnp.int32, (HALF, 512), 0)
    lane = lax.broadcasted_iota(jnp.int32, (HALF, 512), 1)
    causal = jnp.where(row <= lane % HALF, 0.0, MASKED)
    is_prompt = lane % ROWS < HALF
    bias[0:HALF, :] = jnp.where(is_prompt, causal, 0.0)
    for k in range(1, 4):
        level = jnp.where((place ^ k) < place, 0.0, MASKED)
        bias[block(k, HALF), :] = jnp.where(is_prompt, level, 0.0)
    bias[4 * HALF :, :] = jnp.where(is_prompt, MASKED, causal)


def fill_keys(refs, keys, values):
    for j in range(4):
        keys[block(j, HALF), :] = refs[j][0:HALF, 0:KVW]
        values[block(j, HALF), :] = refs[j][0:HALF, KVW:D]
    keys[4 * HALF :, :] = refs[0][HALF:ROWS, 0:KVW]
    values[4 * HALF :, :] = refs[0][HALF:ROWS, KVW:D]


def doubled(ref, pair, odd):
    both = ref[:, spot(pair, 128)]
    other = pltpu.roll(both.astype(F32), HDIM, axis=1).astype(BF16)
    lane = lax.broadcasted_iota(jnp.int32, both.shape, 1)
    return jnp.where((lane < HDIM) == (odd == 0), both, other)


def stacked(ref, head, scale):
    rows = ref[:, spot(head, 128)]
    lane = lax.broadcasted_iota(jnp.int32, rows.shape, 1)
    rows = rows * jnp.asarray(scale, rows.dtype)
    none = jnp.zeros_like(rows)
    return jnp.concatenate(
        [jnp.where(lane < HDIM, rows, none), jnp.where(lane < HDIM, none, rows)], axis=0
    )


def attend_kernel(s_ref, q, kv0, kv1, kv2, kv3, mixed_o, lse_o, bias, keys, values):
    fill_bias(s_ref[0], bias)
    fill_keys((kv0, kv1, kv2, kv3), keys, values)

    def one_pair(pair, carry):
        for odd in range(2):
            head = 2 * pair + odd
            kk = doubled(keys, pair, odd)
            vv = doubled(values, pair, odd)
            scores = nt(kk, stacked(q, head, SCORE_SCALE)) + bias[...]
            highest = jnp.max(scores, axis=0, keepdims=True)
            raised = jnp.exp(scores - highest)
            totals = jnp.sum(raised, axis=0, keepdims=True)
            probs = (raised * (1.0 / totals)).astype(BF16)
            lse_o[pl.ds(head, 1), :] = highest + jnp.log(totals)
            out = tn(vv, probs).T
            lane = lax.broadcasted_iota(jnp.int32, (ROWS, 128), 1)
            mixed_o[:, spot(head, 128)] = jnp.where(
                lane < HDIM, out[0:ROWS], out[ROWS : 2 * ROWS]
            ).astype(BF16)
        return carry

    lax.fori_loop(0, PAIRS, one_pair, 0)


attend = whole_call(
    attend_kernel,
    "attend",
    [shaped((ROWS, D), BF16), shaped((8, 512), F32)],
    scratch=[
        pltpu.VMEM((KEYS, 512), F32),
        pltpu.VMEM((KEYS, KVW), BF16),
        pltpu.VMEM((KEYS, KVW), BF16),
    ],
    limit=56,
)


def route_kernel(s_ref, mixed_ref, o0, o1, o2, o3, xr, gain, rt, rp, rc, hid_o, b_o, gates_o):
    for k, part in enumerate((o0, o1, o2, o3)):
        total = nn(mixed_ref[:, block(0, QUART)], part[:, block(0, QUART)])
        for g in range(1, 4):
            total = total + nn(mixed_ref[:, block(g, QUART)], part[:, block(g, QUART)])
        hid_o[:, block(k, QUART)] = xr[:, block(k, QUART)].astype(F32) + RESIDUAL_SCALE * total
    hidden = hid_o[...]
    inverse = lax.rsqrt(jnp.mean(hidden * hidden, axis=1, keepdims=True) + EPSILON)
    b_o[:, 0:D] = (hidden * inverse * gain[0:1, D : 2 * D]).astype(BF16)
    logits = nt(rt[...], b_o[:, 0:D])
    expert = lax.broadcasted_iota(jnp.int32, (16, HALF), 0)
    for half, routes in enumerate((rp, rc)):
        chosen = routes[0:1, :] == expert
        for r in range(1, 8):
            chosen = chosen | (routes[r : r + 1, :] == expert)
        level = jnp.where(chosen, logits[:, block(half, HALF)], MASKED)
        raised = jnp.exp(level - jnp.max(level, axis=0, keepdims=True))
        gates = raised / jnp.sum(raised, axis=0, keepdims=True)
        gates = jnp.concatenate([gates, jnp.zeros((112, HALF), F32)], axis=0).T
        gates_o[block(half, HALF), :] = gates
        high = gates.astype(BF16).astype(F32)
        b_o[block(half, HALF), D:BOUT] = (high + pltpu.roll(gates - high, 16, axis=1)).astype(BF16)


route = whole_call(
    route_kernel,
    "route",
    [shaped((ROWS, D), F32), shaped((ROWS, BOUT), BF16), shaped((ROWS, 128), F32)],
    limit=56,
)


def piece_at(at, r, n):
    return ((at[0] + 4 - r) % 4) * at[2] + ((at[1] + 4 - n) % 4) * at[3]


def piece_at(at, r, n):
    return ((at[0] + 4 - r) % 4) * at[2] + ((at[1] + 4 - n) % 4) * at[3]


def fill_weights(at, own, other, far_parts, dest, lanes):
    dest[block(0, QUART), lanes] = own
    dest[block(1, QUART), lanes] = other
    for r in range(4):
        for n in range(4):
            piece = piece_at(at, r, n)
            for k in range(2):
                dest[spot((2 + k) * PIECES + piece, PROWS), lanes] = far_parts[r][n, k]


def expert_kernel(
    s_ref, at_ref, b0, b1, b2, b3, g0, g1, g2, g3, w0, w1, f0, f1, f2, f3,
    dudw_o, gz_o, dbk_o, dbs_o, xs, gs, gates, dgs, wgu, wd, dudw
):
    step = pl.program_id(0)
    place = s_ref[0]

    @pl.when(step == 0)
    def _():
        for j, (b_ref, g_ref) in enumerate(zip((b0, b1, b2, b3), (g0, g1, g2, g3))):
            rows = block(j, ROWS)
            for k in range(4):
                xs[rows, block(k, QUART)] = b_ref[:, block(k ^ j, QUART)]
                gs[rows, block(k, QUART)] = g_ref[:, spot(place ^ k, QUART)]
            both = b_ref[:, D:BOUT].astype(F32)
            gates[rows, :] = both + pltpu.roll(both, 112, axis=1)
        dgs[...] = jnp.zeros_like(dgs)

    here_gu = spot(step, 2 * GROUP * FSLICE)
    for n in range(GROUP):
        up = slice(n * TILE, n * TILE + 2 * FSLICE)
        down = slice(n * TILE + 2 * FSLICE, (n + 1) * TILE)
        for k, part in enumerate((w0, w1)):
            wgu[step, block(k, QUART), block(n, 2 * FSLICE)] = part[n, :, 0 : 2 * FSLICE]
            wd[block(k, QUART), block(n, FSLICE)] = part[n, :, 2 * FSLICE :]
        for r, part in enumerate((f0, f1, f2, f3)):
            for m in range(4):
                for k in range(2):
                    rows = spot((2 + k) * PIECES + piece_at(at_ref, r, m), PROWS)
                    wgu[step, rows, block(n, 2 * FSLICE)] = part[m, k, :, up]
                    wd[rows, block(n, FSLICE)] = part[m, k, :, down]
    both = nn(xs[...], wgu[step])
    h_all = RESIDUAL_SCALE * nn(gs[...], wd[...])
    lane = lax.broadcasted_iota(jnp.int32, (TOKENS, 128), 1)
    added = jnp.zeros((TOKENS, 128), F32)
    for n in range(GROUP):
        e = step * GROUP + n
        u = both[:, 2 * n * FSLICE : (2 * n + 1) * FSLICE]
        w = both[:, (2 * n + 1) * FSLICE : (2 * n + 2) * FSLICE]
        h = h_all[:, block(n, FSLICE)]
        gate = jnp.sum(jnp.where(lane == e, gates[...], 0.0), axis=1, keepdims=True)
        sig = jax.nn.sigmoid(u)
        silu = u * sig
        z = (silu * w).astype(BF16).astype(F32)
        gz_o[:, block(n, FSLICE)] = (gate * z).astype(BF16)
        added = added + jnp.where(lane == e, jnp.sum(z * h, axis=1, keepdims=True), 0.0)
        dz = gate * h
        du = (dz * w * sig * (1.0 + u * (1.0 - sig))).astype(BF16)
        dw = (dz * silu).astype(BF16)
        dudw_o[:, block(2 * n, FSLICE)] = du
        dudw_o[:, block(2 * n + 1, FSLICE)] = dw
    dgs[...] += added
    dudw[:, here_gu] = dudw_o[...]

    @pl.when(step == EXPERTS // GROUP - 1)
    def _():
        width = 2 * GROUP * FSLICE
        whole = nt(dudw[:, 0:width], wgu[0])
        for n in range(1, EXPERTS // GROUP):
            whole = whole + nt(dudw[:, block(n, width)], wgu[n])
        whole = whole.astype(BF16)
        for j in range(4):
            out = (dbk_o, dbs_o)[j % 2]
            rows = block(j, ROWS)
            for k in range(4):
                out[j // 2, :, block(k ^ j, QUART)] = whole[rows, block(k, QUART)]
            dg = dgs[rows, 0:16]
            high = dg.astype(BF16).astype(F32)
            out[j // 2, :, D:BOUT] = jnp.concatenate(
                [high, dg - high, jnp.zeros((ROWS, 96), F32)], axis=1
            ).astype(BF16)


def fixed(rank):
    return lambda e: (0,) * rank


def experts(place, at, b_parts, g_parts, w_parts):
    return pl.pallas_call(
        expert_kernel,
        name="experts",
        grid=(EXPERTS // GROUP,),
        in_specs=[SMEM] * 2
        + [pl.BlockSpec((ROWS, BOUT), fixed(2))] * 4
        + [pl.BlockSpec((ROWS, D), fixed(2))] * 4
        + [pl.BlockSpec((GROUP, QUART, TILE), lambda e: (e, 0, 0))] * 2
        + [pl.BlockSpec((4, 2, PROWS, GROUP * TILE), lambda e: (0, 0, 0, e))] * 4,
        out_specs=[
            pl.BlockSpec((TOKENS, 2 * GROUP * FSLICE), lambda e: (0, e)),
            pl.BlockSpec((TOKENS, GROUP * FSLICE), lambda e: (0, e)),
            pl.BlockSpec((2, ROWS, BOUT), fixed(3)),
            pl.BlockSpec((2, ROWS, BOUT), fixed(3)),
        ],
        out_shape=[
            shaped((TOKENS, EXPERTS * 2 * FSLICE), BF16),
            shaped((TOKENS, EXPERTS * FSLICE), BF16),
            shaped((2, ROWS, BOUT), BF16),
            shaped((2, ROWS, BOUT), BF16),
        ],
        scratch_shapes=[
            pltpu.VMEM((TOKENS, D), BF16),
            pltpu.VMEM((TOKENS, D), BF16),
            pltpu.VMEM((TOKENS, 128), F32),
            pltpu.VMEM((TOKENS, 128), F32),
            pltpu.VMEM((EXPERTS // GROUP, D, 2 * GROUP * FSLICE), BF16),
            pltpu.VMEM((D, GROUP * FSLICE), BF16),
            pltpu.VMEM((TOKENS, EXPERTS * 2 * FSLICE), BF16),
        ],
        compiler_params=pltpu.CompilerParams(vmem_limit_bytes=58 * 1024 * 1024),
        cost_estimate=COST,
    )(place, at, *b_parts, *g_parts, *w_parts)


def piece_to(at, r, v):
    return ((at[0] + r) % 4) * at[2] + v * at[3]


def grad_rows(at_ref, steps, source, dest):
    for i, r in enumerate(steps):
        for v in range(4):
            for k in range(4):
                rows = spot(PIECES * k + piece_to(at_ref, r, v), PROWS)
                dest[block(PIECES * i + 4 * v + k, PROWS), :] = source[rows, :]


def grad_blocks(outs, x_rows, g_rows, dudw, gz):
    first = nn(x_rows[...], dudw[...]).astype(BF16)
    second = (RESIDUAL_SCALE * nn(g_rows[...], gz[...])).astype(BF16)
    for i, out in enumerate(outs):
        for v in range(4):
            for k in range(4):
                rows = block(PIECES * i + 4 * v + k, PROWS)
                for n in range(GROUP):
                    out[v, k, n, :, 0 : 2 * FSLICE] = first[rows, block(n, 2 * FSLICE)]
                    out[v, k, n, :, 2 * FSLICE :] = second[rows, block(n, FSLICE)]


def near_grad_kernel(
    s_ref, at_ref, b0, b1, b2, b3, g0, g1, g2, g3, dudw, gz, t1, t3, xt, gt, x_rows, g_rows
):
    @pl.when(pl.program_id(0) == 0)
    def _():
        for j, (b_ref, g_ref) in enumerate(zip((b0, b1, b2, b3), (g0, g1, g2, g3))):
            for k in range(4):
                xt[block(k, QUART), block(j, ROWS)] = b_ref[:, block(k ^ j, QUART)].T
                gt[block(k, QUART), block(j, ROWS)] = g_ref[:, spot(s_ref[0] ^ k, QUART)].T
        grad_rows(at_ref, (1, 3), xt, x_rows)
        grad_rows(at_ref, (1, 3), gt, g_rows)

    grad_blocks((t1, t3), x_rows, g_rows, dudw, gz)


def rest_grad_kernel(s_ref, at_ref, xt, gt, dudw, gz, t0, t2, x_rows, g_rows):
    @pl.when(pl.program_id(0) == 0)
    def _():
        grad_rows(at_ref, (0, 2), xt, x_rows)
        grad_rows(at_ref, (0, 2), gt, g_rows)

    grad_blocks((t0, t2), x_rows, g_rows, dudw, gz)


def expert_grads(kernel, place, at, inputs, outputs, dudw, gz):
    block_out = pl.BlockSpec((4, 4, GROUP, PROWS, TILE), lambda e: (0, 0, e, 0, 0))
    return pl.pallas_call(
        kernel,
        name=kernel.__name__,
        grid=(EXPERTS // GROUP,),
        in_specs=[SMEM] * 2
        + [pl.BlockSpec(part.shape, fixed(2)) for part in inputs]
        + [
            pl.BlockSpec((TOKENS, 2 * GROUP * FSLICE), lambda e: (0, e)),
            pl.BlockSpec((TOKENS, GROUP * FSLICE), lambda e: (0, e)),
        ],
        out_specs=[block_out] * 2 + [pl.BlockSpec(out.shape, fixed(2)) for out in outputs],
        out_shape=[shaped((4, 4, EXPERTS, PROWS, TILE), BF16)] * 2 + outputs,
        scratch_shapes=[pltpu.VMEM((2 * QUART, TOKENS), BF16)] * 2,
        compiler_params=pltpu.CompilerParams(vmem_limit_bytes=56 * 1024 * 1024),
        cost_estimate=COST,
    )(place, at, *inputs, dudw, gz)


def mixture_kernel(at_ref, gz, w0, w1, f0, f1, f2, f3, keep_o, send_o, wide):
    for e in range(EXPERTS):
        at = slice(e * TILE + 2 * FSLICE, (e + 1) * TILE)
        parts = [part.at[:, :, :, at] for part in (f0, f1, f2, f3)]
        fill_weights(at_ref, w0[e], w1[e], parts, wide, block(e, FSLICE))
    for j in range(4):
        out = (keep_o, send_o)[j % 2]
        total = nt(gz[block(j, ROWS), :], wide[...]).astype(BF16)
        for k in range(4):
            out[j // 2, :, block(k ^ j, QUART)] = total[:, block(k, QUART)]


def mixture(at, gz, w_parts):
    down = [pl.BlockSpec((EXPERTS, QUART, FSLICE), lambda i: (0, 0, 2))] * 2 + [
        pl.BlockSpec((4, 2, PROWS, SHAREW), lambda i: (0, 0, 0, 0))
    ] * 4
    return pl.pallas_call(
        mixture_kernel,
        name="mixture",
        grid=(1,),
        in_specs=[SMEM, pl.BlockSpec((TOKENS, EXPERTS * FSLICE), fixed(2))] + down,
        out_specs=[pl.BlockSpec((2, ROWS, D), fixed(3))] * 2,
        out_shape=[shaped((2, ROWS, D), BF16)] * 2,
        scratch_shapes=[pltpu.VMEM((D, EXPERTS * FSLICE), BF16)],
        compiler_params=pltpu.CompilerParams(vmem_limit_bytes=56 * 1024 * 1024),
        cost_estimate=COST,
    )(at, gz, *w_parts)


def attend_back_kernel(
    s_ref, db_keep, db_come, db_far, hid, b, gates_ref, gp, gc, gain, rt, mixed, lse,
    q, kv0, kv1, kv2, kv3, o0, o1, o2, o3,
    hgrad_o, small_o, dwok_o, dwos_o, dq_o, kvk_o, kvs_o, dk_o, dv_o,
    bias, keys, values, dmix, grow
):
    place = s_ref[0]
    parts = (o0, o1, o2, o3)
    fill_bias(place, bias)
    fill_keys((kv0, kv1, kv2, kv3), keys, values)
    total = db_keep[0].astype(F32) + db_come[0].astype(F32) + db_far[...].astype(F32)
    tail = total[:, D:BOUT]
    dgate = (tail + pltpu.roll(tail, 112, axis=1))[:, 0:16]
    gates = gates_ref[:, 0:16]
    dlog = (gates * (dgate - jnp.sum(gates * dgate, axis=1, keepdims=True))).astype(BF16)
    dbt = total[:, 0:D] + nn(dlog, rt[...])
    small_o[...] = jnp.zeros_like(small_o)
    small_o[16:32, :] = tn(dlog, b[:, 0:D])
    hidden = hid[...]
    inverse = lax.rsqrt(jnp.mean(hidden * hidden, axis=1, keepdims=True) + EPSILON)
    n2 = hidden * inverse
    small_o[1:2, :] = jnp.sum(dbt * n2, axis=0, keepdims=True)
    scaled = dbt * gain[0:1, D : 2 * D]
    for k in range(4):
        there = spot(place ^ k, QUART)
        grow[0:HALF, block(k, QUART)] = gp[:, there]
        grow[HALF:ROWS, block(k, QUART)] = gc[:, there]
    hgrad = grow[...].astype(F32) + inverse * (
        scaled - n2 * jnp.mean(scaled * n2, axis=1, keepdims=True)
    )
    hgrad_o[...] = hgrad
    agrad = (RESIDUAL_SCALE * hgrad).astype(BF16)
    for g in range(4):
        total = nt(agrad[:, block(0, QUART)], parts[0][:, block(g, QUART)])
        for k in range(1, 4):
            total = total + nt(agrad[:, block(k, QUART)], parts[k][:, block(g, QUART)])
        dmix[:, block(g, QUART)] = total.astype(BF16)
    for g in range(4):
        rows = tn(mixed[:, block(g, QUART)], agrad).astype(BF16)
        for k in range(4):
            out = (dwok_o, dwos_o)[k % 2]
            out[k // 2, :, block(g, QUART)] = rows[:, block(k, QUART)]

    def one_pair(pair, carry):
        dks = []
        dvs = []
        lane = lax.broadcasted_iota(jnp.int32, (ROWS, 128), 1)
        for odd in range(2):
            head = 2 * pair + odd
            kk = doubled(keys, pair, odd)
            vv = doubled(values, pair, odd)
            qs = stacked(q, head, SCORE_SCALE)
            ds_rows = stacked(dmix, head, 1.0)
            probs = jnp.exp(nt(kk, qs) + bias[...] - lse[pl.ds(head, 1), :])
            product = dmix[:, spot(head, 128)].astype(F32) * mixed[:, spot(head, 128)].astype(F32)
            product = product.T
            inner = jnp.concatenate(
                [
                    jnp.sum(product[0:HDIM], axis=0, keepdims=True),
                    jnp.sum(product[HDIM:], axis=0, keepdims=True),
                ],
                axis=1,
            )
            sgrad = (probs * (nt(vv, ds_rows) - inner)).astype(BF16)
            dkr = nn(sgrad, qs)
            dvr = nn(probs.astype(BF16), ds_rows)
            dks.append(dkr + pltpu.roll(dkr, HDIM, axis=1))
            dvs.append(dvr + pltpu.roll(dvr, HDIM, axis=1))
            dqt = (SCORE_SCALE * tn(kk, sgrad)).T
            dq_o[:, spot(head, 128)] = jnp.where(lane < HDIM, dqt[0:ROWS], dqt[ROWS : 2 * ROWS])
        low = lax.broadcasted_iota(jnp.int32, (KEYS, 128), 1) < HDIM
        dk = jnp.where(low, dks[0], dks[1])
        dv = jnp.where(low, dvs[0], dvs[1])
        at = spot(pair, 128)
        at_v = spot(pair + 4, 128)
        for j in range(4):
            side = (kvk_o, kvs_o)[j % 2]
            side[j // 2, :, at] = dk[block(j, HALF)].astype(BF16)
            side[j // 2, :, at_v] = dv[block(j, HALF)].astype(BF16)
        dk_o[:, at] = dk[4 * HALF :]
        dv_o[:, at] = dv[4 * HALF :]
        return carry

    lax.fori_loop(0, PAIRS, one_pair, 0)


attend_back = whole_call(
    attend_back_kernel,
    "attend_back",
    [
        shaped((ROWS, D), F32),
        shaped((32, D), F32),
        shaped((2, QUART, D), BF16),
        shaped((2, QUART, D), BF16),
        shaped((ROWS, D), F32),
        shaped((2, HALF, D), BF16),
        shaped((2, HALF, D), BF16),
        shaped((HALF, KVW), F32),
        shaped((HALF, KVW), F32),
    ],
    scratch=[
        pltpu.VMEM((KEYS, 512), F32),
        pltpu.VMEM((KEYS, KVW), BF16),
        pltpu.VMEM((KEYS, KVW), BF16),
        pltpu.VMEM((ROWS, D), BF16),
        pltpu.VMEM((ROWS, D), BF16),
    ],
    limit=36,
    parts={n: ((1, ROWS, BOUT), (0, 0, 0)) for n in (1, 2)},
)


def turn_back(values, cosine, sine):
    return values * cosine - swapped(values) * sine


def query_back_kernel(
    s_ref, dq, nq, inv, gain, cos, sin, ar, a0, a1, a2, a3, dwqk_o, dwqs_o, da_o, qg_o, grads
):
    cosine = here(s_ref[0], cos)
    sine = here(s_ref[0], sin)
    inv_q = inv[:, 0:1]
    dot = jnp.zeros((ROWS, 1), F32)
    for g in range(8):
        at = block(g, 128)
        back = turn_back(dq[:, at], cosine, sine)
        near = nq[:, at]
        qg_o[0:1, at] = jnp.sum(back * near, axis=0, keepdims=True)
        scaled = back * gain[0:1, 2 * D + g * 128 : 2 * D + (g + 1) * 128]
        dot = dot + jnp.sum(scaled * near, axis=1, keepdims=True)
        grads[:, at] = scaled
    pre = (inv_q * (grads[...] - nq[...] * (dot / D))).astype(BF16)
    for k, part in enumerate((a0, a1, a2, a3)):
        da_o[:, block(k, QUART)] = nt(pre, part[...])
        out = (dwqk_o, dwqs_o)[k % 2]
        out[k // 2] = tn(ar[:, block(k, QUART)], pre).astype(BF16)


query_back = whole_call(
    query_back_kernel,
    "query_back",
    [
        shaped((2, QUART, D), BF16),
        shaped((2, QUART, D), BF16),
        shaped((ROWS, D), F32),
        shaped((8, D), F32),
    ],
    scratch=[pltpu.VMEM((ROWS, D), F32)],
    parts={n: ((QUART, D), (0, 0)) for n in range(8, 12)},
)


def key_back_kernel(
    s_ref, kv_keep, kv_come, dk, dv, nk, inv, gain, cos, sin, ar, xr, hgrad, da_q, qg, small,
    a0, a1, a2, a3, keep_o, send_o, xp_o, xc_o, grads, both, da, cols
):
    place = s_ref[0]
    cosine = here(s_ref[0], cos)
    sine = here(s_ref[0], sin)
    inv_k = inv[:, 1:2]
    grads[0:HALF, :] = kv_keep[:, 0:KVW].astype(F32) + kv_come[:, 0:KVW].astype(F32)
    grads[HALF:ROWS, :] = dk[...]
    both[0:HALF, KVW:D] = (kv_keep[:, KVW:D].astype(F32) + kv_come[:, KVW:D].astype(F32)).astype(BF16)
    both[HALF:ROWS, KVW:D] = dv[...].astype(BF16)
    cols[...] = jnp.zeros_like(cols)
    dot = jnp.zeros((ROWS, 1), F32)
    for g in range(4):
        at = block(g, 128)
        back = turn_back(grads[:, at], cosine, sine)
        near = nk[:, at]
        kgrad = jnp.sum(back * near, axis=0, keepdims=True)
        cols[3:4, spot(place ^ g, QUART)] = jnp.concatenate([kgrad, jnp.zeros_like(kgrad)], axis=1)
        scaled = back * gain[0:1, 3 * D + g * 128 : 3 * D + (g + 1) * 128]
        dot = dot + jnp.sum(scaled * near, axis=1, keepdims=True)
        grads[:, at] = scaled
    both[:, 0:KVW] = (inv_k * (grads[...] - nk[...] * (dot / KVW))).astype(BF16)
    pre = both[...]
    for k, part in enumerate((a0, a1, a2, a3)):
        da[:, block(k, QUART)] = da_q[:, block(k, QUART)] + nt(pre, part[...])
        out = (keep_o, send_o)[k % 2]
        out[k // 2, :, 0:D] = tn(ar[:, block(k, QUART)], pre).astype(BF16)
    x = xr[...].astype(F32)
    inverse = inv[:, 2:3]
    n1 = x * inverse
    grad = da[...]
    cols[0:1, :] = jnp.sum(grad * n1, axis=0, keepdims=True)
    cols[1:2, :] = small[1:2, :]
    cols[16:32, :] = small[16:32, :]
    for k in range(4):
        cols[2:3, block(k, QUART)] = qg[0:1, spot(place ^ k, QUART)]
    for k in range(4):
        out = (keep_o, send_o)[k % 2]
        out[k // 2, :, D:BOUT] = cols[:, block(k, QUART)].T.astype(BF16)
    scaled = grad * gain[0:1, 0:D]
    result = hgrad[...] + inverse * (scaled - n1 * jnp.mean(scaled * n1, axis=1, keepdims=True))
    low = result.astype(BF16)
    for k in range(4):
        there = spot(place ^ k, QUART)
        xp_o[:, there] = low[0:HALF, block(k, QUART)]
        xc_o[:, there] = low[HALF:ROWS, block(k, QUART)]


key_back = whole_call(
    key_back_kernel,
    "key_back",
    [
        shaped((2, QUART, BOUT), BF16),
        shaped((2, QUART, BOUT), BF16),
        shaped((HALF, D), BF16),
        shaped((HALF, D), BF16),
    ],
    scratch=[
        pltpu.VMEM((ROWS, KVW), F32),
        pltpu.VMEM((ROWS, D), BF16),
        pltpu.VMEM((ROWS, D), F32),
        pltpu.VMEM((128, D), F32),
    ],
    parts={n: ((QUART, D), (1, 0)) for n in range(16, 20)},
)


def finish_kernel(s_ref, hid, keep, come, xp_o, xc_o):
    total = hid[...] + RESIDUAL_SCALE * (keep[...].astype(F32) + come[...].astype(F32))
    low = total.astype(BF16)
    for k in range(4):
        there = spot(s_ref[0] ^ k, QUART)
        xp_o[:, there] = low[0:HALF, block(k, QUART)]
        xc_o[:, there] = low[HALF:ROWS, block(k, QUART)]


finish = whole_call(
    finish_kernel,
    "finish",
    [shaped((HALF, D), BF16), shaped((HALF, D), BF16)],
)


def pair_kernel(at_ref, qk, qc, lk, lc, ok, oc, t0, t1, t2, t3):
    for r, out in enumerate((t0, t1, t2, t3)):
        for v in range(4):
            rows = spot(piece_to(at_ref, r, v), PROWS)
            last = (lk[0, rows, :].astype(F32) + lc[0, rows, :].astype(F32)).astype(BF16)
            out[v, 0, :, 0:D] = (qk[0, rows, :].astype(F32) + qc[0, rows, :].astype(F32)).astype(BF16)
            out[v, 0, :, D:QKVW] = last[:, 0:D]
            out[v, 0, :, QKVW : QKVW + D] = (
                ok[0, rows, :].astype(F32) + oc[0, rows, :].astype(F32)
            ).astype(BF16)
            out[v, 0, :, QKVW + D :] = last[:, D:]


def pair(at, *parts):
    return pl.pallas_call(
        pair_kernel,
        name="pair",
        grid=(2,),
        in_specs=[SMEM]
        + [pl.BlockSpec((1, QUART, part.shape[2]), lambda k: (k, 0, 0)) for part in parts],
        out_specs=[pl.BlockSpec((4, 1, PROWS, ATTW), lambda k: (0, k, 0, 0))] * 4,
        out_shape=[shaped((4, 2, PROWS, ATTW), BF16)] * 4,
        compiler_params=pltpu.CompilerParams(vmem_limit_bytes=24 * 1024 * 1024),
        cost_estimate=COST,
    )(at, *parts)


def fold_kernel(at_ref, i0, i1, i2, i3, o0, o1, o2, o3):
    for r, out in enumerate((o0, o1, o2, o3)):
        there = (at_ref[1] + r) % 4
        total = i0[there].astype(F32) + i1[there].astype(F32)
        out[...] = (total + i2[there].astype(F32) + i3[there].astype(F32)).astype(BF16)


def fold(at, parts, rows, steps):
    shape = parts[0].shape
    width = shape[-1]
    flat = [part.reshape(4, rows, width) for part in parts]
    height = rows // steps
    outs = pl.pallas_call(
        fold_kernel,
        name="fold",
        grid=(steps,),
        in_specs=[SMEM] + [pl.BlockSpec((4, height, width), lambda i: (0, i, 0))] * 4,
        out_specs=[pl.BlockSpec((height, width), lambda i: (i, 0))] * 4,
        out_shape=[shaped((rows, width), BF16)] * 4,
        compiler_params=pltpu.CompilerParams(vmem_limit_bytes=24 * 1024 * 1024),
        cost_estimate=COST,
    )(at, *flat)
    return [out.reshape(shape[1:]) for out in outs]


def unpack_kernel(s_ref, at_ref, p0, p1, p2, p3, p4, gate_o, up_o, down_o, tile):
    for r, part, low in ((0, p0, 0), (1, p1, 0), (2, p2, 0), (2, p3, 2), (3, p4, 0)):
        for n in range(part.shape[0]):
            rows = spot(piece_at(at_ref, r, low + n), PROWS)
            for k in range(4):
                there = spot(s_ref[0] ^ k, FSLICE)
                gate_o[0, rows, there] = part[n, k, 0, :, 0:FSLICE].astype(F32)
                up_o[0, rows, there] = part[n, k, 0, :, FSLICE : 2 * FSLICE].astype(F32)
                tile[rows, block(k, FSLICE)] = part[n, k, 0, :, 2 * FSLICE :].astype(F32)
    for k in range(4):
        down_o[0, spot(s_ref[0] ^ k, FSLICE), :] = tile[:, block(k, FSLICE)].T


def unpack_experts(place, at, parts):
    specs = [
        pl.BlockSpec((part.shape[0], 4, 1, PROWS, TILE), lambda e: (0, 0, e, 0, 0))
        for part in parts
    ]
    return pl.pallas_call(
        unpack_kernel,
        name="unpack_experts",
        grid=(EXPERTS,),
        in_specs=[SMEM] * 2 + specs,
        out_specs=[
            pl.BlockSpec((1, QUART, 512), lambda e: (e, 0, 0)),
            pl.BlockSpec((1, QUART, 512), lambda e: (e, 0, 0)),
            pl.BlockSpec((1, 512, QUART), lambda e: (e, 0, 0)),
        ],
        out_shape=[
            shaped((EXPERTS, QUART, 512), F32),
            shaped((EXPERTS, QUART, 512), F32),
            shaped((EXPERTS, 512, QUART), F32),
        ],
        scratch_shapes=[pltpu.VMEM((QUART, 512), F32)],
        compiler_params=pltpu.CompilerParams(vmem_limit_bytes=24 * 1024 * 1024),
        cost_estimate=COST,
    )(place, at, *parts)


def unpack_attention_kernel(
    at_ref, p0, p1, p2, p3, wq_o, wk_o, wv_o, wo_o, attn_o, ffn_o, qg_o, kg_o, router_o, wide
):
    for r, part in enumerate((p0, p1, p2, p3)):
        for n in range(4):
            wide[spot(piece_at(at_ref, r, n), PROWS), :] = part[n]
    wq_o[...] = wide[:, 0:D].astype(F32)
    wk_o[...] = wide[:, D : D + KVW].astype(F32)
    wv_o[...] = wide[:, D + KVW : QKVW].astype(F32)
    for g in range(4):
        wo_o[block(g, QUART), :] = wide[:, QKVW + g * QUART : QKVW + (g + 1) * QUART].astype(F32)
    tail = wide[:, QKVW + D :].astype(F32)
    rows = tail.T
    attn_o[...] = rows[0:1]
    ffn_o[...] = rows[1:2]
    qg_o[...] = rows[2:3]
    kg_o[...] = rows[3:4, 0:HALF]
    router_o[...] = rows[16 : 16 + EXPERTS]


unpack_attention = whole_call(
    unpack_attention_kernel,
    "unpack_attention",
    [
        shaped((QUART, D), F32),
        shaped((QUART, KVW), F32),
        shaped((QUART, KVW), F32),
        shaped((D, QUART), F32),
        shaped((1, QUART), F32),
        shaped((1, QUART), F32),
        shaped((1, QUART), F32),
        shaped((1, HALF), F32),
        shaped((EXPERTS, QUART), F32),
    ],
    scratch=[pltpu.VMEM((QUART, ATTW), BF16)],
)


def body(
    prompt_x, cont_x, prompt_cot, cont_cot, prompt_routes, cont_routes,
    attn_gain, w_query, w_key, w_value, query_gain, key_gain,
    w_out, ffn_gain, w_router, w_gate, w_up, w_down,
):
    def moved(value, axes, change):
        sizes = [lax.axis_size(a) for a in axes]
        pairs = []
        count = 1
        for size in sizes:
            count *= size
        for index in range(count):
            rest, coords = index, []
            for size in reversed(sizes):
                coords.append(rest % size)
                rest //= size
            to = change(*reversed(coords))
            target = 0
            for size, coord in zip(sizes, to):
                target = target * size + coord
            pairs.append((index, target))
        return lax.ppermute(value, axes, pairs)

    def sib(value):
        return moved(value, ("c",), lambda c: (1 - c,))

    def far(value):
        return moved(value, ("xh",), lambda h: (1 - h,))

    def far_sib(value):
        return moved(value, ("xh", "c"), lambda h, c: (1 - h, 1 - c))

    def cross(value):
        return moved(value, ("xl", "xh"), lambda low, high: (1 - low, 1 - high))

    def cross_sib(value):
        return moved(value, ("xl", "xh", "c"), lambda low, high, c: (1 - low, 1 - high, 1 - c))

    def near(value):
        return moved(value, ("xl",), lambda low: (1 - low,))

    def along(value, by, core_of_z):
        def change(at_z, at_y, c):
            if c == core_of_z:
                return ((at_z + by) % 4, at_y, c)
            return (at_z, (at_y + by) % 4, c)

        return moved(value, ("z", "y", "c"), change)

    def first(value, by):
        return along(value, by, 1)

    def second(value, by):
        return along(value, by, 0)

    def spread(value, way):
        return [value] + [way(value, by) for by in (1, 2, 3)]

    def added(parts):
        total = parts[0].astype(F32)
        for part in parts[1:]:
            total = total + part.astype(F32)
        return total.astype(BF16)

    after = lax.optimization_barrier

    z = lax.axis_index("z").astype(jnp.int32)
    y = lax.axis_index("y").astype(jnp.int32)
    core = lax.axis_index("c").astype(jnp.int32)
    low_core = core == 0
    at = jnp.stack(
        [
            jnp.where(low_core, y, z),
            jnp.where(low_core, z, y),
            jnp.where(low_core, 1, 4),
            jnp.where(low_core, 4, 1),
        ]
    )
    position = lax.axis_index(("xh", "c")).astype(jnp.int32)
    place = position[None]
    piece = 4 * z + y
    cont_in = cont_x.reshape(HALF, D)
    cont_up = cont_cot.reshape(HALF, D)

    def held(value, *others):
        return after((value, others))[0]

    share_two, share_three = share_experts(
        jnp.concatenate([piece[None], place]), w_gate, w_up, w_down
    )
    place_in, share_two, share_three = after((place, share_two, share_three))
    share_two = cross(share_two)
    share_three = cross_sib(share_three)
    own_in = prepare(
        place_in, w_query, w_key, w_value, attn_gain[None], ffn_gain[None], query_gain[None],
        key_gain[None], w_router.T,
    )
    place_in, own_in, share_two = after((place, own_in, share_two))
    in_two = cross(own_in)
    row = jnp.stack(spread(jnp.stack([share_two, share_three]), second))
    own_out = prepare_out(place_in, w_out)
    packed = pack_experts(place_in, w_gate, w_up, w_down)
    in_two, packed, row, own_in_sib, own_out, out_sib = after(
        (in_two, packed, row, sib(own_in), own_out, sib(own_out))
    )
    in_parts = (own_in, own_in_sib, in_two, sib(in_two))

    cosine, sine = (jnp.asarray(table) for table in angle_tables())

    kv, kv_own, nk, inv, xr, ar, gain, rt = project_keys(
        place, prompt_x, cont_in, *in_parts, cosine, sine
    )
    kv_two = far(kv_own)
    row_one = first(row, 1)
    row_three = first(row, 3)
    q, nq, inv_q = project_query(place, ar, gain, *in_parts, cosine, sine)
    kv_two = held(kv_two, q)
    out_two = cross(own_out)
    upstream = jnp.concatenate([prompt_cot, cont_up], axis=0)
    up_two = cross(upstream)
    kv_parts = (kv, sib(held(kv_own, q)), kv_two, sib(kv_two))
    kv_parts, out_two = after((kv_parts, out_two))
    mixed, lse = attend(place, q, *kv_parts)
    row, row_one, row_three, packed, upstream, up_two = after(
        (row, row_one, row_three, packed, upstream, up_two, mixed)
    )[0:6]
    row_two = first(row, 2)
    out_parts = (own_out, out_sib, out_two, sib(out_two))
    hidden, b, gates = route(
        place, mixed, *out_parts, xr, gain, rt, prompt_routes.T, cont_routes.reshape(HALF, 8).T
    )
    up_sib = sib(upstream)
    packed_sib = sib(packed[1])
    b, up_sib, packed_sib = after((b, up_sib, packed_sib))
    w_parts = (packed[0], packed_sib, row, row_one, row_two, row_three)
    b_two, up_sib_two = after((cross(b), sib(up_two)))
    up_parts = (upstream, up_sib, up_two, up_sib_two)
    b_parts = (b, sib(b), b_two, sib(b_two))
    dudw, gz, db_keep, db_send = experts(place, at, b_parts, up_parts, w_parts)

    db_come = sib(db_send)
    db_sum = added([db_keep[1], db_come[1]])
    db_sum, dudw = after((db_sum, dudw))
    db_far = cross(db_sum)
    turned = [shaped((D, TOKENS), BF16)] * 2
    grad_one, grad_three, xt, gt = expert_grads(
        near_grad_kernel, place, at, [*b_parts, *up_parts], turned, dudw, gz
    )
    place_in, xt, db_far = after((place, xt, db_far))
    grad_own, grad_next = expert_grads(rest_grad_kernel, place_in, at, [xt, gt], [], dudw, gz)
    grad_one = first(grad_one, 1)
    grad_three = first(grad_three, 3)
    grad_two = first(grad_next, 2)
    later = held(place, grad_own)

    hgrad, small, dwo_keep, dwo_send, dq, kv_keep, kv_send, dk, dv = attend_back(
        later, db_keep, db_come, db_far, hidden, b, gates, prompt_cot, cont_up, gain, rt, mixed, lse,
        q, *kv_parts, *out_parts,
    )

    kv_come = sib(kv_send)
    kv_sum = added([kv_keep, kv_come])
    kv_far = far(kv_sum[1])
    dq, kv_sum = after((dq, kv_sum))
    dwq_keep, dwq_send, da_q, qg = query_back(
        place, dq, nq, inv_q, gain, cosine, sine, ar, *in_parts
    )
    grad_one, grad_two, grad_three, da_q = after((grad_one, grad_two, grad_three, da_q))
    grad_rest = fold(at, [grad_own, grad_one, grad_two, grad_three], 4 * EXPERTS * PROWS, 2)
    da_q, grad_rest = after((da_q, grad_rest))
    last_keep, last_send, prompt_grad, cont_grad = key_back(
        place, kv_sum[0], kv_far, dk, dv, nk, inv, gain, cosine, sine, ar, xr, hgrad, da_q, qg,
        small, *in_parts,
    )

    paired = pair(
        held(at, grad_rest), dwq_keep, sib(dwq_send), last_keep, sib(last_send), dwo_keep, sib(dwo_send)
    )
    grad_rest = [grad_rest[0]] + [second(grad_rest[by], by) for by in (1, 2, 3)]
    summed = added(held(grad_rest, paired[0]))
    paired = [paired[0]] + [first(paired[by], by) for by in (1, 2, 3)]

    turned_parts = [summed[0], sib(summed[1]), far(summed[2]), far_sib(summed[3])]
    paired[1], paired[3], turned_parts = after((paired[1], paired[3], turned_parts))
    turned_parts = jnp.stack(turned_parts, axis=0)
    near_parts = near(turned_parts)
    mix_keep, mix_send = mixture(at, held(gz, turned_parts), w_parts)
    own_sum = added([turned_parts, held(near_parts, mix_keep)])
    steps = jnp.stack(spread(own_sum, second))
    paired = held(fold(at, held(paired, turned_parts), 2 * PROWS, 1), steps)
    steps_one = first(steps, 1)
    steps_three = first(steps, 3)

    mix_sum = added([mix_keep, sib(mix_send)])
    mix_far = cross(mix_sum[1])
    prompt_out, cont_out = finish(place, hidden, mix_sum[0], mix_far)

    part = added([paired[0]] + [second(paired[by], by) for by in (1, 2, 3)])
    part = added([part[0], near(part[0]), far(part[1]), cross(part[1])])
    part_steps = jnp.stack(spread(part, second))
    steps_one, steps_three, part_steps = after((steps_one, steps_three, part_steps))
    steps_two = (first(steps_one[0:2], 1), first(steps_three[2:4], 3))
    full = spread(part_steps, first)
    gate_grad, up_grad, down_grad = unpack_experts(
        place, at, (steps, steps_one, *steps_two, steps_three)
    )
    wq_grad, wk_grad, wv_grad, wo_grad, attn_grad, ffn_grad, qg_grad, kg_grad, router_grad = (
        unpack_attention(at, *held(full, gate_grad))
    )

    return (
        prompt_out,
        cont_out.reshape(1, HALF, D),
        prompt_grad,
        cont_grad.reshape(1, HALF, D),
        attn_grad[0],
        wq_grad,
        wk_grad,
        wv_grad,
        qg_grad[0],
        kg_grad[0],
        wo_grad,
        ffn_grad[0],
        router_grad.T,
        gate_grad,
        up_grad,
        down_grad,
    )


def solution(mesh):
    fine = Mesh(mesh.devices.reshape(2, 4, 4, 2, 2), AXES)
    shard = ("xh", "c")
    tokens = P(AXES, None)
    series = P(AXES, None, None)
    weights = (
        P(shard),
        P(shard, None),
        P(shard, None),
        P(shard, None),
        P(shard),
        P(shard),
        P(None, shard),
        P(shard),
        P(shard, None),
        P(None, shard, None),
        P(None, shard, None),
        P(None, None, shard),
    )
    return jax.shard_map(
        body,
        mesh=fine,
        in_specs=(tokens, series, tokens, series, tokens, series, *weights),
        out_specs=(tokens, series, tokens, series, *weights),
        check_vma=False,
    )
```
